128 devices in a mesh: gx: 8 (over z_lo, y), gy: 8 (over x, core), gz: 2 (over z_hi).
Axes of the slice: x: 4, y: 4, z: 4 (z_hi: 2, z_lo: 2; z = z_hi * 2 + z_lo), core: 2. Of those that a mesh axis runs over, the one named last changes fastest.
Arguments:
- orbitals: float32 [32, 64, 64, 256], P(None, 'gx', 'gy', 'gz'), may hold values from -6 to 6
- potential: float32 [64, 64, 256], P('gx', 'gy', 'gz'), may hold values from 0 to 2
- projector: float32 [4, 1048576], P(None, ('gx', 'gy', 'gz')), may hold values from -0.1875 to 0.1875
- point_cell: int32 [1048576], P(('gx', 'gy', 'gz')), may hold values from 0 to 8191
- target: int32 [1048576], P(('gx', 'gy', 'gz')), may hold values from 0 to 53
- point_count: int32 [8, 8, 2], P('gx', 'gy', 'gz'), may hold values from 2730 to 8192, as said below
- coupling: float32 [256, 4], P(('gx', 'gy', 'gz')), may hold values from 1 to 3
Outputs:
- subspace: float32 [32, 64, 64, 256], P(None, 'gx', 'gy', 'gz')
The draws below stay inside these ranges and needn't reach their ends.
Inputs may be any that keep to these rules, and one draw needn't show every extreme that they name: Some domain has exactly 8192 live point slots; slots from point_count on are ignored.
All inputs are finite; a program needn't handle non-finite values.
Results may differ from the reference program's by a relative error of at most 0.0003.
Values sent between devices are 32-bit elements; how exact they have to be, the bound alone decides.
No kernel may reach another device: no remote copies, remote signals or barrier semaphores. Data moves between devices by JAX's collectives and lax.ppermute only.
A program may use at most 128 MiB of HBM per device.

```python
import math
import jax
import jax.numpy as jnp
from jax import lax

NB = 32
NPJ = 4
DEGREE = 4
CX = 8
CY = 8
CZ = 128
ATOM_DEV = 2
PTS = 8192
DOM_X = 8
DOM_Y = 8
DOM_Z = 2
NX = 64
NY = 64
NZ = 256
ATOMS = 256
POINTS = 1048576


def draw_point_count(key, part):
    key = jax.random.fold_in(key, 7)
    grid_shape = (NX // CX, NY // CY, NZ // CZ)
    domains = grid_shape[0] * grid_shape[1] * grid_shape[2]
    counts = jax.random.randint(jax.random.fold_in(key, 1), (domains,), PTS // 3, PTS + 1)
    chosen = jax.random.randint(jax.random.fold_in(key, 2), (), 0, domains)
    counts = counts.at[chosen].set(PTS)
    return counts.reshape(grid_shape).astype(jnp.int32)


def plant(entries, key, low, high):
    shape = entries.shape
    index_at = [jax.random.randint(jax.random.fold_in(key, axis), (), 0, shape[axis]) for axis in range(len(shape))]
    entries = entries.at[tuple(index_at)].set(low)
    longest = shape.index(max(shape))
    index_at[longest] = (index_at[longest] + 1) % shape[longest]
    return entries.at[tuple(index_at)].set(high)


def shard_levels(own_key, shape, split, least, high):
    gain = 1.0
    for dim, shards_of in split:
        steps = jax.random.uniform(jax.random.fold_in(jax.random.fold_in(own_key, 6), dim), (shards_of,), jnp.float32, least / len(split), high / len(split))
        gain = gain * jnp.repeat(jnp.exp(steps), shape[dim] // shards_of).reshape((-1,) + (1,) * (len(shape) - 1 - dim))
    return gain


def scatter_about(key, dims, deviation, bound, pieces=(), kind=jnp.bfloat16):
    drawn = jax.random.normal(key, dims, jnp.float32) * deviation
    if len(pieces) > 0:
        drawn = shard_levels(key, dims, pieces, -0.22, 0.18) * drawn
    return jnp.clip(drawn, min=-bound, max=bound).astype(kind)


def setup_inputs(seed: int = 0) -> dict:
    key_of = jax.random.split(jax.random.key(seed), 8)
    return {
        "orbitals": scatter_about(key_of[0], (NB, NX, NY, NZ), 1.0, 6.0, ((1, 8), (2, 8), (3, 2)), jnp.float32),
        "potential": jnp.clip(2.0 * jax.random.uniform(key_of[1], (NX, NY, NZ), jnp.float32) ** shard_levels(key_of[1], (NX, NY, NZ), ((0, 8), (1, 8), (2, 2)), -0.2, 0.2), 0.0, 2.0),
        "projector": scatter_about(key_of[2], (NPJ, POINTS), (2 * PTS // (9 * ATOM_DEV)) ** -0.5, 0.1875, ((1, 128),), jnp.float32),
        "point_cell": plant(jax.random.randint(key_of[3], (POINTS,), 0, CX * CY * CZ), jax.random.fold_in(key_of[3], 1), 0, (CX * CY * CZ) - 1).astype(jnp.int32),
        "target": plant(jax.random.randint(key_of[4], (POINTS,), 0, 27 * ATOM_DEV), jax.random.fold_in(key_of[4], 1), 0, (27 * ATOM_DEV) - 1).astype(jnp.int32),
        "point_count": draw_point_count(jax.random.fold_in(key_of[7], 71), 0),
        "coupling": jnp.clip(jnp.exp(math.log(3.0) - 1.0986123 * jax.random.uniform(key_of[6], (ATOMS, NPJ), jnp.float32) ** shard_levels(key_of[6], (ATOMS, NPJ), ((0, 128),), -0.2, 0.2)), 1.0, 3.0),
    }


STENCIL = (-5369.0 / 1800.0, 12.0 / 7.0, -15.0 / 56.0, 10.0 / 189.0, -1.0 / 112.0, 2.0 / 1925.0, -1.0 / 16632.0)
FILTER_CENTRE = 9.5
FILTER_HALF = 5.5

def laplace(field):
    summed = 3.0 * STENCIL[0] * field
    for grid_axis in (0, 1, 2):
        for offset in range(1, 7):
            summed = summed + STENCIL[offset] * (jnp.roll(field, offset, grid_axis) + jnp.roll(field, -offset, grid_axis))
    return summed

def reference(orbitals, potential, projector, point_cell, target, point_count, coupling):
    point_index = jnp.arange(POINTS, dtype=jnp.int32)
    domain = point_index // PTS
    dom_x = domain // (DOM_Y * DOM_Z)
    dom_y = domain // DOM_Z % DOM_Y
    dom_z = domain % DOM_Z
    alive_mask = (point_index % PTS < point_count[dom_x, dom_y, dom_z]).astype(projector.dtype)
    cell_x = point_cell // (CY * CZ)
    cell_y = point_cell // CZ % CY
    cell_z = point_cell % CZ
    global_cell = (((dom_x * CX + cell_x) * NY + dom_y * CY + cell_y) * NZ + dom_z * CZ + cell_z).astype(jnp.int32)
    offset_code = target // ATOM_DEV
    slot_index = target % ATOM_DEV
    owner_domain = ((dom_x + offset_code // 9 - 1) % DOM_X * DOM_Y + (dom_y + offset_code // 3 % 3 - 1) % DOM_Y) * DOM_Z + (dom_z + offset_code % 3 - 1) % DOM_Z
    atom_index = (owner_domain * ATOM_DEV + slot_index).astype(jnp.int32)
    weight = projector * alive_mask[None, :]
    total_cells = NX * NY * NZ

    def band_nonlocal(band):
        flat_band = band.reshape(total_cells)
        at_points = flat_band[global_cell]
        back = jnp.zeros((POINTS,), band.dtype)
        for channel in range(NPJ):
            coeffs = jax.ops.segment_sum(at_points * weight[channel], atom_index, ATOMS)
            scaled = coeffs * coupling[:, channel]
            back = back + scaled[atom_index] * weight[channel]
        added = jax.ops.segment_sum(back, global_cell, total_cells)
        return added.reshape(band.shape)

    def band_hamiltonian(band):
        return -0.5 * laplace(band) + potential * band + band_nonlocal(band)

    def hamiltonian(field):
        return lax.map(band_hamiltonian, field)
    previous = orbitals
    current = (hamiltonian(orbitals) - FILTER_CENTRE * orbitals) / FILTER_HALF
    for degree_step in range(DEGREE - 1):
        following = 2.0 * (hamiltonian(current) - FILTER_CENTRE * current) / FILTER_HALF - previous
        previous, current = (current, following)
    flattened = current.reshape(NB, total_cells)
    gram_matrix = jnp.dot(flattened, flattened.T, precision=lax.Precision.HIGHEST) / float(total_cells)
    lower_factor = jnp.linalg.cholesky(gram_matrix)
    inverse = jax.scipy.linalg.solve_triangular(lower_factor, jnp.eye(NB, dtype=gram_matrix.dtype), lower=True)
    return jnp.dot(inverse, flattened, precision=lax.Precision.HIGHEST).reshape(orbitals.shape)
```

```python
import functools

import jax
import jax.numpy as jnp
import numpy as np
from jax import lax
from jax.experimental import pallas as pl
from jax.experimental.pallas import tpu as pltpu
from jax.sharding import PartitionSpec as P

DEGREE = 4
STENCIL = (
    -5369.0 / 1800.0,
    12.0 / 7.0,
    -15.0 / 56.0,
    10.0 / 189.0,
    -1.0 / 112.0,
    2.0 / 1925.0,
    -1.0 / 16632.0,
)
FILTER_CENTRE = 9.5
FILTER_HALF = 5.5
REACH = 6

NB = 32
SX = 8
SY = 8
SZ = 128
ROWS = SX * SY
PAIRS = ROWS // 2
FACE = REACH * SY
NPJ = 4
SLOTS = 8192
TGT = 40
CH = NPJ * TGT
GROUPS = ROWS // 4
ZROWS = GROUPS * 16
LANES = 128
F32 = jnp.float32
BF16 = jnp.bfloat16
NN = (((1,), (0,)), ((), ()))
NT = (((1,), (1,)), ((), ()))
VMEM_LIMIT = 40 * 1024 * 1024


def dot(a, b, dims=NN):
    return lax.dot_general(a, b, dims, preferred_element_type=F32)


def split2(v):
    hi = v.astype(BF16)
    return hi, (v - hi.astype(F32)).astype(BF16)


def split3(v):
    hi = v.astype(BF16)
    rest = v - hi.astype(F32)
    mid = rest.astype(BF16)
    return hi, mid, (rest - mid.astype(F32)).astype(BF16)


def z_matrices():
    half = [0.0] + [-0.5 * c for c in STENCIL[1:]]
    inner = np.zeros((SZ, SZ), np.float32)
    face = np.zeros((16, SZ), np.float32)
    for z in range(SZ):
        for source in range(SZ):
            if 1 <= abs(z - source) <= REACH:
                inner[source, z] = half[abs(z - source)]
        for e in range(8):
            if 1 <= abs(SZ + e - z) <= REACH:
                face[e, z] = half[abs(SZ + e - z)]
            if 1 <= abs(z + 8 - e) <= REACH:
                face[8 + e, z] = half[abs(z + 8 - e)]

    def split(m):
        hi = m.astype(jnp.bfloat16)
        return hi, (m - hi.astype(np.float32)).astype(jnp.bfloat16)

    inner_hi, inner_lo = split(inner)
    face_hi, face_lo = split(face)
    first = np.concatenate([inner_hi, inner_hi], axis=0)
    second = np.concatenate(
        [inner_lo, face_hi, face_hi, face_lo, np.zeros((SZ - 48, SZ), jnp.bfloat16)], axis=0
    )
    return jnp.asarray(first), jnp.asarray(second)


def any_specs(count):
    return [pl.BlockSpec(memory_space=pl.ANY)] * count


def vmem_specs(count):
    return [pl.BlockSpec(memory_space=pltpu.VMEM)] * count


PARAMS = pltpu.CompilerParams(vmem_limit_bytes=VMEM_LIMIT)


def rearrange_kernel(src, field, x_low, x_high, y_low, y_high, held, in_sem, out_sem):
    loads = [
        pltpu.make_async_copy(src.at[:, row, :], held.at[row], in_sem.at[row]) for row in range(ROWS)
    ]
    for load in loads:
        load.start()
    for load in loads:
        load.wait()
    held4 = held.reshape(SX, SY, NB, SZ)
    stores = [
        pltpu.make_async_copy(held.at[pl.ds(0, FACE)], x_low, out_sem.at[0]),
        pltpu.make_async_copy(held.at[pl.ds(ROWS - FACE, FACE)], x_high, out_sem.at[1]),
        pltpu.make_async_copy(held4.at[:, pl.ds(0, REACH)], y_low, out_sem.at[2]),
        pltpu.make_async_copy(held4.at[:, pl.ds(SY - REACH, REACH)], y_high, out_sem.at[3]),
        pltpu.make_async_copy(held, field, out_sem.at[4]),
    ]
    for store in stores:
        store.start()
    for store in stores:
        store.wait()


def rearrange(orbitals):
    return pl.pallas_call(
        rearrange_kernel,
        out_shape=[
            jax.ShapeDtypeStruct((ROWS, NB, SZ), F32),
            jax.ShapeDtypeStruct((FACE, NB, SZ), F32),
            jax.ShapeDtypeStruct((FACE, NB, SZ), F32),
            jax.ShapeDtypeStruct((SX, REACH, NB, SZ), F32),
            jax.ShapeDtypeStruct((SX, REACH, NB, SZ), F32),
        ],
        in_specs=any_specs(1),
        out_specs=any_specs(5),
        scratch_shapes=[
            pltpu.VMEM((ROWS, NB, SZ), F32),
            pltpu.SemaphoreType.DMA((ROWS,)),
            pltpu.SemaphoreType.DMA((5,)),
        ],
        compiler_params=PARAMS,
        name="rearrange",
    )(orbitals)


def build_kernel(starts, keys, w0, w1, w2, w3, out, held, weights):
    held[pl.ds(0, SLOTS // LANES), :] = keys[...]
    held[pl.ds(SLOTS // LANES, 8), :] = jnp.full((8, LANES), ROWS * SZ * 64, jnp.int32)
    for j, w in enumerate((w0, w1, w2, w3)):
        weights[j, pl.ds(0, SLOTS // LANES), :] = w[...]
        weights[j, pl.ds(SLOTS // LANES, 8), :] = jnp.zeros((8, LANES), F32)
    target_at = lax.broadcasted_iota(jnp.int32, (TGT, 2 * LANES), 0)
    z_at = lax.broadcasted_iota(jnp.int32, (SZ, 2 * LANES), 0)

    def window(row, block):
        key = jnp.concatenate([held[pl.ds(block, 1), :], held[pl.ds(block + 1, 1), :]], axis=1)
        target = jnp.where((key >> 13) == row, key & 63, 63)
        chosen = target_at == target
        parts = []
        for j in range(NPJ):
            w = jnp.concatenate(
                [weights[j, pl.ds(block, 1), :], weights[j, pl.ds(block + 1, 1), :]], axis=1
            )
            parts.append(jnp.where(chosen, w, 0.0))
        hi, lo = split2(jnp.concatenate(parts, axis=0))
        place = jnp.where(z_at == ((key >> 6) & 127), 1.0, 0.0).astype(BF16)
        both = dot(jnp.concatenate([hi, lo], axis=0), place, NT)
        return both[:CH] + both[CH:]

    @pl.loop(0, PAIRS)
    def _(pair):
        for parity in range(2):
            row = 2 * pair + parity
            low = starts[row]
            high = starts[row + 1]
            base = low // LANES
            windows = (high - base * LANES + 2 * LANES - 1) // (2 * LANES)
            total = window(row, base)

            total = lax.fori_loop(
                1, windows, lambda i, acc: acc + window(row, base + 2 * i), total
            )
            hi, lo = split2(total)
            out[pair, :, pl.ds(parity * SZ, SZ)] = jnp.concatenate([hi, lo], axis=0)


def build(starts, keys, weights):
    return pl.pallas_call(
        build_kernel,
        out_shape=jax.ShapeDtypeStruct((PAIRS, 2 * CH, 2 * SZ), BF16),
        in_specs=[pl.BlockSpec(memory_space=pltpu.SMEM)] + vmem_specs(5),
        out_specs=pl.BlockSpec(memory_space=pltpu.VMEM),
        scratch_shapes=[
            pltpu.VMEM((SLOTS // LANES + 8, LANES), jnp.int32),
            pltpu.VMEM((NPJ, SLOTS // LANES + 8, LANES), F32),
        ],
        compiler_params=PARAMS,
        name="build",
    )(starts, keys, *weights)


def partial_of(mat, values):
    hi, lo = split2(values)
    return dot(mat, jnp.concatenate([hi, lo], axis=0), NT)


def packed_partial(total):
    joined = total[:CH, :NB] + total[:CH, NB:] + total[CH:, :NB]
    return jnp.concatenate([joined[j * TGT : (j + 1) * TGT] for j in range(NPJ)], axis=1)


def z_faces(rows):
    turned = jnp.concatenate(rows, axis=0).T
    return jnp.concatenate([turned[:8], turned[SZ - 8 :]], axis=0)


def first_kernel(field, mat, message, total):
    total[...] = jnp.zeros_like(total)

    @pl.loop(0, SX)
    def _(x):
        acc = total[...]
        for half in range(2):
            rows = [field[x * SY + 4 * half + i] for i in range(4)]
            message[pl.ds((2 * x + half) * 16, 16), :] = z_faces(rows)
            for p in range(2):
                values = jnp.concatenate(rows[2 * p : 2 * p + 2], axis=1)
                acc = acc + partial_of(mat[x * 4 + 2 * half + p], values)
        total[...] = acc

    message[pl.ds(ZROWS, TGT), :] = packed_partial(total[...])


def first(field, mat):
    return pl.pallas_call(
        first_kernel,
        out_shape=jax.ShapeDtypeStruct((ZROWS + TGT, LANES), F32),
        in_specs=vmem_specs(2),
        out_specs=pl.BlockSpec(memory_space=pltpu.VMEM),
        scratch_shapes=[pltpu.VMEM((2 * CH, 2 * NB), F32)],
        compiler_params=PARAMS,
        name="first",
    )(field, mat)


def spread(frame, me, out, at, step, stride):
    row = lax.broadcasted_iota(jnp.int32, (TGT, LANES), 0)
    digit = (row // stride) % 3
    for distance in range(-3, 5):
        slot = (me + distance + 8) % 8
        if abs(distance) > 2:
            piece = jnp.zeros((TGT, LANES), F32)
        else:
            moved = frame if distance == 0 else pltpu.roll(frame, (-stride * distance) % TGT, 0)
            valid = (digit + distance >= 0) & (digit + distance <= 2) & (row < 36)
            piece = jnp.where(valid, moved, 0.0)
        out[slot, pl.ds(at, TGT), :] = piece


def spread_z_kernel(frames, me, mine, other, out):
    row = lax.broadcasted_iota(jnp.int32, (TGT, LANES), 0)
    for f in range(frames):
        theirs = other[pl.ds(f * TGT, TGT), :]
        swapped = jnp.where(
            row & 2 == 0, pltpu.roll(theirs, TGT - 2, 0), pltpu.roll(theirs, 2, 0)
        )
        spread(mine[pl.ds(f * TGT, TGT), :] + swapped, me[0], out, f * TGT, 1, 4)


def spread_x_kernel(frames, me, came, out):
    for f in range(frames):
        frame = came[0, pl.ds(f * TGT, TGT), :]
        for slot in range(1, 8):
            frame = frame + came[slot, pl.ds(f * TGT, TGT), :]
        spread(frame, me[0], out, f * TGT, 1, 12)


def spread_call(kernel, frames, me, *arrays):
    return pl.pallas_call(
        functools.partial(kernel, frames),
        out_shape=jax.ShapeDtypeStruct((8, frames * TGT, LANES), F32),
        in_specs=[pl.BlockSpec(memory_space=pltpu.SMEM)] + vmem_specs(len(arrays)),
        out_specs=pl.BlockSpec(memory_space=pltpu.VMEM),
        compiler_params=PARAMS,
        name="spread",
    )(me, *arrays)


def step_kernel(
    first_step, last_step,
    field, previous, x_left, x_right, y_left, y_right, faces, came, coupling, potential, mat, first_z, second_z,
    *rest,
):
    if last_step:
        (new, gram), rest = rest[:2], rest[2:]
    else:
        (new, x_low, x_high, y_low, y_high, message), rest = rest[:6], rest[6:]
    (
        wide, y_left_v, y_right_v, old, faces_v, came_v, coupling_v, potential_v, mat_v, first_v, second_v,
        made, message_v, total, coef, in_sem, mat_sem, out_sem,
    ) = rest
    shifted = 0 if first_step else 1
    alpha = (1.0 if first_step else 2.0) / FILTER_HALF
    half = [0.0] + [-0.5 * c for c in STENCIL[1:]]
    diagonal = -1.5 * STENCIL[0] - FILTER_CENTRE

    loads = [
        pltpu.make_async_copy(came, came_v, in_sem.at[0]),
        pltpu.make_async_copy(coupling, coupling_v, in_sem.at[1]),
        pltpu.make_async_copy(field, wide.at[pl.ds(FACE, ROWS)], in_sem.at[2]),
        pltpu.make_async_copy(x_left, wide.at[pl.ds(0, FACE)], in_sem.at[3]),
        pltpu.make_async_copy(x_right, wide.at[pl.ds(FACE + ROWS, FACE)], in_sem.at[4]),
        pltpu.make_async_copy(y_left, y_left_v, in_sem.at[5]),
        pltpu.make_async_copy(y_right, y_right_v, in_sem.at[6]),
        pltpu.make_async_copy(faces.at[pl.ds(0, ZROWS)], faces_v, in_sem.at[7]),
        pltpu.make_async_copy(potential, potential_v, in_sem.at[8]),
        pltpu.make_async_copy(first_z, first_v, in_sem.at[9]),
        pltpu.make_async_copy(second_z, second_v, in_sem.at[10]),
    ]
    if shifted:
        loads.append(pltpu.make_async_copy(previous, old, in_sem.at[11]))
    mat_loads = [
        pltpu.make_async_copy(mat.at[pl.ds(4 * x, 4)], mat_v.at[pl.ds(4 * x, 4)], mat_sem.at[x])
        for x in range(SX)
    ]
    for load in loads:
        load.start()
    for load in mat_loads:
        load.start()
    loads[0].wait()
    loads[1].wait()
    frame = came_v[0]
    for slot in range(1, 8):
        frame = frame + came_v[slot]
    frame = frame * coupling_v[...]
    stacked = jnp.concatenate([frame[:, j * NB : (j + 1) * NB] for j in range(NPJ)], axis=0)
    turned = stacked.T
    coef_hi = turned.astype(BF16).astype(F32)
    coef[pl.ds(0, NB), :] = jnp.concatenate([coef_hi, coef_hi], axis=1).astype(BF16)
    coef[pl.ds(NB, NB), pl.ds(0, CH)] = (turned - coef_hi).astype(BF16)
    total[...] = jnp.zeros_like(total)
    for load in loads[2:]:
        load.wait()

    def out_copies(x):
        rows = made.at[pl.ds(x * SY, SY)]
        copies = [pltpu.make_async_copy(rows, new.at[pl.ds(x * SY, SY)], out_sem.at[0, x])]
        if not last_step:
            copies += [
                pltpu.make_async_copy(made.at[pl.ds(x * SY, REACH)], y_low.at[x], out_sem.at[1, x]),
                pltpu.make_async_copy(
                    made.at[pl.ds(x * SY + SY - REACH, REACH)], y_high.at[x], out_sem.at[2, x]
                ),
            ]
        return copies

    def x_low_copy(x):
        return pltpu.make_async_copy(
            made.at[pl.ds(x * SY, SY)], x_low.at[pl.ds(x * SY, SY)], out_sem.at[3, x]
        )

    def x_high_copy(x):
        return pltpu.make_async_copy(
            made.at[pl.ds(x * SY, SY)],
            x_high.at[pl.ds((x - (SX - REACH)) * SY, SY)],
            out_sem.at[4, x],
        )

    @pl.loop(0, SX)
    def _(x):
        pltpu.make_async_copy(
            mat.at[pl.ds(4 * x, 4)], mat_v.at[pl.ds(4 * x, 4)], mat_sem.at[x]
        ).wait()
        c_hi = coef[pl.ds(0, NB), :]
        c_lo = coef[pl.ds(NB, NB), pl.ds(0, CH)]
        middle = (x + REACH) * SY

        def row_at(y):
            if y < 0:
                return y_left_v[x, y + REACH]
            if y >= SY:
                return y_right_v[x, y - SY]
            return wide[middle + y]

        acc = None
        for part in range(2):
            rows = [row_at(4 * part + i) for i in range(4)]
            block = jnp.concatenate(rows, axis=0)
            hi, lo = split2(block)
            face = faces_v[pl.ds((2 * x + part) * 16, 16), :]
            face_hi = face.astype(BF16).astype(F32)
            side = jnp.concatenate(
                [face_hi, face - face_hi, face_hi, jnp.zeros((LANES - 48, LANES), F32)], axis=0
            ).T.astype(BF16)
            along_z = dot(jnp.concatenate([hi, lo], axis=1), first_v[...]) + dot(
                jnp.concatenate([hi, side], axis=1), second_v[...]
            )
            made_rows = []
            for p in range(2):
                pair_mat = mat_v[x * 4 + 2 * part + p]
                nonlocal_part = dot(c_hi, pair_mat) + dot(c_lo, pair_mat[:CH])
                for q in range(2):
                    i = 2 * p + q
                    y = 4 * part + i
                    value = rows[i]
                    summed = along_z[i * NB : (i + 1) * NB] + nonlocal_part[:, q * SZ : (q + 1) * SZ]
                    for m in range(1, REACH + 1):
                        around = (wide[middle + y + m * SY] + wide[middle + y - m * SY]) + (
                            row_at(y + m) + row_at(y - m)
                        )
                        summed = summed + half[m] * around
                    summed = summed + (potential_v[pl.ds(x * SY + y, 1), :] + diagonal) * value
                    result = alpha * summed
                    if shifted:
                        result = result - old[x * SY + y]
                    made[x * SY + y] = result
                    made_rows.append(result)
            if last_step:
                for p in range(2):
                    parts = split3(jnp.concatenate(made_rows[2 * p : 2 * p + 2], axis=1))
                    joined = jnp.concatenate(parts, axis=0)
                    here = dot(joined, joined, NT)
                    acc = here if acc is None else acc + here
            else:
                message_v[pl.ds((2 * x + part) * 16, 16), :] = z_faces(made_rows)
                for p in range(2):
                    values = jnp.concatenate(made_rows[2 * p : 2 * p + 2], axis=1)
                    here = partial_of(mat_v[x * 4 + 2 * part + p], values)
                    acc = here if acc is None else acc + here
        total[...] = total[...] + acc
        for copy in out_copies(x):
            copy.start()
        if not last_step:

            @pl.when(x < REACH)
            def _():
                x_low_copy(x).start()

            @pl.when(x >= SX - REACH)
            def _():
                x_high_copy(x).start()

    if last_step:
        t = total[...]
        summed = t[2 * NB :, :NB] + t[:NB, 2 * NB :] + t[NB : 2 * NB, NB : 2 * NB]
        summed = summed + (t[NB : 2 * NB, :NB] + t[:NB, NB : 2 * NB]) + t[:NB, :NB]
        message_v[...] = jnp.concatenate([summed[8 * q : 8 * q + 8] for q in range(4)], axis=1)
        final = pltpu.make_async_copy(message_v, gram, in_sem.at[12])
    else:
        message_v[pl.ds(ZROWS, TGT), :] = packed_partial(total[...])
        final = pltpu.make_async_copy(message_v, message, in_sem.at[12])
    final.start()
    for x in range(SX):
        for copy in out_copies(x):
            copy.wait()
        if not last_step:
            if x < REACH:
                x_low_copy(x).wait()
            if x >= SX - REACH:
                x_high_copy(x).wait()
    final.wait()


def step(first_step, last_step, *arrays):
    block = jax.ShapeDtypeStruct((ROWS, NB, SZ), F32)
    x_face = jax.ShapeDtypeStruct((FACE, NB, SZ), F32)
    y_face = jax.ShapeDtypeStruct((SX, REACH, NB, SZ), F32)
    if last_step:
        message_rows = 8
        total = (3 * NB, 3 * NB)
        outs = [block, jax.ShapeDtypeStruct((message_rows, LANES), F32)]
    else:
        message_rows = ZROWS + TGT
        total = (2 * CH, 2 * NB)
        outs = [block, x_face, x_face, y_face, y_face, jax.ShapeDtypeStruct((message_rows, LANES), F32)]
    return pl.pallas_call(
        functools.partial(step_kernel, first_step, last_step),
        out_shape=outs,
        in_specs=any_specs(len(arrays)),
        out_specs=any_specs(len(outs)),
        scratch_shapes=[
            pltpu.VMEM((ROWS + 2 * FACE, NB, SZ), F32),
            pltpu.VMEM((SX, REACH, NB, SZ), F32),
            pltpu.VMEM((SX, REACH, NB, SZ), F32),
            pltpu.VMEM((ROWS, NB, SZ), F32),
            pltpu.VMEM((ZROWS, LANES), F32),
            pltpu.VMEM((8, TGT, LANES), F32),
            pltpu.VMEM((TGT, LANES), F32),
            pltpu.VMEM((ROWS, SZ), F32),
            pltpu.VMEM((PAIRS, 2 * CH, 2 * SZ), BF16),
            pltpu.VMEM((2 * SZ, SZ), BF16),
            pltpu.VMEM((2 * SZ, SZ), BF16),
            pltpu.VMEM((ROWS, NB, SZ), F32),
            pltpu.VMEM((message_rows, LANES), F32),
            pltpu.VMEM(total, F32),
            pltpu.VMEM((2 * NB, 2 * CH), BF16),
            pltpu.SemaphoreType.DMA((13,)),
            pltpu.SemaphoreType.DMA((SX,)),
            pltpu.SemaphoreType.DMA((5, SX)),
        ],
        compiler_params=PARAMS,
        name="step",
    )(*arrays)


def finish_kernel(scale, field, grams, out, held, made, inverse, in_sem, out_sem):
    loads = [
        pltpu.make_async_copy(field.at[pl.ds(x * SY, SY)], held.at[pl.ds(x * SY, SY)], in_sem.at[x])
        for x in range(SX)
    ]
    for load in loads:
        load.start()
    packed = grams[0]
    for slot in range(1, grams.shape[0]):
        packed = packed + grams[slot]
    packed = packed * scale
    gram = jnp.concatenate([packed[:, q * NB : (q + 1) * NB] for q in range(4)], axis=0)
    row = lax.broadcasted_iota(jnp.int32, (NB, NB), 0)
    column = lax.broadcasted_iota(jnp.int32, (NB, NB), 1)
    eye = jnp.where(row == column, 1.0, 0.0)
    work = jnp.concatenate([gram, eye], axis=1)
    below = lax.broadcasted_iota(jnp.int32, (NB, 2 * NB), 0)
    for k in range(NB):
        root = 1.0 / jnp.sqrt(work[k : k + 1, k : k + 1])
        line = work[k : k + 1, :] * root
        inverse[pl.ds(k, 1), :] = line[:, NB:]
        if k < NB - 1:
            factor = work[:, k : k + 1] * root
            work = work - jnp.where(below > k, factor * line, 0.0)
    hi, mid, lo = split3(inverse[...])
    left = jnp.concatenate([lo, mid, hi, mid, hi, hi], axis=1)

    @pl.loop(0, SX)
    def _(x):
        pltpu.make_async_copy(
            field.at[pl.ds(x * SY, SY)], held.at[pl.ds(x * SY, SY)], in_sem.at[x]
        ).wait()
        for p in range(SY // 2):
            at = x * SY + 2 * p
            values = jnp.concatenate([held[at], held[at + 1]], axis=1)
            f_hi, f_mid, f_lo = split3(values)
            right = jnp.concatenate([f_hi, f_mid, f_lo, f_hi, f_mid, f_hi], axis=0)
            result = dot(left, right)
            made[at] = result[:, :SZ]
            made[at + 1] = result[:, SZ:]
            for q in range(2):
                pltpu.make_async_copy(made.at[at + q], out.at[:, at + q, :], out_sem.at[at + q]).start()

    for r in range(ROWS):
        pltpu.make_async_copy(made.at[r], out.at[:, r, :], out_sem.at[r]).wait()


def finish(scale, field, grams):
    return pl.pallas_call(
        functools.partial(finish_kernel, scale),
        out_shape=jax.ShapeDtypeStruct((NB, ROWS, SZ), F32),
        in_specs=any_specs(1) + vmem_specs(1),
        out_specs=pl.BlockSpec(memory_space=pl.ANY),
        scratch_shapes=[
            pltpu.VMEM((ROWS, NB, SZ), F32),
            pltpu.VMEM((ROWS, NB, SZ), F32),
            pltpu.VMEM((NB, NB), F32),
            pltpu.SemaphoreType.DMA((SX,)),
            pltpu.SemaphoreType.DMA((ROWS,)),
        ],
        compiler_params=PARAMS,
        name="finish",
    )(field, grams)


def shift(value, axis, by):
    count = lax.axis_size(axis)
    return lax.ppermute(value, axis, [(i, (i + by) % count) for i in range(count)])


def local(orbitals, potential, projector, point_cell, target, point_count, coupling):
    bands, size_x, size_y, size_z = orbitals.shape
    me_x = lax.axis_index("gx").astype(jnp.int32).reshape(1)
    me_y = lax.axis_index("gy").astype(jnp.int32).reshape(1)

    field, x_low, x_high, y_low, y_high = rearrange(orbitals.reshape(NB, ROWS, SZ))
    pot = potential.reshape(ROWS, SZ)
    first_z, second_z = z_matrices()

    alive = lax.iota(jnp.int32, SLOTS) < point_count.reshape(())
    code = target // 2
    z_other = (code % 3 != 1).astype(jnp.int32)
    wanted = ((code // 3) * 2 + z_other) * 2 + target % 2
    key = jnp.where(alive, point_cell * 64 + wanted, ROWS * SZ * 64)
    starts = jnp.sum(
        (key[None, :] < (lax.iota(jnp.int32, ROWS + 1) * (SZ * 64))[:, None]).astype(jnp.int32), axis=1
    )
    ordered = lax.sort((key,) + tuple(projector[j] for j in range(NPJ)), num_keys=1, is_stable=False)
    ordered = [o.reshape(SLOTS // LANES, LANES) for o in ordered]
    mat = build(starts, ordered[0], ordered[1:])

    own = jnp.repeat(coupling, NB, axis=1)
    coupling_frame = jnp.zeros((TGT, LANES), F32).at[16:18].set(own)

    message = first(field, mat)
    previous = field
    scale_frame = None
    for k in range(DEGREE):
        x_left = shift(x_high, "gx", 1)
        x_right = shift(x_low, "gx", -1)
        y_left = shift(y_high, "gy", 1)
        y_right = shift(y_low, "gy", -1)
        if k == 0:
            message = jnp.concatenate([message, coupling_frame], axis=0)
        other = shift(message, "gz", 1)
        frames = 2 if k == 0 else 1
        sends = spread_call(spread_z_kernel, frames, me_y, message[ZROWS:], other[ZROWS:])
        came = lax.all_to_all(sends, "gy", 0, 0)
        sends = spread_call(spread_x_kernel, frames, me_x, came)
        came = lax.all_to_all(sends, "gx", 0, 0)
        if k == 0:
            scale_frame = jnp.sum(came[:, TGT:], axis=0)
            came = came[:, :TGT]
        outs = step(
            k == 0, k == DEGREE - 1,
            field, previous, x_left, x_right, y_left, y_right, other, came, scale_frame, pot, mat, first_z, second_z,
        )
        previous = field
        if k < DEGREE - 1:
            field, x_low, x_high, y_low, y_high, message = outs
        else:
            field, gram = outs
    axes = ("gx", "gy", "gz")
    devices = 1
    for axis in axes:
        devices *= lax.axis_size(axis)
    grams = lax.all_to_all(jnp.broadcast_to(gram[None], (devices,) + gram.shape), axes, 0, 0)
    result = finish(1.0 / float(devices * ROWS * SZ), field, grams)
    return result.reshape(bands, size_x, size_y, size_z)


def solution(mesh):
    in_specs = (
        P(None, "gx", "gy", "gz"),
        P("gx", "gy", "gz"),
        P(None, ("gx", "gy", "gz")),
        P(("gx", "gy", "gz")),
        P(("gx", "gy", "gz")),
        P("gx", "gy", "gz"),
        P(("gx", "gy", "gz"), None),
    )
    out_specs = P(None, "gx", "gy", "gz")
    return jax.shard_map(local, mesh=mesh, in_specs=in_specs, out_specs=out_specs, check_vma=False)
```

```python
import functools

import jax
import jax.numpy as jnp
import numpy as np
from jax import lax
from jax.experimental import pallas as pl
from jax.experimental.pallas import tpu as pltpu
from jax.sharding import PartitionSpec as P

DEGREE = 4
STENCIL = (
    -5369.0 / 1800.0,
    12.0 / 7.0,
    -15.0 / 56.0,
    10.0 / 189.0,
    -1.0 / 112.0,
    2.0 / 1925.0,
    -1.0 / 16632.0,
)
FILTER_CENTRE = 9.5
FILTER_HALF = 5.5
REACH = 6

NB = 32
SX = 8
SY = 8
SZ = 128
ROWS = SX * SY
PAIRS = ROWS // 2
FACE = REACH * SY
NPJ = 4
SLOTS = 8192
TGT = 40
CH = NPJ * TGT
GROUPS = ROWS // 4
TOTAL = (2 * CH, 2 * NB)
ZROWS = GROUPS * 16
LANES = 128
F32 = jnp.float32
BF16 = jnp.bfloat16
NN = (((1,), (0,)), ((), ()))
NT = (((1,), (1,)), ((), ()))
VMEM_LIMIT = 32 * 1024 * 1024


def dot(a, b, dims=NN):
    return lax.dot_general(a, b, dims, preferred_element_type=F32)


def split2(v):
    hi = v.astype(BF16)
    return hi, (v - hi.astype(F32)).astype(BF16)


def split3(v):
    hi = v.astype(BF16)
    rest = v - hi.astype(F32)
    mid = rest.astype(BF16)
    return hi, mid, (rest - mid.astype(F32)).astype(BF16)


def z_matrices():
    half = [0.0] + [-0.5 * c for c in STENCIL[1:]]
    inner = np.zeros((SZ, SZ), np.float32)
    face = np.zeros((16, SZ), np.float32)
    for z in range(SZ):
        for source in range(SZ):
            if 1 <= abs(z - source) <= REACH:
                inner[source, z] = half[abs(z - source)]
        for e in range(8):
            if 1 <= abs(SZ + e - z) <= REACH:
                face[e, z] = half[abs(SZ + e - z)]
            if 1 <= abs(z + 8 - e) <= REACH:
                face[8 + e, z] = half[abs(z + 8 - e)]

    def split(m):
        hi = m.astype(jnp.bfloat16)
        return hi, (m - hi.astype(np.float32)).astype(jnp.bfloat16)

    inner_hi, inner_lo = split(inner)
    face_hi, face_lo = split(face)
    first = np.concatenate([inner_hi, inner_hi], axis=0)
    second = np.concatenate(
        [inner_lo, face_hi, face_hi, face_lo, np.zeros((SZ - 48, SZ), jnp.bfloat16)], axis=0
    )
    return jnp.asarray(first), jnp.asarray(second)


def any_specs(count):
    return [pl.BlockSpec(memory_space=pl.ANY)] * count


def vmem_specs(count):
    return [pl.BlockSpec(memory_space=pltpu.VMEM)] * count


PARAMS = pltpu.CompilerParams(vmem_limit_bytes=VMEM_LIMIT)


def cost(us):
    return pl.CostEstimate(flops=0, bytes_accessed=int(us * 3.5e6), transcendentals=0)


def z_faces(rows):
    turned = jnp.concatenate(rows, axis=0).T
    return jnp.concatenate([turned[:8], turned[SZ - 8 :]], axis=0)


def write_faces(field, x_low, x_high, y_low, y_high):
    x_low[...] = field[pl.ds(0, FACE)]
    x_high[...] = field[pl.ds(ROWS - FACE, FACE)]
    for x in range(SX):
        y_low[x] = field[pl.ds(x * SY, REACH)]
        y_high[x] = field[pl.ds(x * SY + SY - REACH, REACH)]


BLOCK = jax.ShapeDtypeStruct((ROWS, NB, SZ), F32)
X_FACE = jax.ShapeDtypeStruct((FACE, NB, SZ), F32)
Y_FACE = jax.ShapeDtypeStruct((SX, REACH, NB, SZ), F32)
Z_FACE = jax.ShapeDtypeStruct((ZROWS, LANES), F32)
FACES = [X_FACE, X_FACE, Y_FACE, Y_FACE, Z_FACE]


def rearrange_kernel(src, field, x_low, x_high, y_low, y_high, z_face, in_sem):
    loads = [
        pltpu.make_async_copy(src.at[:, row, :], field.at[row], in_sem.at[row]) for row in range(ROWS)
    ]
    for load in loads:
        load.start()
    for load in loads:
        load.wait()
    write_faces(field, x_low, x_high, y_low, y_high)
    for g in range(GROUPS):
        z_face[pl.ds(16 * g, 16), :] = z_faces([field[4 * g + i] for i in range(4)])


def rearrange(orbitals):
    return pl.pallas_call(
        rearrange_kernel,
        out_shape=[BLOCK] + FACES,
        in_specs=any_specs(1),
        out_specs=vmem_specs(6),
        scratch_shapes=[pltpu.SemaphoreType.DMA((ROWS,))],
        compiler_params=PARAMS,
        cost_estimate=cost(3),
        name="rearrange",
    )(orbitals)


def build_kernel(starts, keys, w0, w1, w2, w3, out, held, weights):
    held[pl.ds(0, SLOTS // LANES), :] = keys[...]
    held[pl.ds(SLOTS // LANES, 8), :] = jnp.full((8, LANES), ROWS * SZ * 64, jnp.int32)
    for j, w in enumerate((w0, w1, w2, w3)):
        weights[j, pl.ds(0, SLOTS // LANES), :] = w[...]
        weights[j, pl.ds(SLOTS // LANES, 8), :] = jnp.zeros((8, LANES), F32)
    target_at = lax.broadcasted_iota(jnp.int32, (TGT, 2 * LANES), 0)
    z_at = lax.broadcasted_iota(jnp.int32, (SZ, 2 * LANES), 0)

    def window(row, block):
        key = jnp.concatenate([held[pl.ds(block, 1), :], held[pl.ds(block + 1, 1), :]], axis=1)
        target = jnp.where((key >> 13) == row, key & 63, 63)
        chosen = target_at == target
        parts = []
        for j in range(NPJ):
            w = jnp.concatenate(
                [weights[j, pl.ds(block, 1), :], weights[j, pl.ds(block + 1, 1), :]], axis=1
            )
            parts.append(jnp.where(chosen, w, 0.0))
        hi, lo = split2(jnp.concatenate(parts, axis=0))
        place = jnp.where(z_at == ((key >> 6) & 127), 1.0, 0.0).astype(BF16)
        both = dot(jnp.concatenate([hi, lo], axis=0), place, NT)
        return both[:CH] + both[CH:]

    @pl.loop(0, PAIRS)
    def _(pair):
        for parity in range(2):
            row = 2 * pair + parity
            low = starts[row]
            high = starts[row + 1]
            base = low // LANES
            windows = (high - base * LANES + 2 * LANES - 1) // (2 * LANES)
            total = window(row, base)

            total = lax.fori_loop(
                1, windows, lambda i, acc: acc + window(row, base + 2 * i), total
            )
            hi, lo = split2(total)
            out[pair, :, pl.ds(parity * SZ, SZ)] = jnp.concatenate([hi, lo], axis=0)


def build(starts, keys, weights):
    return pl.pallas_call(
        build_kernel,
        out_shape=jax.ShapeDtypeStruct((PAIRS, 2 * CH, 2 * SZ), BF16),
        in_specs=[pl.BlockSpec(memory_space=pltpu.SMEM)] + vmem_specs(5),
        out_specs=pl.BlockSpec(memory_space=pltpu.VMEM),
        scratch_shapes=[
            pltpu.VMEM((SLOTS // LANES + 8, LANES), jnp.int32),
            pltpu.VMEM((NPJ, SLOTS // LANES + 8, LANES), F32),
        ],
        compiler_params=PARAMS,
        cost_estimate=cost(15),
        name="build",
    )(starts, keys, *weights)


def partial_of(mat, values):
    hi, lo = split2(values)
    return dot(mat, jnp.concatenate([hi, lo], axis=0), NT)


def packed_partial(total):
    joined = total[:CH, :NB] + total[:CH, NB:] + total[CH:, :NB]
    return jnp.concatenate([joined[j * TGT : (j + 1) * TGT] for j in range(NPJ)], axis=1)


def first_kernel(field, mat, out, total):
    total[...] = jnp.zeros_like(total)

    @pl.loop(0, SX)
    def _(x):
        acc = total[...]
        for p in range(4):
            at = x * SY + 2 * p
            values = jnp.concatenate([field[at], field[at + 1]], axis=1)
            acc = acc + partial_of(mat[x * 4 + p], values)
        total[...] = acc

    out[...] = packed_partial(total[...])


def first(field, mat):
    return pl.pallas_call(
        first_kernel,
        out_shape=jax.ShapeDtypeStruct((TGT, LANES), F32),
        in_specs=vmem_specs(2),
        out_specs=pl.BlockSpec(memory_space=pltpu.VMEM),
        scratch_shapes=[pltpu.VMEM(TOTAL, F32)],
        compiler_params=PARAMS,
        cost_estimate=cost(3),
        name="first",
    )(field, mat)


def pieces(frame, stride):
    row = lax.broadcasted_iota(jnp.int32, (TGT, LANES), 0)
    digit = (row // stride) % 3
    for distance in range(-2, 3):
        moved = frame if distance == 0 else pltpu.roll(frame, (-stride * distance) % TGT, 0)
        valid = (digit + distance >= 0) & (digit + distance <= 2) & (row < 36)
        yield distance, jnp.where(valid, moved, 0.0)


def spread_y_kernel(frames, me, mine, out):
    for f in range(frames):
        at = pl.ds(f * TGT, TGT)
        for distance in (-3, 3, 4):
            out[(me[0] + distance + 8) % 8, at, :] = jnp.zeros((TGT, LANES), F32)
        for distance, piece in pieces(mine[at, :], 4):
            out[(me[0] + distance + 8) % 8, at, :] = piece


def spread_xz_kernel(frames, me, came, out):
    row = lax.broadcasted_iota(jnp.int32, (TGT, LANES), 0)
    for f in range(frames):
        at = pl.ds(f * TGT, TGT)
        frame = came[0, at, :]
        for slot in range(1, 8):
            frame = frame + came[slot, at, :]
        for distance in (-3, 3, 4):
            for z in range(2):
                out[((me[0] + distance + 8) % 8) * 2 + z, at, :] = jnp.zeros((TGT, LANES), F32)
        for distance, piece in pieces(frame, 12):
            swapped = jnp.where(
                row & 2 == 0, pltpu.roll(piece, TGT - 2, 0), pltpu.roll(piece, 2, 0)
            )
            slot = ((me[0] + distance + 8) % 8) * 2
            out[slot + me[1], at, :] = piece
            out[slot + 1 - me[1], at, :] = swapped


def spread_call(kernel, slots, frames, me, array):
    return pl.pallas_call(
        functools.partial(kernel, frames),
        out_shape=jax.ShapeDtypeStruct((slots, frames * TGT, LANES), F32),
        in_specs=[pl.BlockSpec(memory_space=pltpu.SMEM)] + vmem_specs(1),
        out_specs=pl.BlockSpec(memory_space=pltpu.VMEM),
        compiler_params=PARAMS,
        cost_estimate=cost(0.7),
        name="spread",
    )(me, array)


def local_kernel(first_step, *refs):
    if first_step:
        field, x_left, x_right, y_left, y_right, faces, potential, first_z, second_z, out = refs
        previous = None
    else:
        field, previous, x_left, x_right, y_left, y_right, faces, potential, first_z, second_z, out = refs
    alpha = (1.0 if first_step else 2.0) / FILTER_HALF
    half = [0.0] + [-0.5 * c for c in STENCIL[1:]]
    diagonal = -1.5 * STENCIL[0] - FILTER_CENTRE

    def at(x, y):
        if x < 0:
            return x_left[(x + REACH) * SY + y]
        if x >= SX:
            return x_right[(x - SX) * SY + y]
        if y < 0:
            return y_left[x, y + REACH]
        if y >= SY:
            return y_right[x, y - SY]
        return field[x * SY + y]

    for g in range(GROUPS):
        rows = [field[4 * g + i] for i in range(4)]
        hi, lo = split2(jnp.concatenate(rows, axis=0))
        face = faces[pl.ds(g * 16, 16), :]
        face_hi = face.astype(BF16).astype(F32)
        side = jnp.concatenate(
            [face_hi, face - face_hi, face_hi, jnp.zeros((LANES - 48, LANES), F32)], axis=0
        ).T.astype(BF16)
        along_z = dot(jnp.concatenate([hi, lo], axis=1), first_z[...]) + dot(
            jnp.concatenate([hi, side], axis=1), second_z[...]
        )
        for i in range(4):
            x, y = divmod(4 * g + i, SY)
            summed = along_z[i * NB : (i + 1) * NB]
            for m in range(1, REACH + 1):
                around = (at(x + m, y) + at(x - m, y)) + (at(x, y + m) + at(x, y - m))
                summed = summed + half[m] * around
            summed = summed + (potential[pl.ds(4 * g + i, 1), :] + diagonal) * rows[i]
            result = alpha * summed
            if not first_step:
                result = result - previous[4 * g + i]
            out[4 * g + i] = result


def local_part(first_step, *arrays):
    return pl.pallas_call(
        functools.partial(local_kernel, first_step),
        out_shape=BLOCK,
        in_specs=vmem_specs(len(arrays)),
        out_specs=pl.BlockSpec(memory_space=pltpu.VMEM),
        compiler_params=PARAMS,
        cost_estimate=cost(4),
        name="local",
    )(*arrays)


def coupled_kernel(first_step, last_step, *refs):
    if first_step:
        (base, came, mat), refs = refs[:3], refs[3:]
    else:
        (base, came, mat, coupling), refs = refs[:4], refs[4:]
    if last_step:
        new, gram, total, coef = refs
    else:
        (new, x_low, x_high, y_low, y_high, z_face, partial), refs = refs[:7], refs[7:]
        if first_step:
            coupling, refs = refs[0], refs[1:]
        total, coef = refs
    alpha = (1.0 if first_step else 2.0) / FILTER_HALF
    frame = came[0]
    for slot in range(1, came.shape[0]):
        frame = frame + came[slot]
    if first_step:
        coupling[...] = frame[TGT:]
        frame = frame[:TGT]
    frame = frame * (alpha * coupling[...])
    stacked = jnp.concatenate([frame[:, j * NB : (j + 1) * NB] for j in range(NPJ)], axis=0)
    turned = stacked.T
    coef_hi = turned.astype(BF16).astype(F32)
    coef[pl.ds(0, NB), :] = jnp.concatenate([coef_hi, coef_hi], axis=1).astype(BF16)
    coef[pl.ds(NB, NB), pl.ds(0, CH)] = (turned - coef_hi).astype(BF16)
    total[...] = jnp.zeros_like(total)

    @pl.loop(0, SX)
    def _(x):
        c_hi = coef[pl.ds(0, NB), :]
        c_lo = coef[pl.ds(NB, NB), pl.ds(0, CH)]
        acc = total[...]
        for part in range(2):
            rows = []
            for p in range(2):
                pair_mat = mat[x * 4 + 2 * part + p]
                added = dot(c_hi, pair_mat) + dot(c_lo, pair_mat[:CH])
                for q in range(2):
                    at = x * SY + 4 * part + 2 * p + q
                    result = base[at] + added[:, q * SZ : (q + 1) * SZ]
                    new[at] = result
                    rows.append(result)
            for p in range(2):
                values = jnp.concatenate(rows[2 * p : 2 * p + 2], axis=1)
                if last_step:
                    joined = jnp.concatenate(split3(values), axis=0)
                    acc = acc + dot(joined, joined, NT)
                else:
                    acc = acc + partial_of(mat[x * 4 + 2 * part + p], values)
            if not last_step:
                z_face[pl.ds((2 * x + part) * 16, 16), :] = z_faces(rows)
        total[...] = acc

    if last_step:
        t = total[...]
        summed = t[2 * NB :, :NB] + t[:NB, 2 * NB :] + t[NB : 2 * NB, NB : 2 * NB]
        summed = summed + (t[NB : 2 * NB, :NB] + t[:NB, NB : 2 * NB]) + t[:NB, :NB]
        gram[...] = jnp.concatenate([summed[8 * q : 8 * q + 8] for q in range(4)], axis=1)
    else:
        partial[...] = packed_partial(total[...])
        write_faces(new, x_low, x_high, y_low, y_high)


def coupled_part(first_step, last_step, *arrays):
    frame = jax.ShapeDtypeStruct((TGT, LANES), F32)
    if last_step:
        outs, total = [BLOCK, jax.ShapeDtypeStruct((8, LANES), F32)], (3 * NB, 3 * NB)
    else:
        outs, total = [BLOCK] + FACES + [frame], TOTAL
        if first_step:
            outs.append(frame)
    return pl.pallas_call(
        functools.partial(coupled_kernel, first_step, last_step),
        out_shape=outs,
        in_specs=vmem_specs(len(arrays)),
        out_specs=vmem_specs(len(outs)),
        scratch_shapes=[pltpu.VMEM(total, F32), pltpu.VMEM((2 * NB, 2 * CH), BF16)],
        compiler_params=PARAMS,
        cost_estimate=cost(6),
        name="coupled",
    )(*arrays)


def finish_kernel(scale, field, grams, out, held, made, inverse, in_sem, out_sem):
    loads = [
        pltpu.make_async_copy(field.at[pl.ds(x * SY, SY)], held.at[pl.ds(x * SY, SY)], in_sem.at[x])
        for x in range(SX)
    ]
    for load in loads:
        load.start()
    packed = grams[0]
    for slot in range(1, grams.shape[0]):
        packed = packed + grams[slot]
    packed = packed * scale
    gram = jnp.concatenate([packed[:, q * NB : (q + 1) * NB] for q in range(4)], axis=0)
    row = lax.broadcasted_iota(jnp.int32, (NB, NB), 0)
    column = lax.broadcasted_iota(jnp.int32, (NB, NB), 1)
    eye = jnp.where(row == column, 1.0, 0.0)
    work = jnp.concatenate([gram, eye], axis=1)
    below = lax.broadcasted_iota(jnp.int32, (NB, 2 * NB), 0)
    for k in range(NB):
        root = 1.0 / jnp.sqrt(work[k : k + 1, k : k + 1])
        line = work[k : k + 1, :] * root
        inverse[pl.ds(k, 1), :] = line[:, NB:]
        if k < NB - 1:
            factor = work[:, k : k + 1] * root
            work = work - jnp.where(below > k, factor * line, 0.0)
    hi, mid, lo = split3(inverse[...])
    left = jnp.concatenate([lo, mid, hi, mid, hi, hi], axis=1)

    @pl.loop(0, SX)
    def _(x):
        pltpu.make_async_copy(
            field.at[pl.ds(x * SY, SY)], held.at[pl.ds(x * SY, SY)], in_sem.at[x]
        ).wait()
        for p in range(SY // 2):
            at = x * SY + 2 * p
            values = jnp.concatenate([held[at], held[at + 1]], axis=1)
            f_hi, f_mid, f_lo = split3(values)
            right = jnp.concatenate([f_hi, f_mid, f_lo, f_hi, f_mid, f_hi], axis=0)
            result = dot(left, right)
            made[at] = result[:, :SZ]
            made[at + 1] = result[:, SZ:]
            for q in range(2):
                pltpu.make_async_copy(made.at[at + q], out.at[:, at + q, :], out_sem.at[at + q]).start()

    for r in range(ROWS):
        pltpu.make_async_copy(made.at[r], out.at[:, r, :], out_sem.at[r]).wait()


def finish(scale, field, grams):
    return pl.pallas_call(
        functools.partial(finish_kernel, scale),
        out_shape=jax.ShapeDtypeStruct((NB, ROWS, SZ), F32),
        in_specs=any_specs(1) + vmem_specs(1),
        out_specs=pl.BlockSpec(memory_space=pl.ANY),
        scratch_shapes=[
            pltpu.VMEM((ROWS, NB, SZ), F32),
            pltpu.VMEM((ROWS, NB, SZ), F32),
            pltpu.VMEM((NB, NB), F32),
            pltpu.SemaphoreType.DMA((SX,)),
            pltpu.SemaphoreType.DMA((ROWS,)),
        ],
        compiler_params=PARAMS,
        name="finish",
    )(field, grams)


def shift(value, axis, by):
    count = lax.axis_size(axis)
    return lax.ppermute(value, axis, [(i, (i + by) % count) for i in range(count)])


def local(orbitals, potential, projector, point_cell, target, point_count, coupling):
    bands, size_x, size_y, size_z = orbitals.shape
    me_x = lax.axis_index("gx").astype(jnp.int32).reshape(1)
    me_y = lax.axis_index("gy").astype(jnp.int32).reshape(1)
    me_z = lax.axis_index("gz").astype(jnp.int32).reshape(1)
    me_xz = jnp.concatenate([me_x, me_z])

    field, x_low, x_high, y_low, y_high, z_face = rearrange(orbitals.reshape(NB, ROWS, SZ))
    pot = potential.reshape(ROWS, SZ)
    first_z, second_z = z_matrices()

    alive = lax.iota(jnp.int32, SLOTS) < point_count.reshape(())
    code = target // 2
    z_other = (code % 3 != 1).astype(jnp.int32)
    wanted = ((code // 3) * 2 + z_other) * 2 + target % 2
    key = jnp.where(alive, point_cell * 64 + wanted, ROWS * SZ * 64)
    starts = jnp.sum(
        (key[None, :] < (lax.iota(jnp.int32, ROWS + 1) * (SZ * 64))[:, None]).astype(jnp.int32), axis=1
    )
    ordered = lax.sort((key,) + tuple(projector[j] for j in range(NPJ)), num_keys=1, is_stable=False)
    ordered = [o.reshape(SLOTS // LANES, LANES) for o in ordered]
    mat = build(starts, ordered[0], ordered[1:])

    own = jnp.repeat(coupling, NB, axis=1)
    coupling_frame = jnp.zeros((TGT, LANES), F32).at[16:18].set(own)

    previous = ()
    scales = ()
    for k in range(DEGREE):
        start, last = k == 0, k == DEGREE - 1
        x_left = shift(x_high, "gx", 1)
        x_right = shift(x_low, "gx", -1)
        if start:
            y_left = shift(y_high, "gy", 1)
            y_right = shift(y_low, "gy", -1)
            faces = shift(z_face, "gz", 1)
            mat, field, x_left, x_right, y_left, y_right, faces = lax.optimization_barrier(
                (mat, field, x_left, x_right, y_left, y_right, faces)
            )
            partial = first(field, mat)
            partial = jnp.concatenate([partial, coupling_frame], axis=0)
        frames = 2 if start else 1
        sends = spread_call(spread_y_kernel, 8, frames, me_y, partial)
        came = lax.all_to_all(sends, "gy", 0, 0)
        if not start:
            came, y_low, y_high, z_face = lax.optimization_barrier((came, y_low, y_high, z_face))
            y_left = shift(y_high, "gy", 1)
            y_right = shift(y_low, "gy", -1)
            faces = shift(z_face, "gz", 1)
        sends = spread_call(spread_xz_kernel, 16, frames, me_xz, came)
        came = lax.all_to_all(sends, ("gx", "gz"), 0, 0)
        base = local_part(
            start, field, *previous, x_left, x_right, y_left, y_right, faces, pot, first_z, second_z
        )
        outs = coupled_part(start, last, base, came, mat, *scales)
        previous = (field,)
        if last:
            field, gram = outs
        else:
            field, x_low, x_high, y_low, y_high, z_face, partial = outs[:7]
            if start:
                scales = (outs[7],)
    axes = ("gx", "gy", "gz")
    devices = 1
    for axis in axes:
        devices *= lax.axis_size(axis)
    grams = lax.all_to_all(jnp.broadcast_to(gram[None], (devices,) + gram.shape), axes, 0, 0)
    result = finish(1.0 / float(devices * ROWS * SZ), field, grams)
    return result.reshape(bands, size_x, size_y, size_z)


def solution(mesh):
    in_specs = (
        P(None, "gx", "gy", "gz"),
        P("gx", "gy", "gz"),
        P(None, ("gx", "gy", "gz")),
        P(("gx", "gy", "gz")),
        P(("gx", "gy", "gz")),
        P("gx", "gy", "gz"),
        P(("gx", "gy", "gz"), None),
    )
    out_specs = P(None, "gx", "gy", "gz")
    return jax.shard_map(local, mesh=mesh, in_specs=in_specs, out_specs=out_specs, check_vma=False)
```

```python
import functools

import jax
import jax.numpy as jnp
import numpy as np
from jax import lax
from jax.experimental import pallas as pl
from jax.experimental.pallas import tpu as pltpu
from jax.sharding import PartitionSpec as P

DEGREE = 4
STENCIL = (
    -5369.0 / 1800.0,
    12.0 / 7.0,
    -15.0 / 56.0,
    10.0 / 189.0,
    -1.0 / 112.0,
    2.0 / 1925.0,
    -1.0 / 16632.0,
)
FILTER_CENTRE = 9.5
FILTER_HALF = 5.5
REACH = 6

NB = 32
SX = 8
SY = 8
SZ = 128
ROWS = SX * SY
PAIRS = ROWS // 2
FACE = REACH * SY
NPJ = 4
SLOTS = 8192
TGT = 40
CH = NPJ * TGT
GROUPS = ROWS // 4
TOTAL = (2 * CH, 2 * NB)
BATCH = 4
ZROWS = GROUPS * 16
LANES = 128
F32 = jnp.float32
BF16 = jnp.bfloat16
NN = (((1,), (0,)), ((), ()))
NT = (((1,), (1,)), ((), ()))
VMEM_LIMIT = 16 * 1024 * 1024


def dot(a, b, dims=NN):
    return lax.dot_general(a, b, dims, preferred_element_type=F32)


def split2(v):
    hi = v.astype(BF16)
    return hi, (v - hi.astype(F32)).astype(BF16)


def split3(v):
    hi = v.astype(BF16)
    rest = v - hi.astype(F32)
    mid = rest.astype(BF16)
    return hi, mid, (rest - mid.astype(F32)).astype(BF16)


def z_matrices():
    half = [0.0] + [-0.5 * c for c in STENCIL[1:]]
    inner = np.zeros((SZ, SZ), np.float32)
    face = np.zeros((16, SZ), np.float32)
    for z in range(SZ):
        for source in range(SZ):
            if 1 <= abs(z - source) <= REACH:
                inner[source, z] = half[abs(z - source)]
        for e in range(8):
            if 1 <= abs(SZ + e - z) <= REACH:
                face[e, z] = half[abs(SZ + e - z)]
            if 1 <= abs(z + 8 - e) <= REACH:
                face[8 + e, z] = half[abs(z + 8 - e)]

    def split(m):
        hi = m.astype(jnp.bfloat16)
        return hi, (m - hi.astype(np.float32)).astype(jnp.bfloat16)

    inner_hi, inner_lo = split(inner)
    face_hi, face_lo = split(face)
    first = np.concatenate([inner_hi, inner_hi], axis=0)
    second = np.concatenate(
        [inner_lo, face_hi, face_hi, face_lo, np.zeros((SZ - 48, SZ), jnp.bfloat16)], axis=0
    )
    return jnp.asarray(first), jnp.asarray(second)


def any_specs(count):
    return [pl.BlockSpec(memory_space=pl.ANY)] * count


def vmem_specs(count):
    return [pl.BlockSpec(memory_space=pltpu.VMEM)] * count


PARAMS = pltpu.CompilerParams(vmem_limit_bytes=VMEM_LIMIT)


def cost(us):
    return pl.CostEstimate(flops=0, bytes_accessed=int(us * 3.5e6), transcendentals=0)


def z_faces(rows):
    turned = jnp.concatenate(rows, axis=0).T
    return jnp.concatenate([turned[:8], turned[SZ - 8 :]], axis=0)


def write_x_faces(field, x_low, x_high):
    x_low[...] = field[pl.ds(0, FACE)]
    x_high[...] = field[pl.ds(ROWS - FACE, FACE)]


def write_y_faces(field, y_low, y_high):
    for x in range(SX):
        y_low[x] = field[pl.ds(x * SY, REACH)]
        y_high[x] = field[pl.ds(x * SY + SY - REACH, REACH)]


BLOCK = jax.ShapeDtypeStruct((ROWS, NB, SZ), F32)
X_FACE = jax.ShapeDtypeStruct((FACE, NB, SZ), F32)
Y_FACE = jax.ShapeDtypeStruct((SX, REACH, NB, SZ), F32)
Z_FACE = jax.ShapeDtypeStruct((ZROWS, LANES), F32)
FRAME = jax.ShapeDtypeStruct((TGT, LANES), F32)


def rearrange_kernel(src, field, x_low, x_high, y_low, y_high, z_face, in_sem):
    loads = [
        pltpu.make_async_copy(src.at[:, row, :], field.at[row], in_sem.at[row]) for row in range(ROWS)
    ]
    for load in loads:
        load.start()
    for load in loads:
        load.wait()
    write_x_faces(field, x_low, x_high)
    write_y_faces(field, y_low, y_high)
    for g in range(GROUPS):
        z_face[pl.ds(16 * g, 16), :] = z_faces([field[4 * g + i] for i in range(4)])


def rearrange(orbitals):
    return pl.pallas_call(
        rearrange_kernel,
        out_shape=[BLOCK, X_FACE, X_FACE, Y_FACE, Y_FACE, Z_FACE],
        in_specs=any_specs(1),
        out_specs=vmem_specs(6),
        scratch_shapes=[pltpu.SemaphoreType.DMA((ROWS,))],
        compiler_params=PARAMS,
        cost_estimate=cost(3),
        name="rearrange",
    )(orbitals)


def build_kernel(starts, keys, w0, w1, w2, w3, out, held, weights, sem):
    full = pl.ds(0, SLOTS // LANES)
    loads = [pltpu.make_async_copy(keys, held.at[full], sem.at[NPJ])]
    for j, w in enumerate((w0, w1, w2, w3)):
        loads.append(pltpu.make_async_copy(w, weights.at[j, full], sem.at[j]))
    for load in loads:
        load.start()
    held[pl.ds(SLOTS // LANES, 8), :] = jnp.full((8, LANES), ROWS * SZ * 64, jnp.int32)
    for j in range(NPJ):
        weights[j, pl.ds(SLOTS // LANES, 8), :] = jnp.zeros((8, LANES), F32)
    for load in loads:
        load.wait()
    target_at = lax.broadcasted_iota(jnp.int32, (TGT, 2 * LANES), 0)
    z_at = lax.broadcasted_iota(jnp.int32, (SZ, 2 * LANES), 0)

    def window(row, block):
        key = jnp.concatenate([held[pl.ds(block, 1), :], held[pl.ds(block + 1, 1), :]], axis=1)
        target = jnp.where((key >> 13) == row, key & 63, 63)
        chosen = target_at == target
        parts = []
        for j in range(NPJ):
            w = jnp.concatenate(
                [weights[j, pl.ds(block, 1), :], weights[j, pl.ds(block + 1, 1), :]], axis=1
            )
            parts.append(jnp.where(chosen, w, 0.0))
        hi, lo = split2(jnp.concatenate(parts, axis=0))
        place = jnp.where(z_at == ((key >> 6) & 127), 1.0, 0.0).astype(BF16)
        both = dot(jnp.concatenate([hi, lo], axis=0), place, NT)
        return both[:CH] + both[CH:]

    @pl.loop(0, ROWS // BATCH)
    def _(step):
        first_row = step * BATCH
        bases = [starts[first_row + i] // LANES for i in range(BATCH)]
        for i in range(BATCH):
            hi, lo = split2(window(first_row + i, bases[i]))
            at = (step * (BATCH // 2) + i // 2, slice(None), pl.ds((i % 2) * SZ, SZ))
            out[at] = jnp.concatenate([hi, lo], axis=0)

        for i in range(BATCH):
            row = first_row + i
            windows = (starts[row + 1] - bases[i] * LANES + 2 * LANES - 1) // (2 * LANES)

            @pl.when(windows > 1)
            def _():
                total = lax.fori_loop(
                    0,
                    windows,
                    lambda k, acc: acc + window(row, bases[i] + 2 * k),
                    jnp.zeros((CH, SZ), F32),
                )
                hi, lo = split2(total)
                at = (step * (BATCH // 2) + i // 2, slice(None), pl.ds((i % 2) * SZ, SZ))
                out[at] = jnp.concatenate([hi, lo], axis=0)


def build(starts, keys, weights):
    return pl.pallas_call(
        build_kernel,
        out_shape=jax.ShapeDtypeStruct((PAIRS, 2 * CH, 2 * SZ), BF16),
        in_specs=[pl.BlockSpec(memory_space=pltpu.SMEM)] + any_specs(5),
        out_specs=pl.BlockSpec(memory_space=pltpu.VMEM),
        scratch_shapes=[
            pltpu.VMEM((SLOTS // LANES + 8, LANES), jnp.int32),
            pltpu.VMEM((NPJ, SLOTS // LANES + 8, LANES), F32),
            pltpu.SemaphoreType.DMA((NPJ + 1,)),
        ],
        compiler_params=PARAMS,
        cost_estimate=cost(10),
        name="build",
    )(starts, keys, *weights)


def partial_of(mat, values):
    hi, lo = split2(values)
    return dot(mat, jnp.concatenate([hi, lo], axis=0), NT)


def packed_partial(total):
    joined = total[:CH, :NB] + total[:CH, NB:] + total[CH:, :NB]
    return jnp.concatenate([joined[j * TGT : (j + 1) * TGT] for j in range(NPJ)], axis=1)


def partial_kernel(with_faces, *refs):
    if with_faces:
        field, mat, out, y_low, y_high, z_face, total = refs
    else:
        field, mat, out, total = refs
    total[...] = jnp.zeros_like(total)

    @pl.loop(0, SX)
    def _(x):
        acc = total[...]
        for p in range(4):
            at = x * SY + 2 * p
            values = jnp.concatenate([field[at], field[at + 1]], axis=1)
            acc = acc + partial_of(mat[x * 4 + p], values)
        total[...] = acc
        if with_faces:
            for part in range(2):
                z_face[pl.ds((2 * x + part) * 16, 16), :] = z_faces(
                    [field[x * SY + 4 * part + i] for i in range(4)]
                )

    out[...] = packed_partial(total[...])
    if with_faces:
        write_y_faces(field, y_low, y_high)


def partial_part(with_faces, field, mat):
    outs = [FRAME] + ([Y_FACE, Y_FACE, Z_FACE] if with_faces else [])
    return pl.pallas_call(
        functools.partial(partial_kernel, with_faces),
        out_shape=outs,
        in_specs=vmem_specs(2),
        out_specs=vmem_specs(len(outs)),
        scratch_shapes=[pltpu.VMEM(TOTAL, F32)],
        compiler_params=PARAMS,
        cost_estimate=cost(0.1),
        name="partial",
    )(field, mat)


def pieces(frame, stride):
    row = lax.broadcasted_iota(jnp.int32, (TGT, LANES), 0)
    digit = (row // stride) % 3
    for distance in range(-2, 3):
        moved = frame if distance == 0 else pltpu.roll(frame, (-stride * distance) % TGT, 0)
        valid = (digit + distance >= 0) & (digit + distance <= 2) & (row < 36)
        yield distance, jnp.where(valid, moved, 0.0)


def spread_y_kernel(frames, me, mine, out):
    for f in range(frames):
        at = pl.ds(f * TGT, TGT)
        for distance in (-3, 3, 4):
            out[(me[0] + distance + 8) % 8, at, :] = jnp.zeros((TGT, LANES), F32)
        for distance, piece in pieces(mine[at, :], 4):
            out[(me[0] + distance + 8) % 8, at, :] = piece


def spread_xz_kernel(frames, me, came, out):
    row = lax.broadcasted_iota(jnp.int32, (TGT, LANES), 0)
    for f in range(frames):
        at = pl.ds(f * TGT, TGT)
        frame = came[0, at, :]
        for slot in range(1, 8):
            frame = frame + came[slot, at, :]
        for distance in (-3, 3, 4):
            for z in range(2):
                out[((me[0] + distance + 8) % 8) * 2 + z, at, :] = jnp.zeros((TGT, LANES), F32)
        for distance, piece in pieces(frame, 12):
            swapped = jnp.where(
                row & 2 == 0, pltpu.roll(piece, TGT - 2, 0), pltpu.roll(piece, 2, 0)
            )
            slot = ((me[0] + distance + 8) % 8) * 2
            out[slot + me[1], at, :] = piece
            out[slot + 1 - me[1], at, :] = swapped


def spread_call(kernel, slots, frames, me, array):
    return pl.pallas_call(
        functools.partial(kernel, frames),
        out_shape=jax.ShapeDtypeStruct((slots, frames * TGT, LANES), F32),
        in_specs=[pl.BlockSpec(memory_space=pltpu.SMEM)] + vmem_specs(1),
        out_specs=pl.BlockSpec(memory_space=pltpu.VMEM),
        compiler_params=PARAMS,
        cost_estimate=cost(0.1),
        name="spread",
    )(me, array)


def local_kernel(first_step, *refs):
    if first_step:
        field, x_left, x_right, y_left, y_right, faces, potential, first_z, second_z, out = refs
        previous = None
    else:
        field, previous, x_left, x_right, y_left, y_right, faces, potential, first_z, second_z, out = refs
    alpha = (1.0 if first_step else 2.0) / FILTER_HALF
    half = [0.0] + [-0.5 * c for c in STENCIL[1:]]
    diagonal = -1.5 * STENCIL[0] - FILTER_CENTRE

    def at(x, y):
        if x < 0:
            return x_left[(x + REACH) * SY + y]
        if x >= SX:
            return x_right[(x - SX) * SY + y]
        if y < 0:
            return y_left[x, y + REACH]
        if y >= SY:
            return y_right[x, y - SY]
        return field[x * SY + y]

    for g in range(GROUPS):
        rows = [field[4 * g + i] for i in range(4)]
        hi, lo = split2(jnp.concatenate(rows, axis=0))
        face = faces[pl.ds(g * 16, 16), :]
        face_hi = face.astype(BF16).astype(F32)
        side = jnp.concatenate(
            [face_hi, face - face_hi, face_hi, jnp.zeros((LANES - 48, LANES), F32)], axis=0
        ).T.astype(BF16)
        along_z = dot(jnp.concatenate([hi, lo], axis=1), first_z[...]) + dot(
            jnp.concatenate([hi, side], axis=1), second_z[...]
        )
        for i in range(4):
            x, y = divmod(4 * g + i, SY)
            summed = along_z[i * NB : (i + 1) * NB]
            for m in range(1, REACH + 1):
                around = (at(x + m, y) + at(x - m, y)) + (at(x, y + m) + at(x, y - m))
                summed = summed + half[m] * around
            summed = summed + (potential[pl.ds(4 * g + i, 1), :] + diagonal) * rows[i]
            result = alpha * summed
            if not first_step:
                result = result - previous[4 * g + i]
            out[4 * g + i] = result


def local_part(first_step, *arrays):
    return pl.pallas_call(
        functools.partial(local_kernel, first_step),
        out_shape=BLOCK,
        in_specs=vmem_specs(len(arrays)),
        out_specs=pl.BlockSpec(memory_space=pltpu.VMEM),
        compiler_params=PARAMS,
        cost_estimate=cost(0.1),
        name="local",
    )(*arrays)


def coupled_kernel(first_step, last_step, *refs):
    if first_step:
        base, came, mat, new, x_low, x_high, coupling, coef = refs
    elif last_step:
        base, came, mat, coupling, new, gram, total, coef = refs
        total[...] = jnp.zeros_like(total)
    else:
        base, came, mat, coupling, new, x_low, x_high, coef = refs
    alpha = (1.0 if first_step else 2.0) / FILTER_HALF
    frame = came[0]
    for slot in range(1, came.shape[0]):
        frame = frame + came[slot]
    if first_step:
        coupling[...] = frame[TGT:]
        frame = frame[:TGT]
    frame = frame * (alpha * coupling[...])
    stacked = jnp.concatenate([frame[:, j * NB : (j + 1) * NB] for j in range(NPJ)], axis=0)
    turned = stacked.T
    coef_hi = turned.astype(BF16).astype(F32)
    coef[pl.ds(0, NB), :] = jnp.concatenate([coef_hi, coef_hi], axis=1).astype(BF16)
    coef[pl.ds(NB, NB), pl.ds(0, CH)] = (turned - coef_hi).astype(BF16)

    @pl.loop(0, SX)
    def _(x):
        c_hi = coef[pl.ds(0, NB), :]
        c_lo = coef[pl.ds(NB, NB), pl.ds(0, CH)]
        if last_step:
            acc = total[...]
        for p in range(4):
            pair_mat = mat[x * 4 + p]
            added = dot(c_hi, pair_mat) + dot(c_lo, pair_mat[:CH])
            rows = []
            for q in range(2):
                at = x * SY + 2 * p + q
                rows.append(base[at] + added[:, q * SZ : (q + 1) * SZ])
                new[at] = rows[q]
            if last_step:
                joined = jnp.concatenate(split3(jnp.concatenate(rows, axis=1)), axis=0)
                acc = acc + dot(joined, joined, NT)
        if last_step:
            total[...] = acc

    if last_step:
        t = total[...]
        summed = t[2 * NB :, :NB] + t[:NB, 2 * NB :] + t[NB : 2 * NB, NB : 2 * NB]
        summed = summed + (t[NB : 2 * NB, :NB] + t[:NB, NB : 2 * NB]) + t[:NB, :NB]
        gram[...] = jnp.concatenate([summed[8 * q : 8 * q + 8] for q in range(4)], axis=1)
    else:
        write_x_faces(new, x_low, x_high)


def coupled_part(first_step, last_step, *arrays):
    scratch = [pltpu.VMEM((2 * NB, 2 * CH), BF16)]
    if last_step:
        outs = [BLOCK, jax.ShapeDtypeStruct((8, LANES), F32)]
        scratch = [pltpu.VMEM((3 * NB, 3 * NB), F32)] + scratch
    else:
        outs = [BLOCK, X_FACE, X_FACE] + ([FRAME] if first_step else [])
    return pl.pallas_call(
        functools.partial(coupled_kernel, first_step, last_step),
        out_shape=outs,
        in_specs=vmem_specs(len(arrays)),
        out_specs=vmem_specs(len(outs)),
        scratch_shapes=scratch,
        compiler_params=PARAMS,
        cost_estimate=cost(0.1),
        name="coupled",
    )(*arrays)


def finish_kernel(scale, field, grams, out, held, made, inverse, in_sem, out_sem):
    loads = [
        pltpu.make_async_copy(field.at[pl.ds(x * SY, SY)], held.at[pl.ds(x * SY, SY)], in_sem.at[x])
        for x in range(SX)
    ]
    for load in loads:
        load.start()
    packed = grams[0]
    for slot in range(1, grams.shape[0]):
        packed = packed + grams[slot]
    packed = packed * scale
    gram = jnp.concatenate([packed[:, q * NB : (q + 1) * NB] for q in range(4)], axis=0)
    row = lax.broadcasted_iota(jnp.int32, (NB, NB), 0)
    column = lax.broadcasted_iota(jnp.int32, (NB, NB), 1)
    eye = jnp.where(row == column, 1.0, 0.0)
    work = jnp.concatenate([gram, eye], axis=1)
    below = lax.broadcasted_iota(jnp.int32, (NB, 2 * NB), 0)
    for k in range(NB):
        root = 1.0 / jnp.sqrt(work[k : k + 1, k : k + 1])
        line = work[k : k + 1, :] * root
        inverse[pl.ds(k, 1), :] = line[:, NB:]
        if k < NB - 1:
            factor = work[:, k : k + 1] * root
            work = work - jnp.where(below > k, factor * line, 0.0)
    hi, mid, lo = split3(inverse[...])
    left = jnp.concatenate([lo, mid, hi, mid, hi, hi], axis=1)

    @pl.loop(0, SX)
    def _(x):
        pltpu.make_async_copy(
            field.at[pl.ds(x * SY, SY)], held.at[pl.ds(x * SY, SY)], in_sem.at[x]
        ).wait()
        for p in range(SY // 2):
            at = x * SY + 2 * p
            values = jnp.concatenate([held[at], held[at + 1]], axis=1)
            f_hi, f_mid, f_lo = split3(values)
            right = jnp.concatenate([f_hi, f_mid, f_lo, f_hi, f_mid, f_hi], axis=0)
            result = dot(left, right)
            made[at] = result[:, :SZ]
            made[at + 1] = result[:, SZ:]
            for q in range(2):
                pltpu.make_async_copy(made.at[at + q], out.at[:, at + q, :], out_sem.at[at + q]).start()

    for r in range(ROWS):
        pltpu.make_async_copy(made.at[r], out.at[:, r, :], out_sem.at[r]).wait()


def finish(scale, field, grams):
    return pl.pallas_call(
        functools.partial(finish_kernel, scale),
        out_shape=jax.ShapeDtypeStruct((NB, ROWS, SZ), F32),
        in_specs=any_specs(1) + vmem_specs(1),
        out_specs=pl.BlockSpec(memory_space=pl.ANY),
        scratch_shapes=[
            pltpu.VMEM((ROWS, NB, SZ), F32),
            pltpu.VMEM((ROWS, NB, SZ), F32),
            pltpu.VMEM((NB, NB), F32),
            pltpu.SemaphoreType.DMA((SX,)),
            pltpu.SemaphoreType.DMA((ROWS,)),
        ],
        compiler_params=PARAMS,
        name="finish",
    )(field, grams)


def shift(value, axis, by):
    count = lax.axis_size(axis)
    return lax.ppermute(value, axis, [(i, (i + by) % count) for i in range(count)])


def local(orbitals, potential, projector, point_cell, target, point_count, coupling):
    bands, size_x, size_y, size_z = orbitals.shape
    me_x = lax.axis_index("gx").astype(jnp.int32).reshape(1)
    me_y = lax.axis_index("gy").astype(jnp.int32).reshape(1)
    me_z = lax.axis_index("gz").astype(jnp.int32).reshape(1)
    me_xz = jnp.concatenate([me_x, me_z])

    field, x_low, x_high, y_low, y_high, z_face = rearrange(orbitals.reshape(NB, ROWS, SZ))
    pot = potential.reshape(ROWS, SZ)
    first_z, second_z = z_matrices()

    alive = lax.iota(jnp.int32, SLOTS) < point_count.reshape(())
    code = target // 2
    z_other = (code % 3 != 1).astype(jnp.int32)
    wanted = ((code // 3) * 2 + z_other) * 2 + target % 2
    key = jnp.where(alive, point_cell * 64 + wanted, ROWS * SZ * 64)
    starts = jnp.sum(
        (key[None, :] < (lax.iota(jnp.int32, ROWS + 1) * (SZ * 64))[:, None]).astype(jnp.int32), axis=1
    )
    ordered = lax.sort((key,) + tuple(projector[j] for j in range(NPJ)), num_keys=1, is_stable=False)
    ordered = [o.reshape(SLOTS // LANES, LANES) for o in ordered]
    mat = build(starts, ordered[0], ordered[1:])

    own = jnp.repeat(coupling, NB, axis=1)
    coupling_frame = jnp.zeros((TGT, LANES), F32).at[16:18].set(own)

    previous = ()
    scales = ()
    for k in range(DEGREE):
        start, last = k == 0, k == DEGREE - 1
        x_left = shift(x_high, "gx", 1)
        x_right = shift(x_low, "gx", -1)
        if start:
            y_left = shift(y_high, "gy", 1)
            y_right = shift(y_low, "gy", -1)
            faces = shift(z_face, "gz", 1)
            mat, field, x_left, x_right, y_left, y_right, faces = lax.optimization_barrier(
                (mat, field, x_left, x_right, y_left, y_right, faces)
            )
            (partial,) = partial_part(False, field, mat)
            partial = jnp.concatenate([partial, coupling_frame], axis=0)
        else:
            partial, y_low, y_high, z_face = partial_part(True, field, mat)
        frames = 2 if start else 1
        sends = spread_call(spread_y_kernel, 8, frames, me_y, partial)
        if not start:
            sends, y_low, y_high, z_face = lax.optimization_barrier((sends, y_low, y_high, z_face))
            y_left = shift(y_high, "gy", 1)
            y_right = shift(y_low, "gy", -1)
            faces = shift(z_face, "gz", 1)
        came = lax.all_to_all(sends, "gy", 0, 0)
        sends = spread_call(spread_xz_kernel, 16, frames, me_xz, came)
        came = lax.all_to_all(sends, ("gx", "gz"), 0, 0)
        base = local_part(
            start, field, *previous, x_left, x_right, y_left, y_right, faces, pot, first_z, second_z
        )
        outs = coupled_part(start, last, base, came, mat, *scales)
        previous = (field,)
        if last:
            field, gram = outs
        else:
            field, x_low, x_high = outs[:3]
            if start:
                scales = (outs[3],)
    axes = ("gx", "gy", "gz")
    devices = 1
    for axis in axes:
        devices *= lax.axis_size(axis)
    grams = lax.all_to_all(jnp.broadcast_to(gram[None], (devices,) + gram.shape), axes, 0, 0)
    result = finish(1.0 / float(devices * ROWS * SZ), field, grams)
    return result.reshape(bands, size_x, size_y, size_z)


def solution(mesh):
    in_specs = (
        P(None, "gx", "gy", "gz"),
        P("gx", "gy", "gz"),
        P(None, ("gx", "gy", "gz")),
        P(("gx", "gy", "gz")),
        P(("gx", "gy", "gz")),
        P("gx", "gy", "gz"),
        P(("gx", "gy", "gz"), None),
    )
    out_specs = P(None, "gx", "gy", "gz")
    return jax.shard_map(local, mesh=mesh, in_specs=in_specs, out_specs=out_specs, check_vma=False)
```

```python
import functools

import jax
import jax.numpy as jnp
import numpy as np
from jax import lax
from jax.experimental import pallas as pl
from jax.experimental.pallas import tpu as pltpu
from jax.sharding import PartitionSpec as P

DEGREE = 4
STENCIL = (
    -5369.0 / 1800.0,
    12.0 / 7.0,
    -15.0 / 56.0,
    10.0 / 189.0,
    -1.0 / 112.0,
    2.0 / 1925.0,
    -1.0 / 16632.0,
)
FILTER_CENTRE = 9.5
FILTER_HALF = 5.5
REACH = 6

NB = 32
SX = 8
SY = 8
SZ = 128
ROWS = SX * SY
PAIRS = ROWS // 2
FACE = REACH * SY
NPJ = 4
SLOTS = 8192
TGT = 40
CH = NPJ * TGT
GROUPS = ROWS // 4
TOTAL = (2 * CH, 2 * NB)
BATCH = 4
ZROWS = GROUPS * 16
LANES = 128
F32 = jnp.float32
BF16 = jnp.bfloat16
NN = (((1,), (0,)), ((), ()))
NT = (((1,), (1,)), ((), ()))
VMEM_LIMIT = 60 * 1024 * 1024


def dot(a, b, dims=NN):
    return lax.dot_general(a, b, dims, preferred_element_type=F32)


def split2(v):
    hi = v.astype(BF16)
    return hi, (v - hi.astype(F32)).astype(BF16)


def split3(v):
    hi = v.astype(BF16)
    rest = v - hi.astype(F32)
    mid = rest.astype(BF16)
    return hi, mid, (rest - mid.astype(F32)).astype(BF16)


def z_matrices():
    half = [0.0] + [-0.5 * c for c in STENCIL[1:]]
    inner = np.zeros((SZ, SZ), np.float32)
    face = np.zeros((16, SZ), np.float32)
    for z in range(SZ):
        for source in range(SZ):
            if 1 <= abs(z - source) <= REACH:
                inner[source, z] = half[abs(z - source)]
        for e in range(8):
            if 1 <= abs(SZ + e - z) <= REACH:
                face[e, z] = half[abs(SZ + e - z)]
            if 1 <= abs(z + 8 - e) <= REACH:
                face[8 + e, z] = half[abs(z + 8 - e)]

    def split(m):
        hi = m.astype(jnp.bfloat16)
        return hi, (m - hi.astype(np.float32)).astype(jnp.bfloat16)

    inner_hi, inner_lo = split(inner)
    face_hi, face_lo = split(face)
    first = np.concatenate([inner_hi, inner_hi], axis=0)
    second = np.concatenate(
        [inner_lo, face_hi, face_hi, face_lo, np.zeros((SZ - 48, SZ), jnp.bfloat16)], axis=0
    )
    return jnp.asarray(first), jnp.asarray(second)


def any_specs(count):
    return [pl.BlockSpec(memory_space=pl.ANY)] * count


def vmem_specs(count):
    return [pl.BlockSpec(memory_space=pltpu.VMEM)] * count


PARAMS = pltpu.CompilerParams(vmem_limit_bytes=VMEM_LIMIT)
SMALL = pltpu.CompilerParams(vmem_limit_bytes=52 * 1024 * 1024)


def z_faces(rows):
    turned = jnp.concatenate(rows, axis=0).T
    return jnp.concatenate([turned[:8], turned[SZ - 8 :]], axis=0)


BLOCK = jax.ShapeDtypeStruct((ROWS, NB, SZ), F32)
X_FACE = jax.ShapeDtypeStruct((FACE, NB, SZ), F32)
Y_FACE = jax.ShapeDtypeStruct((SX, REACH, NB, SZ), F32)
Z_FACE = jax.ShapeDtypeStruct((ZROWS, LANES), F32)
FRAME = jax.ShapeDtypeStruct((TGT, LANES), F32)


def face_copies(x, field, x_low, x_high, y_low, y_high, sem):
    copies = [
        pltpu.make_async_copy(field.at[pl.ds(x * SY, REACH)], y_low.at[x], sem.at[0, x]),
        pltpu.make_async_copy(field.at[pl.ds(x * SY + SY - REACH, REACH)], y_high.at[x], sem.at[1, x]),
    ]
    return copies


def low_copy(x, field, x_low, sem):
    rows = pl.ds(x * SY, SY)
    return pltpu.make_async_copy(field.at[rows], x_low.at[rows], sem.at[2, x])


def high_copy(x, field, x_high, sem):
    to = pl.ds((x - (SX - REACH)) * SY, SY)
    return pltpu.make_async_copy(field.at[pl.ds(x * SY, SY)], x_high.at[to], sem.at[3, x])


def block_copy(x, field, out, sem):
    rows = pl.ds(x * SY, SY)
    return pltpu.make_async_copy(field.at[rows], out.at[rows], sem.at[4, x])


def start_faces(x, field, outs, sem):
    new, x_low, x_high, y_low, y_high = outs
    for copy in face_copies(x, field, x_low, x_high, y_low, y_high, sem):
        copy.start()
    block_copy(x, field, new, sem).start()

    @pl.when(x < REACH)
    def _():
        low_copy(x, field, x_low, sem).start()

    @pl.when(x >= SX - REACH)
    def _():
        high_copy(x, field, x_high, sem).start()


def wait_faces(field, outs, sem):
    new, x_low, x_high, y_low, y_high = outs
    for x in range(SX):
        for copy in face_copies(x, field, x_low, x_high, y_low, y_high, sem):
            copy.wait()
        block_copy(x, field, new, sem).wait()
        if x < REACH:
            low_copy(x, field, x_low, sem).wait()
        if x >= SX - REACH:
            high_copy(x, field, x_high, sem).wait()


def rearrange_kernel(src, *refs):
    outs, (z_face, field, in_sem, out_sem) = refs[:5], refs[5:]
    for row in range(ROWS):
        pltpu.make_async_copy(src.at[:, row, :], field.at[row], in_sem.at[row]).start()

    @pl.loop(0, SX)
    def _(x):
        for y in range(SY):
            row = x * SY + y
            pltpu.make_async_copy(src.at[:, row, :], field.at[row], in_sem.at[row]).wait()
        start_faces(x, field, outs, out_sem)
        for part in range(2):
            z_face[pl.ds((2 * x + part) * 16, 16), :] = z_faces(
                [field[x * SY + 4 * part + i] for i in range(4)]
            )

    wait_faces(field, outs, out_sem)


def rearrange(orbitals):
    return pl.pallas_call(
        rearrange_kernel,
        out_shape=[BLOCK, X_FACE, X_FACE, Y_FACE, Y_FACE, Z_FACE],
        in_specs=any_specs(1),
        out_specs=any_specs(5) + vmem_specs(1),
        scratch_shapes=[
            pltpu.VMEM((ROWS, NB, SZ), F32),
            pltpu.SemaphoreType.DMA((ROWS,)),
            pltpu.SemaphoreType.DMA((5, SX)),
        ],
        compiler_params=PARAMS,
        name="rearrange",
    )(orbitals)


def build_kernel(starts, keys, w0, w1, w2, w3, out_hbm, held, weights, out, sem, out_sem):
    full = pl.ds(0, SLOTS // LANES)
    loads = [pltpu.make_async_copy(keys, held.at[full], sem.at[NPJ])]
    for j, w in enumerate((w0, w1, w2, w3)):
        loads.append(pltpu.make_async_copy(w, weights.at[j, full], sem.at[j]))
    for load in loads:
        load.start()
    held[pl.ds(SLOTS // LANES, 8), :] = jnp.full((8, LANES), ROWS * SZ * 64, jnp.int32)
    for j in range(NPJ):
        weights[j, pl.ds(SLOTS // LANES, 8), :] = jnp.zeros((8, LANES), F32)
    for load in loads:
        load.wait()
    target_at = lax.broadcasted_iota(jnp.int32, (TGT, 2 * LANES), 0)
    z_at = lax.broadcasted_iota(jnp.int32, (SZ, 2 * LANES), 0)

    def window(row, block):
        key = jnp.concatenate([held[pl.ds(block, 1), :], held[pl.ds(block + 1, 1), :]], axis=1)
        target = jnp.where((key >> 13) == row, key & 63, 63)
        chosen = target_at == target
        parts = []
        for j in range(NPJ):
            w = jnp.concatenate(
                [weights[j, pl.ds(block, 1), :], weights[j, pl.ds(block + 1, 1), :]], axis=1
            )
            parts.append(jnp.where(chosen, w, 0.0))
        hi, lo = split2(jnp.concatenate(parts, axis=0))
        place = jnp.where(z_at == ((key >> 6) & 127), 1.0, 0.0).astype(BF16)
        both = dot(jnp.concatenate([hi, lo], axis=0), place, NT)
        return both[:CH] + both[CH:]

    def store_of(step):
        done = pl.ds(step * (BATCH // 2), BATCH // 2)
        return pltpu.make_async_copy(out.at[done], out_hbm.at[done], out_sem.at[step])

    @pl.loop(0, ROWS // BATCH)
    def _(step):
        first_row = step * BATCH
        bases = [starts[first_row + i] // LANES for i in range(BATCH)]
        for i in range(BATCH):
            hi, lo = split2(window(first_row + i, bases[i]))
            at = (step * (BATCH // 2) + i // 2, slice(None), pl.ds((i % 2) * SZ, SZ))
            out[at] = jnp.concatenate([hi, lo], axis=0)

        for i in range(BATCH):
            row = first_row + i
            windows = (starts[row + 1] - bases[i] * LANES + 2 * LANES - 1) // (2 * LANES)

            @pl.when(windows > 1)
            def _():
                total = lax.fori_loop(
                    0,
                    windows,
                    lambda k, acc: acc + window(row, bases[i] + 2 * k),
                    jnp.zeros((CH, SZ), F32),
                )
                hi, lo = split2(total)
                at = (step * (BATCH // 2) + i // 2, slice(None), pl.ds((i % 2) * SZ, SZ))
                out[at] = jnp.concatenate([hi, lo], axis=0)

        store_of(step).start()

    for step in range(ROWS // BATCH):
        store_of(step).wait()


def build(starts, keys, weights):
    return pl.pallas_call(
        build_kernel,
        out_shape=jax.ShapeDtypeStruct((PAIRS, 2 * CH, 2 * SZ), BF16),
        in_specs=[pl.BlockSpec(memory_space=pltpu.SMEM)] + any_specs(5),
        out_specs=pl.BlockSpec(memory_space=pl.ANY),
        scratch_shapes=[
            pltpu.VMEM((SLOTS // LANES + 8, LANES), jnp.int32),
            pltpu.VMEM((NPJ, SLOTS // LANES + 8, LANES), F32),
            pltpu.VMEM((PAIRS, 2 * CH, 2 * SZ), BF16),
            pltpu.SemaphoreType.DMA((NPJ + 1,)),
            pltpu.SemaphoreType.DMA((ROWS // BATCH,)),
        ],
        compiler_params=PARAMS,
        name="build",
    )(starts, keys, *weights)


def partial_of(mat, values):
    hi, lo = split2(values)
    return dot(mat, jnp.concatenate([hi, lo], axis=0), NT)


def packed_partial(total):
    joined = total[:CH, :NB] + total[:CH, NB:] + total[CH:, :NB]
    return jnp.concatenate([joined[j * TGT : (j + 1) * TGT] for j in range(NPJ)], axis=1)


def pieces(frame, stride):
    row = lax.broadcasted_iota(jnp.int32, (TGT, LANES), 0)
    digit = (row // stride) % 3
    for distance in range(-2, 3):
        moved = frame if distance == 0 else pltpu.roll(frame, (-stride * distance) % TGT, 0)
        valid = (digit + distance >= 0) & (digit + distance <= 2) & (row < 36)
        yield distance, jnp.where(valid, moved, 0.0)


def spread_y(frame, me, out, at):
    for distance in (-3, 3, 4):
        out[(me[0] + distance + 8) % 8, at, :] = jnp.zeros((TGT, LANES), F32)
    for distance, piece in pieces(frame, 4):
        out[(me[0] + distance + 8) % 8, at, :] = piece


def first_kernel(me, field, mat, own, out, field_v, mat_v, total, in_sem, mat_sem):
    def load(x):
        rows = pl.ds(x * SY, SY)
        some = pl.ds(x * 4, 4)
        return [
            pltpu.make_async_copy(field.at[rows], field_v.at[rows], in_sem.at[x]),
            pltpu.make_async_copy(mat.at[some], mat_v.at[some], mat_sem.at[x]),
        ]

    for x in range(SX):
        for copy in load(x):
            copy.start()
    row = lax.broadcasted_iota(jnp.int32, (TGT, LANES), 0)
    couplings = jnp.where(row == 16, own[pl.ds(0, 1), :], jnp.where(row == 17, own[pl.ds(1, 1), :], 0.0))
    spread_y(couplings, me, out, pl.ds(TGT, TGT))
    total[...] = jnp.zeros_like(total)

    @pl.loop(0, SX)
    def _(x):
        for copy in load(x):
            copy.wait()
        acc = total[...]
        for p in range(4):
            at = x * SY + 2 * p
            values = jnp.concatenate([field_v[at], field_v[at + 1]], axis=1)
            acc = acc + partial_of(mat_v[x * 4 + p], values)
        total[...] = acc

    spread_y(packed_partial(total[...]), me, out, pl.ds(0, TGT))


def first(me, field, mat, own):
    return pl.pallas_call(
        first_kernel,
        out_shape=jax.ShapeDtypeStruct((8, 2 * TGT, LANES), F32),
        in_specs=[pl.BlockSpec(memory_space=pltpu.SMEM)] + any_specs(2) + vmem_specs(1),
        out_specs=pl.BlockSpec(memory_space=pltpu.VMEM),
        scratch_shapes=[
            pltpu.VMEM((ROWS, NB, SZ), F32),
            pltpu.VMEM((PAIRS, 2 * CH, 2 * SZ), BF16),
            pltpu.VMEM(TOTAL, F32),
            pltpu.SemaphoreType.DMA((SX,)),
            pltpu.SemaphoreType.DMA((SX,)),
        ],
        compiler_params=PARAMS,
        name="first",
    )(me, field, mat, own)


def spread_xz_kernel(frames, me, came, out):
    row = lax.broadcasted_iota(jnp.int32, (TGT, LANES), 0)
    for f in range(frames):
        at = pl.ds(f * TGT, TGT)
        frame = came[0, at, :]
        for slot in range(1, 8):
            frame = frame + came[slot, at, :]
        for distance in (-3, 3, 4):
            for z in range(2):
                out[((me[0] + distance + 8) % 8) * 2 + z, at, :] = jnp.zeros((TGT, LANES), F32)
        for distance, piece in pieces(frame, 12):
            swapped = jnp.where(
                row & 2 == 0, pltpu.roll(piece, TGT - 2, 0), pltpu.roll(piece, 2, 0)
            )
            slot = ((me[0] + distance + 8) % 8) * 2
            out[slot + me[1], at, :] = piece
            out[slot + 1 - me[1], at, :] = swapped


def spread_xz(frames, me, array):
    return pl.pallas_call(
        functools.partial(spread_xz_kernel, frames),
        out_shape=jax.ShapeDtypeStruct((16, frames * TGT, LANES), F32),
        in_specs=[pl.BlockSpec(memory_space=pltpu.SMEM)] + vmem_specs(1),
        out_specs=pl.BlockSpec(memory_space=pltpu.VMEM),
        compiler_params=SMALL,
        name="spread",
    )(me, array)


def local_kernel(first_step, *refs):
    count = 9 if first_step else 10
    inputs, out, held, made, in_sem, out_sem = refs[:count], refs[count], refs[count + 1 : -3], *refs[-3:]
    loads = [pltpu.make_async_copy(inputs[i], held[i], in_sem.at[i]) for i in range(count)]
    for load in loads:
        load.start()
    field, faces, potential, first_z, second_z, x_left, x_right, y_left, y_right = held[:9]
    alpha = (1.0 if first_step else 2.0) / FILTER_HALF
    half = [0.0] + [-0.5 * c for c in STENCIL[1:]]
    diagonal = -1.5 * STENCIL[0] - FILTER_CENTRE
    for load in loads[:5]:
        load.wait()

    @pl.loop(0, GROUPS)
    def _(g):
        rows = [field[4 * g + i] for i in range(4)]
        hi, lo = split2(jnp.concatenate(rows, axis=0))
        face = faces[pl.ds(g * 16, 16), :]
        face_hi = face.astype(BF16).astype(F32)
        side = jnp.concatenate(
            [face_hi, face - face_hi, face_hi, jnp.zeros((LANES - 48, LANES), F32)], axis=0
        ).T.astype(BF16)
        along_z = dot(jnp.concatenate([hi, lo], axis=1), first_z[...]) + dot(
            jnp.concatenate([hi, side], axis=1), second_z[...]
        )
        for i in range(4):
            own = (potential[pl.ds(4 * g + i, 1), :] + diagonal) * rows[i]
            made[4 * g + i] = along_z[i * NB : (i + 1) * NB] + own

    for load in loads[5:]:
        load.wait()

    def at(x, y):
        if x < 0:
            return x_left[(x + REACH) * SY + y]
        if x >= SX:
            return x_right[(x - SX) * SY + y]
        if y < 0:
            return y_left[x, y + REACH]
        if y >= SY:
            return y_right[x, y - SY]
        return field[x * SY + y]

    stores = []
    for x in range(SX):
        for y in range(SY):
            row = x * SY + y
            summed = made[row]
            for m in range(1, REACH + 1):
                around = (at(x + m, y) + at(x - m, y)) + (at(x, y + m) + at(x, y - m))
                summed = summed + half[m] * around
            result = alpha * summed
            if not first_step:
                result = result - held[9][row]
            made[row] = result
        rows = pl.ds(x * SY, SY)
        stores.append(pltpu.make_async_copy(made.at[rows], out.at[rows], out_sem.at[x]))
        stores[-1].start()
    for store in stores:
        store.wait()


def local_part(first_step, *arrays):
    return pl.pallas_call(
        functools.partial(local_kernel, first_step),
        out_shape=BLOCK,
        in_specs=any_specs(len(arrays)),
        out_specs=pl.BlockSpec(memory_space=pl.ANY),
        scratch_shapes=[pltpu.VMEM(a.shape, a.dtype) for a in arrays]
        + [
            pltpu.VMEM((ROWS, NB, SZ), F32),
            pltpu.SemaphoreType.DMA((len(arrays),)),
            pltpu.SemaphoreType.DMA((SX,)),
        ],
        compiler_params=SMALL,
        name="local",
    )(*arrays)


def coupled_kernel(first_step, last_step, me, base, came, mat, *refs):
    coupling = None
    if not first_step:
        coupling, refs = refs[0], refs[1:]
    if last_step:
        (new, gram), refs = refs[:2], refs[2:]
    else:
        (new, x_low, x_high, y_low, y_high, z_face, sends), refs = refs[:7], refs[7:]
        if first_step:
            coupling, refs = refs[0], refs[1:]
        outs = (new, x_low, x_high, y_low, y_high)
    made, came_v, mat_v, total, coef, came_sem, in_sem, mat_sem, out_sem = refs
    alpha = (1.0 if first_step else 2.0) / FILTER_HALF
    arrive = pltpu.make_async_copy(came, came_v, came_sem)
    arrive.start()

    def load(x):
        rows = pl.ds(x * SY, SY)
        some = pl.ds(x * 4, 4)
        return [
            pltpu.make_async_copy(base.at[rows], made.at[rows], in_sem.at[x]),
            pltpu.make_async_copy(mat.at[some], mat_v.at[some], mat_sem.at[x]),
        ]

    for x in range(SX):
        for copy in load(x):
            copy.start()
    total[...] = jnp.zeros_like(total)
    arrive.wait()
    frame = came_v[0]
    for slot in range(1, came.shape[0]):
        frame = frame + came_v[slot]
    if first_step:
        coupling[...] = frame[TGT:]
        frame = frame[:TGT]
    frame = frame * (alpha * coupling[...])
    stacked = jnp.concatenate([frame[:, j * NB : (j + 1) * NB] for j in range(NPJ)], axis=0)
    turned = stacked.T
    coef_hi = turned.astype(BF16).astype(F32)
    coef[pl.ds(0, NB), :] = jnp.concatenate([coef_hi, coef_hi], axis=1).astype(BF16)
    coef[pl.ds(NB, NB), pl.ds(0, CH)] = (turned - coef_hi).astype(BF16)

    @pl.loop(0, SX)
    def _(x):
        for copy in load(x):
            copy.wait()
        c_hi = coef[pl.ds(0, NB), :]
        c_lo = coef[pl.ds(NB, NB), pl.ds(0, CH)]
        acc = total[...]
        rows = []
        for p in range(4):
            pair_mat = mat_v[x * 4 + p]
            added = dot(c_hi, pair_mat) + dot(c_lo, pair_mat[:CH])
            for q in range(2):
                at = x * SY + 2 * p + q
                rows.append(made[at] + added[:, q * SZ : (q + 1) * SZ])
                made[at] = rows[-1]
        if last_step:
            block_copy(x, made, new, out_sem).start()
        else:
            start_faces(x, made, outs, out_sem)
        for p in range(4):
            values = jnp.concatenate(rows[2 * p : 2 * p + 2], axis=1)
            if last_step:
                joined = jnp.concatenate(split3(values), axis=0)
                acc = acc + dot(joined, joined, NT)
            else:
                acc = acc + partial_of(mat_v[x * 4 + p], values)
        total[...] = acc
        if not last_step:
            for part in range(2):
                z_face[pl.ds((2 * x + part) * 16, 16), :] = z_faces(rows[4 * part : 4 * part + 4])

    if last_step:
        t = total[...]
        summed = t[2 * NB :, :NB] + t[:NB, 2 * NB :] + t[NB : 2 * NB, NB : 2 * NB]
        summed = summed + (t[NB : 2 * NB, :NB] + t[:NB, NB : 2 * NB]) + t[:NB, :NB]
        gram[...] = jnp.concatenate([summed[8 * q : 8 * q + 8] for q in range(4)], axis=1)
        for x in range(SX):
            block_copy(x, made, new, out_sem).wait()
    else:
        spread_y(packed_partial(total[...]), me, sends, pl.ds(0, TGT))
        wait_faces(made, outs, out_sem)


def coupled_part(first_step, last_step, me, base, came, mat, *scales):
    total = (3 * NB, 3 * NB) if last_step else TOTAL
    if last_step:
        outs = [BLOCK, jax.ShapeDtypeStruct((8, LANES), F32)]
        specs = any_specs(1) + vmem_specs(1)
    else:
        outs = [BLOCK, X_FACE, X_FACE, Y_FACE, Y_FACE, Z_FACE, jax.ShapeDtypeStruct((8, TGT, LANES), F32)]
        specs = any_specs(5) + vmem_specs(2)
        if first_step:
            outs.append(FRAME)
            specs = specs + vmem_specs(1)
    return pl.pallas_call(
        functools.partial(coupled_kernel, first_step, last_step),
        out_shape=outs,
        in_specs=[pl.BlockSpec(memory_space=pltpu.SMEM)] + any_specs(3) + vmem_specs(len(scales)),
        out_specs=specs,
        scratch_shapes=[
            pltpu.VMEM((ROWS, NB, SZ), F32),
            pltpu.VMEM(came.shape, F32),
            pltpu.VMEM((PAIRS, 2 * CH, 2 * SZ), BF16),
            pltpu.VMEM(total, F32),
            pltpu.VMEM((2 * NB, 2 * CH), BF16),
            pltpu.SemaphoreType.DMA(()),
            pltpu.SemaphoreType.DMA((SX,)),
            pltpu.SemaphoreType.DMA((SX,)),
            pltpu.SemaphoreType.DMA((5, SX)),
        ],
        compiler_params=PARAMS,
        name="coupled",
    )(me, base, came, mat, *scales)


def finish_kernel(scale, field, grams, out, held, made, inverse, in_sem, out_sem):
    loads = [
        pltpu.make_async_copy(field.at[pl.ds(x * SY, SY)], held.at[pl.ds(x * SY, SY)], in_sem.at[x])
        for x in range(SX)
    ]
    for load in loads:
        load.start()
    packed = grams[0]
    for slot in range(1, grams.shape[0]):
        packed = packed + grams[slot]
    packed = packed * scale
    gram = jnp.concatenate([packed[:, q * NB : (q + 1) * NB] for q in range(4)], axis=0)
    row = lax.broadcasted_iota(jnp.int32, (NB, NB), 0)
    column = lax.broadcasted_iota(jnp.int32, (NB, NB), 1)
    eye = jnp.where(row == column, 1.0, 0.0)
    work = jnp.concatenate([gram, eye], axis=1)
    below = lax.broadcasted_iota(jnp.int32, (NB, 2 * NB), 0)
    for k in range(NB):
        root = 1.0 / jnp.sqrt(work[k : k + 1, k : k + 1])
        line = work[k : k + 1, :] * root
        inverse[pl.ds(k, 1), :] = line[:, NB:]
        if k < NB - 1:
            factor = work[:, k : k + 1] * root
            work = work - jnp.where(below > k, factor * line, 0.0)
    hi, mid, lo = split3(inverse[...])
    left = jnp.concatenate([lo, mid, hi, mid, hi, hi], axis=1)

    @pl.loop(0, SX)
    def _(x):
        pltpu.make_async_copy(
            field.at[pl.ds(x * SY, SY)], held.at[pl.ds(x * SY, SY)], in_sem.at[x]
        ).wait()
        for p in range(SY // 2):
            at = x * SY + 2 * p
            values = jnp.concatenate([held[at], held[at + 1]], axis=1)
            f_hi, f_mid, f_lo = split3(values)
            right = jnp.concatenate([f_hi, f_mid, f_lo, f_hi, f_mid, f_hi], axis=0)
            result = dot(left, right)
            made[at] = result[:, :SZ]
            made[at + 1] = result[:, SZ:]
            for q in range(2):
                pltpu.make_async_copy(made.at[at + q], out.at[:, at + q, :], out_sem.at[at + q]).start()

    for r in range(ROWS):
        pltpu.make_async_copy(made.at[r], out.at[:, r, :], out_sem.at[r]).wait()


def finish(scale, field, grams):
    return pl.pallas_call(
        functools.partial(finish_kernel, scale),
        out_shape=jax.ShapeDtypeStruct((NB, ROWS, SZ), F32),
        in_specs=any_specs(1) + vmem_specs(1),
        out_specs=pl.BlockSpec(memory_space=pl.ANY),
        scratch_shapes=[
            pltpu.VMEM((ROWS, NB, SZ), F32),
            pltpu.VMEM((ROWS, NB, SZ), F32),
            pltpu.VMEM((NB, NB), F32),
            pltpu.SemaphoreType.DMA((SX,)),
            pltpu.SemaphoreType.DMA((ROWS,)),
        ],
        compiler_params=PARAMS,
        name="finish",
    )(field, grams)


def shift(value, axis, by):
    count = lax.axis_size(axis)
    return lax.ppermute(value, axis, [(i, (i + by) % count) for i in range(count)])


def local(orbitals, potential, projector, point_cell, target, point_count, coupling):
    bands, size_x, size_y, size_z = orbitals.shape
    me_x = lax.axis_index("gx").astype(jnp.int32).reshape(1)
    me_y = lax.axis_index("gy").astype(jnp.int32).reshape(1)
    me_z = lax.axis_index("gz").astype(jnp.int32).reshape(1)
    me_xz = jnp.concatenate([me_x, me_z])

    field, x_low, x_high, y_low, y_high, z_face = rearrange(orbitals.reshape(NB, ROWS, SZ))
    pot = potential.reshape(ROWS, SZ)
    first_z, second_z = z_matrices()

    alive = lax.iota(jnp.int32, SLOTS) < point_count.reshape(())
    code = target // 2
    z_other = (code % 3 != 1).astype(jnp.int32)
    wanted = ((code // 3) * 2 + z_other) * 2 + target % 2
    key = jnp.where(alive, point_cell * 64 + wanted, ROWS * SZ * 64)
    starts = jnp.sum(
        (key[None, :] < (lax.iota(jnp.int32, ROWS + 1) * (SZ * 64))[:, None]).astype(jnp.int32), axis=1
    )
    ordered = lax.sort((key,) + tuple(projector[j] for j in range(NPJ)), num_keys=1, is_stable=False)
    ordered = [o.reshape(SLOTS // LANES, LANES) for o in ordered]
    mat = build(starts, ordered[0], ordered[1:])

    own = jnp.repeat(coupling, NB, axis=1)
    previous = ()
    scales = ()
    sends = None
    for k in range(DEGREE):
        start, last = k == 0, k == DEGREE - 1
        x_left = shift(x_high, "gx", 1)
        x_right = shift(x_low, "gx", -1)
        if start:
            y_left = shift(y_high, "gy", 1)
            y_right = shift(y_low, "gy", -1)
            faces = shift(z_face, "gz", 1)
            mat, field, x_left, x_right, y_left, y_right, faces = lax.optimization_barrier(
                (mat, field, x_left, x_right, y_left, y_right, faces)
            )
            sends = first(me_y, field, mat, own)
        if not start:
            faces = shift(z_face, "gz", 1)
            sends, faces, y_low, y_high = lax.optimization_barrier((sends, faces, y_low, y_high))
        came = lax.all_to_all(sends, "gy", 0, 0)
        if not start:
            y_left = shift(y_high, "gy", 1)
            y_right = shift(y_low, "gy", -1)
        sends = spread_xz(2 if start else 1, me_xz, came)
        came = lax.all_to_all(sends, ("gx", "gz"), 0, 0)
        base = local_part(
            start, field, faces, pot, first_z, second_z, x_left, x_right, y_left, y_right, *previous
        )
        outs = coupled_part(start, last, me_y, base, came, mat, *scales)
        previous = (field,)
        if last:
            field, gram = outs
        else:
            field, x_low, x_high, y_low, y_high, z_face, sends = outs[:7]
            if start:
                scales = (outs[7],)
    axes = ("gx", "gy", "gz")
    devices = 1
    for axis in axes:
        devices *= lax.axis_size(axis)
    grams = lax.all_to_all(jnp.broadcast_to(gram[None], (devices,) + gram.shape), axes, 0, 0)
    result = finish(1.0 / float(devices * ROWS * SZ), field, grams)
    return result.reshape(bands, size_x, size_y, size_z)


def solution(mesh):
    in_specs = (
        P(None, "gx", "gy", "gz"),
        P("gx", "gy", "gz"),
        P(None, ("gx", "gy", "gz")),
        P(("gx", "gy", "gz")),
        P(("gx", "gy", "gz")),
        P("gx", "gy", "gz"),
        P(("gx", "gy", "gz"), None),
    )
    out_specs = P(None, "gx", "gy", "gz")
    return jax.shard_map(local, mesh=mesh, in_specs=in_specs, out_specs=out_specs, check_vma=False)
```

```python
import functools

import jax
import jax.numpy as jnp
from jax import lax
from jax.experimental import pallas as pl
from jax.experimental.pallas import tpu as pltpu
from jax.sharding import PartitionSpec as P

DEGREE = 4
STENCIL = (
    -5369.0 / 1800.0,
    12.0 / 7.0,
    -15.0 / 56.0,
    10.0 / 189.0,
    -1.0 / 112.0,
    2.0 / 1925.0,
    -1.0 / 16632.0,
)
FILTER_CENTRE = 9.5
FILTER_HALF = 5.5
REACH = 6

NB = 32
SX = 8
SY = 8
SZ = 128
ROWS = SX * SY
PAIRS = ROWS // 2
FACE = REACH * SY
NPJ = 4
SLOTS = 8192
TGT = 40
CH = NPJ * TGT
GROUPS = ROWS // 4
TOTAL = (2 * CH, 2 * NB)
BATCH = 4
ZROWS = GROUPS * 16
LANES = 128
F32 = jnp.float32
BF16 = jnp.bfloat16
NN = (((1,), (0,)), ((), ()))
NT = (((1,), (1,)), ((), ()))
VMEM_LIMIT = 16 * 1024 * 1024


def dot(a, b, dims=NN):
    return lax.dot_general(a, b, dims, preferred_element_type=F32)


def split2(v):
    hi = v.astype(BF16)
    return hi, (v - hi.astype(F32)).astype(BF16)


def split3(v):
    hi = v.astype(BF16)
    rest = v - hi.astype(F32)
    mid = rest.astype(BF16)
    return hi, mid, (rest - mid.astype(F32)).astype(BF16)


def band(distance):
    found = jnp.zeros(distance.shape, F32)
    for m in range(1, REACH + 1):
        found = jnp.where(jnp.abs(distance) == m, -0.5 * STENCIL[m], found)
    return found


def write_z_matrices(first, second):
    source = lax.broadcasted_iota(jnp.int32, (SZ, SZ), 0)
    z = lax.broadcasted_iota(jnp.int32, (SZ, SZ), 1)
    inner_hi, inner_lo = split2(band(source - z))
    e = lax.broadcasted_iota(jnp.int32, (16, SZ), 0)
    z = lax.broadcasted_iota(jnp.int32, (16, SZ), 1)
    face_hi, face_lo = split2(band(jnp.where(e < 8, SZ + e - z, z + 16 - e)))
    first[...] = jnp.concatenate([inner_hi, inner_hi], axis=0)
    unused = jnp.zeros((SZ - 48, SZ), BF16)
    second[...] = jnp.concatenate([inner_lo, face_hi, face_hi, face_lo, unused], axis=0)


def any_specs(count):
    return [pl.BlockSpec(memory_space=pl.ANY)] * count


def vmem_specs(count):
    return [pl.BlockSpec(memory_space=pltpu.VMEM)] * count


PARAMS = pltpu.CompilerParams(vmem_limit_bytes=VMEM_LIMIT)


def z_faces(rows):
    turned = jnp.concatenate(rows, axis=0).T
    return jnp.concatenate([turned[:8], turned[SZ - 8 :]], axis=0)


BLOCK = jax.ShapeDtypeStruct((ROWS, NB, SZ), F32)
X_FACE = jax.ShapeDtypeStruct((FACE, NB, SZ), F32)
Y_FACE = jax.ShapeDtypeStruct((SX, REACH, NB, SZ), F32)
MESSAGE = jax.ShapeDtypeStruct((ZROWS + TGT, LANES), F32)
FRAME = jax.ShapeDtypeStruct((TGT, LANES), F32)
MATRIX = jax.ShapeDtypeStruct((PAIRS, 2 * CH, 2 * SZ), BF16)


def face_copies(x, field, x_low, x_high, y_low, y_high, sem):
    copies = [
        pltpu.make_async_copy(field.at[pl.ds(x * SY, REACH)], y_low.at[x], sem.at[0, x]),
        pltpu.make_async_copy(field.at[pl.ds(x * SY + SY - REACH, REACH)], y_high.at[x], sem.at[1, x]),
    ]
    return copies


def low_copy(x, field, x_low, sem):
    rows = pl.ds(x * SY, SY)
    return pltpu.make_async_copy(field.at[rows], x_low.at[rows], sem.at[2, x])


def high_copy(x, field, x_high, sem):
    to = pl.ds((x - (SX - REACH)) * SY, SY)
    return pltpu.make_async_copy(field.at[pl.ds(x * SY, SY)], x_high.at[to], sem.at[3, x])


def start_faces(x, field, outs, sem):
    x_low, x_high, y_low, y_high = outs
    for copy in face_copies(x, field, x_low, x_high, y_low, y_high, sem):
        copy.start()

    @pl.when(x < REACH)
    def _():
        low_copy(x, field, x_low, sem).start()

    @pl.when(x >= SX - REACH)
    def _():
        high_copy(x, field, x_high, sem).start()


def wait_faces(field, outs, sem):
    x_low, x_high, y_low, y_high = outs
    for x in range(SX):
        for copy in face_copies(x, field, x_low, x_high, y_low, y_high, sem):
            copy.wait()
        if x < REACH:
            low_copy(x, field, x_low, sem).wait()
        if x >= SX - REACH:
            high_copy(x, field, x_high, sem).wait()


def rearrange_kernel(src, *refs):
    field, outs, (z_face, in_sem, out_sem) = refs[0], refs[1:5], refs[5:]
    for row in range(ROWS):
        pltpu.make_async_copy(src.at[:, row, :], field.at[row], in_sem.at[row]).start()

    @pl.loop(0, SX)
    def _(x):
        for y in range(SY):
            row = x * SY + y
            pltpu.make_async_copy(src.at[:, row, :], field.at[row], in_sem.at[row]).wait()
        start_faces(x, field, outs, out_sem)
        for part in range(2):
            z_face[pl.ds((2 * x + part) * 16, 16), :] = z_faces(
                [field[x * SY + 4 * part + i] for i in range(4)]
            )

    wait_faces(field, outs, out_sem)


def rearrange(orbitals):
    return pl.pallas_call(
        rearrange_kernel,
        out_shape=[BLOCK, X_FACE, X_FACE, Y_FACE, Y_FACE, jax.ShapeDtypeStruct((ZROWS, LANES), F32)],
        in_specs=any_specs(1),
        out_specs=vmem_specs(6),
        scratch_shapes=[
            pltpu.SemaphoreType.DMA((ROWS,)),
            pltpu.SemaphoreType.DMA((4, SX)),
        ],
        compiler_params=PARAMS,
        name="rearrange",
    )(orbitals)


def build_kernel(starts, keys, w0, w1, w2, w3, out, held, weights, sem):
    full = pl.ds(0, SLOTS // LANES)
    loads = [pltpu.make_async_copy(keys, held.at[full], sem.at[NPJ])]
    for j, w in enumerate((w0, w1, w2, w3)):
        loads.append(pltpu.make_async_copy(w, weights.at[j, full], sem.at[j]))
    for load in loads:
        load.start()
    held[pl.ds(SLOTS // LANES, 8), :] = jnp.full((8, LANES), ROWS * SZ * 64, jnp.int32)
    for j in range(NPJ):
        weights[j, pl.ds(SLOTS // LANES, 8), :] = jnp.zeros((8, LANES), F32)
    for load in loads:
        load.wait()
    target_at = lax.broadcasted_iota(jnp.int32, (TGT, 2 * LANES), 0)
    z_at = lax.broadcasted_iota(jnp.int32, (SZ, 2 * LANES), 0)

    def window(row, block):
        key = jnp.concatenate([held[pl.ds(block, 1), :], held[pl.ds(block + 1, 1), :]], axis=1)
        target = jnp.where((key >> 13) == row, key & 63, 63)
        chosen = target_at == target
        parts = []
        for j in range(NPJ):
            w = jnp.concatenate(
                [weights[j, pl.ds(block, 1), :], weights[j, pl.ds(block + 1, 1), :]], axis=1
            )
            parts.append(jnp.where(chosen, w, 0.0))
        hi, lo = split2(jnp.concatenate(parts, axis=0))
        place = jnp.where(z_at == ((key >> 6) & 127), 1.0, 0.0).astype(BF16)
        both = dot(jnp.concatenate([hi, lo], axis=0), place, NT)
        return both[:CH] + both[CH:]

    @pl.loop(0, ROWS // BATCH)
    def _(step):
        first_row = step * BATCH
        bases = [starts[first_row + i] // LANES for i in range(BATCH)]
        for i in range(BATCH):
            hi, lo = split2(window(first_row + i, bases[i]))
            at = (step * (BATCH // 2) + i // 2, slice(None), pl.ds((i % 2) * SZ, SZ))
            out[at] = jnp.concatenate([hi, lo], axis=0)

        for i in range(BATCH):
            row = first_row + i
            windows = (starts[row + 1] - bases[i] * LANES + 2 * LANES - 1) // (2 * LANES)

            @pl.when(windows > 1)
            def _():
                total = lax.fori_loop(
                    0,
                    windows,
                    lambda k, acc: acc + window(row, bases[i] + 2 * k),
                    jnp.zeros((CH, SZ), F32),
                )
                hi, lo = split2(total)
                at = (step * (BATCH // 2) + i // 2, slice(None), pl.ds((i % 2) * SZ, SZ))
                out[at] = jnp.concatenate([hi, lo], axis=0)


def build(starts, keys, weights):
    return pl.pallas_call(
        build_kernel,
        out_shape=MATRIX,
        in_specs=[pl.BlockSpec(memory_space=pltpu.SMEM)] + any_specs(5),
        out_specs=pl.BlockSpec(memory_space=pltpu.VMEM),
        scratch_shapes=[
            pltpu.VMEM((SLOTS // LANES + 8, LANES), jnp.int32),
            pltpu.VMEM((NPJ, SLOTS // LANES + 8, LANES), F32),
            pltpu.SemaphoreType.DMA((NPJ + 1,)),
        ],
        compiler_params=PARAMS,
        name="build",
    )(starts, keys, *weights)


def partial_of(mat, values):
    hi, lo = split2(values)
    return dot(mat, jnp.concatenate([hi, lo], axis=0), NT)


def packed_partial(total):
    joined = total[:CH, :NB] + total[:CH, NB:] + total[CH:, :NB]
    return jnp.concatenate([joined[j * TGT : (j + 1) * TGT] for j in range(NPJ)], axis=1)


def first_kernel(field, mat, own, out, total):
    row = lax.broadcasted_iota(jnp.int32, (TGT, LANES), 0)
    couplings = jnp.where(row == 16, own[pl.ds(0, 1), :], jnp.where(row == 17, own[pl.ds(1, 1), :], 0.0))
    out[pl.ds(TGT, TGT), :] = couplings
    total[...] = jnp.zeros_like(total)

    @pl.loop(0, SX)
    def _(x):
        acc = total[...]
        for p in range(4):
            at = x * SY + 2 * p
            values = jnp.concatenate([field[at], field[at + 1]], axis=1)
            acc = acc + partial_of(mat[x * 4 + p], values)
        total[...] = acc

    out[pl.ds(0, TGT), :] = packed_partial(total[...])


def first(field, mat, own):
    return pl.pallas_call(
        first_kernel,
        out_shape=jax.ShapeDtypeStruct((2 * TGT, LANES), F32),
        in_specs=vmem_specs(3),
        out_specs=pl.BlockSpec(memory_space=pltpu.VMEM),
        scratch_shapes=[pltpu.VMEM(TOTAL, F32)],
        compiler_params=PARAMS,
        name="first",
    )(field, mat, own)


def spread(frame, axis, stride, out, at):
    me = lax.axis_index(axis)
    row = lax.broadcasted_iota(jnp.int32, (TGT, LANES), 0)
    digit = (row // stride) % 3
    for distance in range(-3, 5):
        if abs(distance) > 2:
            piece = jnp.zeros((TGT, LANES), F32)
        else:
            moved = frame if distance == 0 else pltpu.roll(frame, (-stride * distance) % TGT, 0)
            valid = (digit + distance >= 0) & (digit + distance <= 2) & (row < 36)
            piece = jnp.where(valid, moved, 0.0)
        out[(me + distance + 8) % 8, at, :] = piece


def spread_zy_kernel(frames, mine, other, out):
    row = lax.broadcasted_iota(jnp.int32, (TGT, LANES), 0)
    start = mine.shape[0] - frames * TGT
    for f in range(frames):
        at = pl.ds(start + f * TGT, TGT)
        theirs = other[at, :]
        swapped = jnp.where(row & 2 == 0, pltpu.roll(theirs, TGT - 2, 0), pltpu.roll(theirs, 2, 0))
        spread(mine[at, :] + swapped, "gy", 4, out, pl.ds(f * TGT, TGT))


def spread_x_kernel(frames, came, out):
    for f in range(frames):
        at = pl.ds(f * TGT, TGT)
        frame = came[0, at, :]
        for slot in range(1, 8):
            frame = frame + came[slot, at, :]
        spread(frame, "gx", 12, out, at)


def spread_call(kernel, frames, *arrays):
    return pl.pallas_call(
        functools.partial(kernel, frames),
        out_shape=jax.ShapeDtypeStruct((8, frames * TGT, LANES), F32),
        in_specs=vmem_specs(len(arrays)),
        out_specs=pl.BlockSpec(memory_space=pltpu.VMEM),
        compiler_params=PARAMS,
        name="spread",
    )(*arrays)


def step_kernel(first_step, last_step, *refs):
    count = 9 if first_step else 11
    field, faces, x_left, x_right, y_left, y_right, potential, came, mat = refs[:9]
    if not first_step:
        previous, coupling = refs[9:11]
    refs = refs[count:]
    if last_step:
        (new, gram), refs = refs[:2], refs[2:]
    else:
        (new, x_low, x_high, y_low, y_high, message), refs = refs[:6], refs[6:]
        outs = (x_low, x_high, y_low, y_high)
        if first_step:
            coupling, refs = refs[0], refs[1:]
    total, coef, first_z, second_z, out_sem = refs
    alpha = (1.0 if first_step else 2.0) / FILTER_HALF
    half = [0.0] + [-0.5 * c for c in STENCIL[1:]]
    diagonal = -1.5 * STENCIL[0] - FILTER_CENTRE
    write_z_matrices(first_z, second_z)

    def at(x, y):
        if x < 0:
            return x_left[(x + REACH) * SY + y]
        if x >= SX:
            return x_right[(x - SX) * SY + y]
        if y < 0:
            return y_left[x, y + REACH]
        if y >= SY:
            return y_right[x, y - SY]
        return field[x * SY + y]

    for g in range(GROUPS):
        rows = [field[4 * g + i] for i in range(4)]
        hi, lo = split2(jnp.concatenate(rows, axis=0))
        face = faces[pl.ds(g * 16, 16), :]
        face_hi = face.astype(BF16).astype(F32)
        side = jnp.concatenate(
            [face_hi, face - face_hi, face_hi, jnp.zeros((LANES - 48, LANES), F32)], axis=0
        ).T.astype(BF16)
        along_z = dot(jnp.concatenate([hi, lo], axis=1), first_z[...]) + dot(
            jnp.concatenate([hi, side], axis=1), second_z[...]
        )
        for i in range(4):
            x, y = divmod(4 * g + i, SY)
            summed = along_z[i * NB : (i + 1) * NB]
            for m in range(1, REACH + 1):
                around = (at(x + m, y) + at(x - m, y)) + (at(x, y + m) + at(x, y - m))
                summed = summed + half[m] * around
            summed = summed + (potential[pl.ds(4 * g + i, 1), :] + diagonal) * rows[i]
            result = alpha * summed
            if not first_step:
                result = result - previous[4 * g + i]
            new[4 * g + i] = result

    total[...] = jnp.zeros_like(total)
    frame = came[0]
    for slot in range(1, came.shape[0]):
        frame = frame + came[slot]
    if first_step:
        coupling[...] = frame[TGT:]
        frame = frame[:TGT]
    frame = frame * (alpha * coupling[...])
    stacked = jnp.concatenate([frame[:, j * NB : (j + 1) * NB] for j in range(NPJ)], axis=0)
    turned = stacked.T
    coef_hi = turned.astype(BF16).astype(F32)
    coef[pl.ds(0, NB), :] = jnp.concatenate([coef_hi, coef_hi], axis=1).astype(BF16)
    coef[pl.ds(NB, NB), pl.ds(0, CH)] = (turned - coef_hi).astype(BF16)

    @pl.loop(0, SX)
    def _(x):
        c_hi = coef[pl.ds(0, NB), :]
        c_lo = coef[pl.ds(NB, NB), pl.ds(0, CH)]
        acc = total[...]
        rows = []
        for p in range(4):
            pair_mat = mat[x * 4 + p]
            added = dot(c_hi, pair_mat) + dot(c_lo, pair_mat[:CH])
            for q in range(2):
                here = x * SY + 2 * p + q
                rows.append(new[here] + added[:, q * SZ : (q + 1) * SZ])
                new[here] = rows[-1]
        if not last_step:
            start_faces(x, new, outs, out_sem)
        for p in range(4):
            values = jnp.concatenate(rows[2 * p : 2 * p + 2], axis=1)
            if last_step:
                joined = jnp.concatenate(split3(values), axis=0)
                acc = acc + dot(joined, joined, NT)
            else:
                acc = acc + partial_of(mat[x * 4 + p], values)
        total[...] = acc
        if not last_step:
            for part in range(2):
                message[pl.ds((2 * x + part) * 16, 16), :] = z_faces(rows[4 * part : 4 * part + 4])

    if last_step:
        t = total[...]
        summed = t[2 * NB :, :NB] + t[:NB, 2 * NB :] + t[NB : 2 * NB, NB : 2 * NB]
        summed = summed + (t[NB : 2 * NB, :NB] + t[:NB, NB : 2 * NB]) + t[:NB, :NB]
        gram[...] = jnp.concatenate([summed[8 * q : 8 * q + 8] for q in range(4)], axis=1)
    else:
        message[pl.ds(ZROWS, TGT), :] = packed_partial(total[...])
        wait_faces(new, outs, out_sem)


def step(first_step, last_step, *arrays):
    total = (3 * NB, 3 * NB) if last_step else TOTAL
    if last_step:
        outs = [BLOCK, jax.ShapeDtypeStruct((8, LANES), F32)]
    else:
        outs = [BLOCK, X_FACE, X_FACE, Y_FACE, Y_FACE, MESSAGE] + ([FRAME] if first_step else [])
    return pl.pallas_call(
        functools.partial(step_kernel, first_step, last_step),
        out_shape=outs,
        in_specs=vmem_specs(len(arrays)),
        out_specs=vmem_specs(len(outs)),
        scratch_shapes=[
            pltpu.VMEM(total, F32),
            pltpu.VMEM((2 * NB, 2 * CH), BF16),
            pltpu.VMEM((2 * SZ, SZ), BF16),
            pltpu.VMEM((2 * SZ, SZ), BF16),
            pltpu.SemaphoreType.DMA((4, SX)),
        ],
        compiler_params=PARAMS,
        name="step",
    )(*arrays)


def finish_kernel(scale, field, grams, out, made, inverse, out_sem):
    packed = grams[0]
    for slot in range(1, grams.shape[0]):
        packed = packed + grams[slot]
    packed = packed * scale
    gram = jnp.concatenate([packed[:, q * NB : (q + 1) * NB] for q in range(4)], axis=0)
    row = lax.broadcasted_iota(jnp.int32, (NB, NB), 0)
    column = lax.broadcasted_iota(jnp.int32, (NB, NB), 1)
    eye = jnp.where(row == column, 1.0, 0.0)
    work = jnp.concatenate([gram, eye], axis=1)
    below = lax.broadcasted_iota(jnp.int32, (NB, 2 * NB), 0)
    for k in range(NB):
        root = 1.0 / jnp.sqrt(work[k : k + 1, k : k + 1])
        line = work[k : k + 1, :] * root
        inverse[pl.ds(k, 1), :] = line[:, NB:]
        if k < NB - 1:
            factor = work[:, k : k + 1] * root
            work = work - jnp.where(below > k, factor * line, 0.0)
    hi, mid, lo = split3(inverse[...])
    left = jnp.concatenate([lo, mid, hi, mid, hi, hi], axis=1)

    @pl.loop(0, SX)
    def _(x):
        for p in range(SY // 2):
            at = x * SY + 2 * p
            values = jnp.concatenate([field[at], field[at + 1]], axis=1)
            f_hi, f_mid, f_lo = split3(values)
            right = jnp.concatenate([f_hi, f_mid, f_lo, f_hi, f_mid, f_hi], axis=0)
            result = dot(left, right)
            made[at] = result[:, :SZ]
            made[at + 1] = result[:, SZ:]
            for q in range(2):
                pltpu.make_async_copy(made.at[at + q], out.at[:, at + q, :], out_sem.at[at + q]).start()

    for r in range(ROWS):
        pltpu.make_async_copy(made.at[r], out.at[:, r, :], out_sem.at[r]).wait()


def finish(scale, field, grams):
    return pl.pallas_call(
        functools.partial(finish_kernel, scale),
        out_shape=jax.ShapeDtypeStruct((NB, ROWS, SZ), F32),
        in_specs=vmem_specs(2),
        out_specs=pl.BlockSpec(memory_space=pl.ANY),
        scratch_shapes=[
            pltpu.VMEM((ROWS, NB, SZ), F32),
            pltpu.VMEM((NB, NB), F32),
            pltpu.SemaphoreType.DMA((ROWS,)),
        ],
        compiler_params=PARAMS,
        name="finish",
    )(field, grams)


def shift(value, axis, by):
    count = lax.axis_size(axis)
    return lax.ppermute(value, axis, [(i, (i + by) % count) for i in range(count)])


def local(orbitals, potential, projector, point_cell, target, point_count, coupling):
    bands, size_x, size_y, size_z = orbitals.shape
    field, x_low, x_high, y_low, y_high, z_face = rearrange(orbitals.reshape(NB, ROWS, SZ))
    pot = potential.reshape(ROWS, SZ)

    alive = lax.iota(jnp.int32, SLOTS) < point_count.reshape(())
    code = target // 2
    z_other = (code % 3 != 1).astype(jnp.int32)
    wanted = ((code // 3) * 2 + z_other) * 2 + target % 2
    key = jnp.where(alive, point_cell * 64 + wanted, ROWS * SZ * 64)
    starts = jnp.sum(
        (key[None, :] < (lax.iota(jnp.int32, ROWS + 1) * (SZ * 64))[:, None]).astype(jnp.int32), axis=1
    )
    ordered = lax.sort((key,) + tuple(projector[j] for j in range(NPJ)), num_keys=1, is_stable=False)
    ordered = [o.reshape(SLOTS // LANES, LANES) for o in ordered]
    mat = build(starts, ordered[0], ordered[1:])

    own = jnp.repeat(coupling, NB, axis=1)
    other = ()
    for k in range(DEGREE):
        start, last = k == 0, k == DEGREE - 1
        if start:
            faces = shift(z_face, "gz", 1)
        else:
            came = shift(message, "gz", 1)
            came, x_low, x_high, y_low, y_high = lax.optimization_barrier(
                (came, x_low, x_high, y_low, y_high)
            )
            faces = came
        x_left = shift(x_high, "gx", 1)
        x_right = shift(x_low, "gx", -1)
        y_left = shift(y_high, "gy", 1)
        y_right = shift(y_low, "gy", -1)
        if start:
            mat, field, faces, x_left, x_right, y_left, y_right = lax.optimization_barrier(
                (mat, field, faces, x_left, x_right, y_left, y_right)
            )
            message = first(field, mat, own)
            came = shift(message, "gz", 1)
        frames = 2 if start else 1
        sends = spread_call(spread_zy_kernel, frames, message, came)
        came = lax.all_to_all(sends, "gy", 0, 0)
        sends = spread_call(spread_x_kernel, frames, came)
        came = lax.all_to_all(sends, "gx", 0, 0)
        outs = step(start, last, field, faces, x_left, x_right, y_left, y_right, pot, came, mat, *other)
        previous = field
        if last:
            field, gram = outs
        else:
            field, x_low, x_high, y_low, y_high, message = outs[:6]
            if start:
                scales = outs[6]
            other = (previous, scales)
    axes = ("gx", "gy", "gz")
    devices = 1
    for axis in axes:
        devices *= lax.axis_size(axis)
    grams = lax.all_to_all(jnp.broadcast_to(gram[None], (devices,) + gram.shape), axes, 0, 0)
    result = finish(1.0 / float(devices * ROWS * SZ), field, grams)
    return result.reshape(bands, size_x, size_y, size_z)


def solution(mesh):
    in_specs = (
        P(None, "gx", "gy", "gz"),
        P("gx", "gy", "gz"),
        P(None, ("gx", "gy", "gz")),
        P(("gx", "gy", "gz")),
        P(("gx", "gy", "gz")),
        P("gx", "gy", "gz"),
        P(("gx", "gy", "gz"), None),
    )
    out_specs = P(None, "gx", "gy", "gz")
    return jax.shard_map(local, mesh=mesh, in_specs=in_specs, out_specs=out_specs, check_vma=False)
```

```python
import functools

import jax
import jax.numpy as jnp
from jax import lax
from jax.experimental import pallas as pl
from jax.experimental.pallas import tpu as pltpu
from jax.sharding import PartitionSpec as P

DEGREE = 4
STENCIL = (
    -5369.0 / 1800.0,
    12.0 / 7.0,
    -15.0 / 56.0,
    10.0 / 189.0,
    -1.0 / 112.0,
    2.0 / 1925.0,
    -1.0 / 16632.0,
)
FILTER_CENTRE = 9.5
FILTER_HALF = 5.5
REACH = 6

NB = 32
SX = 8
SY = 8
SZ = 128
ROWS = SX * SY
PAIRS = ROWS // 2
FACE = REACH * SY
NPJ = 4
SLOTS = 8192
TGT = 40
CH = NPJ * TGT
GROUPS = ROWS // 4
TOTAL = (2 * CH, 2 * NB)
BATCH = 4
ZROWS = GROUPS * 16
LANES = 128
F32 = jnp.float32
BF16 = jnp.bfloat16
NN = (((1,), (0,)), ((), ()))
NT = (((1,), (1,)), ((), ()))
VMEM_LIMIT = 16 * 1024 * 1024


def dot(a, b, dims=NN):
    return lax.dot_general(a, b, dims, preferred_element_type=F32)


def split2(v):
    hi = v.astype(BF16)
    return hi, (v - hi.astype(F32)).astype(BF16)


def split3(v):
    hi = v.astype(BF16)
    rest = v - hi.astype(F32)
    mid = rest.astype(BF16)
    return hi, mid, (rest - mid.astype(F32)).astype(BF16)


def band(distance):
    found = jnp.zeros(distance.shape, F32)
    for m in range(1, REACH + 1):
        found = jnp.where(jnp.abs(distance) == m, -0.5 * STENCIL[m], found)
    return found


def write_z_matrices(first, second):
    source = lax.broadcasted_iota(jnp.int32, (SZ, SZ), 0)
    z = lax.broadcasted_iota(jnp.int32, (SZ, SZ), 1)
    inner_hi, inner_lo = split2(band(source - z))
    e = lax.broadcasted_iota(jnp.int32, (16, SZ), 0)
    z = lax.broadcasted_iota(jnp.int32, (16, SZ), 1)
    face_hi, face_lo = split2(band(jnp.where(e < 8, SZ + e - z, z + 16 - e)))
    first[...] = jnp.concatenate([inner_hi, inner_hi], axis=0)
    unused = jnp.zeros((SZ - 48, SZ), BF16)
    second[...] = jnp.concatenate([inner_lo, face_hi, face_hi, face_lo, unused], axis=0)


def any_specs(count):
    return [pl.BlockSpec(memory_space=pl.ANY)] * count


def vmem_specs(count):
    return [pl.BlockSpec(memory_space=pltpu.VMEM)] * count


PARAMS = pltpu.CompilerParams(vmem_limit_bytes=VMEM_LIMIT)


def z_faces(rows):
    turned = jnp.concatenate(rows, axis=0).T
    return jnp.concatenate([turned[:8], turned[SZ - 8 :]], axis=0)


BLOCK = jax.ShapeDtypeStruct((ROWS, NB, SZ), F32)
X_FACE = jax.ShapeDtypeStruct((FACE, NB, SZ), F32)
Y_FACE = jax.ShapeDtypeStruct((SX, REACH, NB, SZ), F32)
MESSAGE = jax.ShapeDtypeStruct((ZROWS + TGT, LANES), F32)
FRAME = jax.ShapeDtypeStruct((TGT, LANES), F32)
MATRIX = jax.ShapeDtypeStruct((PAIRS, 2 * CH, 2 * SZ), BF16)


def write_faces(x, rows, x_low, x_high, y_low, y_high):
    for i in range(REACH):
        y_low[x, i] = rows[i]
        y_high[x, i] = rows[SY - REACH + i]

    if x < REACH:
        for i in range(SY):
            x_low[x * SY + i] = rows[i]

    if x >= SX - REACH:
        for i in range(SY):
            x_high[(x - (SX - REACH)) * SY + i] = rows[i]


def rearrange_kernel(src, *refs):
    field, faces, (z_face, in_sem) = refs[0], refs[1:5], refs[5:]
    for row in range(ROWS):
        pltpu.make_async_copy(src.at[:, row, :], field.at[row], in_sem.at[row]).start()

    for x in range(SX):
        for y in range(SY):
            row = x * SY + y
            pltpu.make_async_copy(src.at[:, row, :], field.at[row], in_sem.at[row]).wait()
        rows = [field[x * SY + y] for y in range(SY)]
        write_faces(x, rows, *faces)
        for part in range(2):
            z_face[pl.ds((2 * x + part) * 16, 16), :] = z_faces(rows[4 * part : 4 * part + 4])


def rearrange(orbitals):
    return pl.pallas_call(
        rearrange_kernel,
        out_shape=[BLOCK, X_FACE, X_FACE, Y_FACE, Y_FACE, jax.ShapeDtypeStruct((ZROWS, LANES), F32)],
        in_specs=any_specs(1),
        out_specs=vmem_specs(6),
        scratch_shapes=[
            pltpu.SemaphoreType.DMA((ROWS,)),
        ],
        compiler_params=PARAMS,
        name="rearrange",
    )(orbitals)


def build_kernel(starts, keys, w0, w1, w2, w3, out, held, weights, sem):
    full = pl.ds(0, SLOTS // LANES)
    loads = [pltpu.make_async_copy(keys, held.at[full], sem.at[NPJ])]
    for j, w in enumerate((w0, w1, w2, w3)):
        loads.append(pltpu.make_async_copy(w, weights.at[j, full], sem.at[j]))
    for load in loads:
        load.start()
    held[pl.ds(SLOTS // LANES, 8), :] = jnp.full((8, LANES), ROWS * SZ * 64, jnp.int32)
    for j in range(NPJ):
        weights[j, pl.ds(SLOTS // LANES, 8), :] = jnp.zeros((8, LANES), F32)
    for load in loads:
        load.wait()
    target_at = lax.broadcasted_iota(jnp.int32, (TGT, 2 * LANES), 0)
    z_at = lax.broadcasted_iota(jnp.int32, (SZ, 2 * LANES), 0)

    def window(row, block):
        key = jnp.concatenate([held[pl.ds(block, 1), :], held[pl.ds(block + 1, 1), :]], axis=1)
        target = jnp.where((key >> 13) == row, key & 63, 63)
        chosen = target_at == target
        parts = []
        for j in range(NPJ):
            w = jnp.concatenate(
                [weights[j, pl.ds(block, 1), :], weights[j, pl.ds(block + 1, 1), :]], axis=1
            )
            parts.append(jnp.where(chosen, w, 0.0))
        hi, lo = split2(jnp.concatenate(parts, axis=0))
        place = jnp.where(z_at == ((key >> 6) & 127), 1.0, 0.0).astype(BF16)
        both = dot(jnp.concatenate([hi, lo], axis=0), place, NT)
        return both[:CH] + both[CH:]

    @pl.loop(0, ROWS // BATCH)
    def _(step):
        first_row = step * BATCH
        bases = [starts[first_row + i] // LANES for i in range(BATCH)]
        for i in range(BATCH):
            hi, lo = split2(window(first_row + i, bases[i]))
            at = (step * (BATCH // 2) + i // 2, slice(None), pl.ds((i % 2) * SZ, SZ))
            out[at] = jnp.concatenate([hi, lo], axis=0)

        for i in range(BATCH):
            row = first_row + i
            windows = (starts[row + 1] - bases[i] * LANES + 2 * LANES - 1) // (2 * LANES)

            @pl.when(windows > 1)
            def _():
                total = lax.fori_loop(
                    0,
                    windows,
                    lambda k, acc: acc + window(row, bases[i] + 2 * k),
                    jnp.zeros((CH, SZ), F32),
                )
                hi, lo = split2(total)
                at = (step * (BATCH // 2) + i // 2, slice(None), pl.ds((i % 2) * SZ, SZ))
                out[at] = jnp.concatenate([hi, lo], axis=0)


def build(starts, keys, weights):
    return pl.pallas_call(
        build_kernel,
        out_shape=MATRIX,
        in_specs=[pl.BlockSpec(memory_space=pltpu.SMEM)] + any_specs(5),
        out_specs=pl.BlockSpec(memory_space=pltpu.VMEM),
        scratch_shapes=[
            pltpu.VMEM((SLOTS // LANES + 8, LANES), jnp.int32),
            pltpu.VMEM((NPJ, SLOTS // LANES + 8, LANES), F32),
            pltpu.SemaphoreType.DMA((NPJ + 1,)),
        ],
        compiler_params=PARAMS,
        name="build",
    )(starts, keys, *weights)


def partial_of(mat, values):
    hi, lo = split2(values)
    return dot(mat, jnp.concatenate([hi, lo], axis=0), NT)


def packed_partial(total):
    joined = total[:CH, :NB] + total[:CH, NB:] + total[CH:, :NB]
    return jnp.concatenate([joined[j * TGT : (j + 1) * TGT] for j in range(NPJ)], axis=1)


def first_kernel(field, mat, own, out, total):
    row = lax.broadcasted_iota(jnp.int32, (TGT, LANES), 0)
    couplings = jnp.where(row == 16, own[pl.ds(0, 1), :], jnp.where(row == 17, own[pl.ds(1, 1), :], 0.0))
    out[pl.ds(TGT, TGT), :] = couplings
    total[...] = jnp.zeros_like(total)
    for pair in range(PAIRS):
        values = jnp.concatenate([field[2 * pair], field[2 * pair + 1]], axis=1)
        total[...] = total[...] + partial_of(mat[pair], values)
    out[pl.ds(0, TGT), :] = packed_partial(total[...])


def first(field, mat, own):
    return pl.pallas_call(
        first_kernel,
        out_shape=jax.ShapeDtypeStruct((2 * TGT, LANES), F32),
        in_specs=vmem_specs(3),
        out_specs=pl.BlockSpec(memory_space=pltpu.VMEM),
        scratch_shapes=[pltpu.VMEM(TOTAL, F32)],
        compiler_params=PARAMS,
        name="first",
    )(field, mat, own)


def spread(frame, axis, stride, out, at):
    me = lax.axis_index(axis)
    row = lax.broadcasted_iota(jnp.int32, (TGT, LANES), 0)
    digit = (row // stride) % 3
    for distance in range(-3, 5):
        if abs(distance) > 2:
            piece = jnp.zeros((TGT, LANES), F32)
        else:
            moved = frame if distance == 0 else pltpu.roll(frame, (-stride * distance) % TGT, 0)
            valid = (digit + distance >= 0) & (digit + distance <= 2) & (row < 36)
            piece = jnp.where(valid, moved, 0.0)
        out[(me + distance + 8) % 8, at, :] = piece


def spread_zy_kernel(frames, mine, other, out):
    row = lax.broadcasted_iota(jnp.int32, (TGT, LANES), 0)
    start = mine.shape[0] - frames * TGT
    for f in range(frames):
        at = pl.ds(start + f * TGT, TGT)
        theirs = other[at, :]
        swapped = jnp.where(row & 2 == 0, pltpu.roll(theirs, TGT - 2, 0), pltpu.roll(theirs, 2, 0))
        spread(mine[at, :] + swapped, "gy", 4, out, pl.ds(f * TGT, TGT))


def spread_x_kernel(frames, came, out):
    for f in range(frames):
        at = pl.ds(f * TGT, TGT)
        frame = came[0, at, :]
        for slot in range(1, 8):
            frame = frame + came[slot, at, :]
        spread(frame, "gx", 12, out, at)


def spread_call(kernel, frames, *arrays):
    return pl.pallas_call(
        functools.partial(kernel, frames),
        out_shape=jax.ShapeDtypeStruct((8, frames * TGT, LANES), F32),
        in_specs=vmem_specs(len(arrays)),
        out_specs=pl.BlockSpec(memory_space=pltpu.VMEM),
        compiler_params=PARAMS,
        name="spread",
    )(*arrays)


def step_kernel(first_step, last_step, *refs):
    count = 9 if first_step else 11
    field, faces, x_left, x_right, y_left, y_right, potential, came, mat = refs[:9]
    if not first_step:
        previous, coupling = refs[9:11]
    refs = refs[count:]
    if last_step:
        (new, gram), refs = refs[:2], refs[2:]
    else:
        (new, x_low, x_high, y_low, y_high, message), refs = refs[:6], refs[6:]
        faces_out = (x_low, x_high, y_low, y_high)
        if first_step:
            coupling, refs = refs[0], refs[1:]
    total, coef, first_z, second_z = refs
    alpha = (1.0 if first_step else 2.0) / FILTER_HALF
    half = [0.0] + [-0.5 * c for c in STENCIL[1:]]
    diagonal = -1.5 * STENCIL[0] - FILTER_CENTRE
    write_z_matrices(first_z, second_z)

    def at(x, y):
        if x < 0:
            return x_left[(x + REACH) * SY + y]
        if x >= SX:
            return x_right[(x - SX) * SY + y]
        if y < 0:
            return y_left[x, y + REACH]
        if y >= SY:
            return y_right[x, y - SY]
        return field[x * SY + y]

    for g in range(GROUPS):
        rows = [field[4 * g + i] for i in range(4)]
        hi, lo = split2(jnp.concatenate(rows, axis=0))
        face = faces[pl.ds(g * 16, 16), :]
        face_hi = face.astype(BF16).astype(F32)
        side = jnp.concatenate(
            [face_hi, face - face_hi, face_hi, jnp.zeros((LANES - 48, LANES), F32)], axis=0
        ).T.astype(BF16)
        along_z = dot(jnp.concatenate([hi, lo], axis=1), first_z[...]) + dot(
            jnp.concatenate([hi, side], axis=1), second_z[...]
        )
        for i in range(4):
            x, y = divmod(4 * g + i, SY)
            summed = along_z[i * NB : (i + 1) * NB]
            for m in range(1, REACH + 1):
                around = (at(x + m, y) + at(x - m, y)) + (at(x, y + m) + at(x, y - m))
                summed = summed + half[m] * around
            summed = summed + (potential[pl.ds(4 * g + i, 1), :] + diagonal) * rows[i]
            result = alpha * summed
            if not first_step:
                result = result - previous[4 * g + i]
            new[4 * g + i] = result

    total[...] = jnp.zeros_like(total)
    frame = came[0]
    for slot in range(1, came.shape[0]):
        frame = frame + came[slot]
    if first_step:
        coupling[...] = frame[TGT:]
        frame = frame[:TGT]
    frame = frame * (alpha * coupling[...])
    stacked = jnp.concatenate([frame[:, j * NB : (j + 1) * NB] for j in range(NPJ)], axis=0)
    turned = stacked.T
    coef[...] = jnp.concatenate(split2(turned), axis=0)

    c_both = coef[...]
    for x in range(SX):
        acc = total[...]
        rows = []
        for p in range(4):
            pair_mat = mat[x * 4 + p]
            both = dot(c_both, pair_mat[:CH])
            added = both[:NB] + both[NB:] + dot(c_both[:NB], pair_mat[CH:])
            for q in range(2):
                here = x * SY + 2 * p + q
                rows.append(new[here] + added[:, q * SZ : (q + 1) * SZ])
                new[here] = rows[-1]
        if not last_step:
            write_faces(x, rows, *faces_out)
        for p in range(4):
            values = jnp.concatenate(rows[2 * p : 2 * p + 2], axis=1)
            if last_step:
                joined = jnp.concatenate(split3(values), axis=0)
                acc = acc + dot(joined, joined, NT)
            else:
                acc = acc + partial_of(mat[x * 4 + p], values)
        total[...] = acc
        if not last_step:
            for part in range(2):
                message[pl.ds((2 * x + part) * 16, 16), :] = z_faces(rows[4 * part : 4 * part + 4])

    if last_step:
        t = total[...]
        summed = t[2 * NB :, :NB] + t[:NB, 2 * NB :] + t[NB : 2 * NB, NB : 2 * NB]
        summed = summed + (t[NB : 2 * NB, :NB] + t[:NB, NB : 2 * NB]) + t[:NB, :NB]
        gram[...] = jnp.concatenate([summed[8 * q : 8 * q + 8] for q in range(4)], axis=1)
    else:
        message[pl.ds(ZROWS, TGT), :] = packed_partial(total[...])


def step(first_step, last_step, *arrays):
    total = (3 * NB, 3 * NB) if last_step else TOTAL
    if last_step:
        outs = [BLOCK, jax.ShapeDtypeStruct((8, LANES), F32)]
    else:
        outs = [BLOCK, X_FACE, X_FACE, Y_FACE, Y_FACE, MESSAGE] + ([FRAME] if first_step else [])
    return pl.pallas_call(
        functools.partial(step_kernel, first_step, last_step),
        out_shape=outs,
        in_specs=vmem_specs(len(arrays)),
        out_specs=vmem_specs(len(outs)),
        scratch_shapes=[
            pltpu.VMEM(total, F32),
            pltpu.VMEM((2 * NB, CH), BF16),
            pltpu.VMEM((2 * SZ, SZ), BF16),
            pltpu.VMEM((2 * SZ, SZ), BF16),
        ],
        compiler_params=PARAMS,
        name="step",
    )(*arrays)


def finish_kernel(scale, field, grams, out, made, inverse, out_sem):
    packed = grams[0]
    for slot in range(1, grams.shape[0]):
        packed = packed + grams[slot]
    packed = packed * scale
    gram = jnp.concatenate([packed[:, q * NB : (q + 1) * NB] for q in range(4)], axis=0)
    row = lax.broadcasted_iota(jnp.int32, (NB, NB), 0)
    column = lax.broadcasted_iota(jnp.int32, (NB, NB), 1)
    eye = jnp.where(row == column, 1.0, 0.0)
    work = jnp.concatenate([gram, eye], axis=1)
    below = lax.broadcasted_iota(jnp.int32, (NB, 2 * NB), 0)
    for k in range(NB):
        root = 1.0 / jnp.sqrt(work[k : k + 1, k : k + 1])
        line = work[k : k + 1, :] * root
        inverse[pl.ds(k, 1), :] = line[:, NB:]
        if k < NB - 1:
            factor = work[:, k : k + 1] * root
            work = work - jnp.where(below > k, factor * line, 0.0)
    hi, mid, lo = split3(inverse[...])
    left = jnp.concatenate([lo, mid, hi, mid, hi, hi], axis=1)

    for x in range(SX):
        for p in range(SY // 2):
            at = x * SY + 2 * p
            values = jnp.concatenate([field[at], field[at + 1]], axis=1)
            f_hi, f_mid, f_lo = split3(values)
            right = jnp.concatenate([f_hi, f_mid, f_lo, f_hi, f_mid, f_hi], axis=0)
            result = dot(left, right)
            made[at] = result[:, :SZ]
            made[at + 1] = result[:, SZ:]
            for q in range(2):
                pltpu.make_async_copy(made.at[at + q], out.at[:, at + q, :], out_sem.at[at + q]).start()

    for r in range(ROWS):
        pltpu.make_async_copy(made.at[r], out.at[:, r, :], out_sem.at[r]).wait()


def finish(scale, field, grams):
    return pl.pallas_call(
        functools.partial(finish_kernel, scale),
        out_shape=jax.ShapeDtypeStruct((NB, ROWS, SZ), F32),
        in_specs=vmem_specs(2),
        out_specs=pl.BlockSpec(memory_space=pl.ANY),
        scratch_shapes=[
            pltpu.VMEM((ROWS, NB, SZ), F32),
            pltpu.VMEM((NB, NB), F32),
            pltpu.SemaphoreType.DMA((ROWS,)),
        ],
        compiler_params=PARAMS,
        name="finish",
    )(field, grams)


def shift(value, axis, by):
    count = lax.axis_size(axis)
    return lax.ppermute(value, axis, [(i, (i + by) % count) for i in range(count)])


def local(orbitals, potential, projector, point_cell, target, point_count, coupling):
    bands, size_x, size_y, size_z = orbitals.shape
    field, x_low, x_high, y_low, y_high, z_face = rearrange(orbitals.reshape(NB, ROWS, SZ))
    pot = potential.reshape(ROWS, SZ)

    alive = lax.iota(jnp.int32, SLOTS) < point_count.reshape(())
    code = target // 2
    z_other = (code % 3 != 1).astype(jnp.int32)
    wanted = ((code // 3) * 2 + z_other) * 2 + target % 2
    key = jnp.where(alive, point_cell * 64 + wanted, ROWS * SZ * 64)
    starts = jnp.sum(
        (key[None, :] < (lax.iota(jnp.int32, ROWS + 1) * (SZ * 64))[:, None]).astype(jnp.int32), axis=1
    )
    ordered = lax.sort((key,) + tuple(projector[j] for j in range(NPJ)), num_keys=1, is_stable=False)
    ordered = [o.reshape(SLOTS // LANES, LANES) for o in ordered]
    mat = build(starts, ordered[0], ordered[1:])

    own = jnp.repeat(coupling, NB, axis=1)
    other = ()
    for k in range(DEGREE):
        start, last = k == 0, k == DEGREE - 1
        if start:
            faces = shift(z_face, "gz", 1)
        else:
            came = shift(message, "gz", 1)
            came, x_low, x_high, y_low, y_high = lax.optimization_barrier(
                (came, x_low, x_high, y_low, y_high)
            )
            faces = came
        x_left = shift(x_high, "gx", 1)
        x_right = shift(x_low, "gx", -1)
        y_left = shift(y_high, "gy", 1)
        y_right = shift(y_low, "gy", -1)
        if start:
            mat, field, faces, x_left, x_right, y_left, y_right = lax.optimization_barrier(
                (mat, field, faces, x_left, x_right, y_left, y_right)
            )
            message = first(field, mat, own)
            came = shift(message, "gz", 1)
        frames = 2 if start else 1
        sends = spread_call(spread_zy_kernel, frames, message, came)
        came = lax.all_to_all(sends, "gy", 0, 0)
        sends = spread_call(spread_x_kernel, frames, came)
        came = lax.all_to_all(sends, "gx", 0, 0)
        outs = step(start, last, field, faces, x_left, x_right, y_left, y_right, pot, came, mat, *other)
        previous = field
        if last:
            field, gram = outs
        else:
            field, x_low, x_high, y_low, y_high, message = outs[:6]
            if start:
                scales = outs[6]
            other = (previous, scales)
    axes = ("gx", "gy", "gz")
    devices = 1
    for axis in axes:
        devices *= lax.axis_size(axis)
    grams = lax.all_to_all(jnp.broadcast_to(gram[None], (devices,) + gram.shape), axes, 0, 0)
    result = finish(1.0 / float(devices * ROWS * SZ), field, grams)
    return result.reshape(bands, size_x, size_y, size_z)


def solution(mesh):
    in_specs = (
        P(None, "gx", "gy", "gz"),
        P("gx", "gy", "gz"),
        P(None, ("gx", "gy", "gz")),
        P(("gx", "gy", "gz")),
        P(("gx", "gy", "gz")),
        P("gx", "gy", "gz"),
        P(("gx", "gy", "gz"), None),
    )
    out_specs = P(None, "gx", "gy", "gz")
    return jax.shard_map(local, mesh=mesh, in_specs=in_specs, out_specs=out_specs, check_vma=False)
```

```python
import functools

import jax
import jax.numpy as jnp
from jax import lax
from jax.experimental import pallas as pl
from jax.experimental.pallas import tpu as pltpu
from jax.sharding import PartitionSpec as P

DEGREE = 4
STENCIL = (
    -5369.0 / 1800.0,
    12.0 / 7.0,
    -15.0 / 56.0,
    10.0 / 189.0,
    -1.0 / 112.0,
    2.0 / 1925.0,
    -1.0 / 16632.0,
)
FILTER_CENTRE = 9.5
FILTER_HALF = 5.5
REACH = 6

NB = 32
SX = 8
SY = 8
SZ = 128
ROWS = SX * SY
PAIRS = ROWS // 2
FACE = REACH * SY
NPJ = 4
SLOTS = 8192
TGT = 40
CH = NPJ * TGT
GROUPS = ROWS // 4
TOTAL = (2 * CH, 2 * NB)
BATCH = 4
ZROWS = GROUPS * 16
LANES = 128
F32 = jnp.float32
BF16 = jnp.bfloat16
NN = (((1,), (0,)), ((), ()))
NT = (((1,), (1,)), ((), ()))
VMEM_LIMIT = 16 * 1024 * 1024


def dot(a, b, dims=NN):
    return lax.dot_general(a, b, dims, preferred_element_type=F32)


def split2(v):
    hi = v.astype(BF16)
    return hi, (v - hi.astype(F32)).astype(BF16)


def split3(v):
    hi = v.astype(BF16)
    rest = v - hi.astype(F32)
    mid = rest.astype(BF16)
    return hi, mid, (rest - mid.astype(F32)).astype(BF16)


def band(distance):
    found = jnp.zeros(distance.shape, F32)
    for m in range(1, REACH + 1):
        found = jnp.where(jnp.abs(distance) == m, -0.5 * STENCIL[m], found)
    return found


def write_z_matrices(first, second):
    source = lax.broadcasted_iota(jnp.int32, (SZ, SZ), 0)
    z = lax.broadcasted_iota(jnp.int32, (SZ, SZ), 1)
    inner_hi, inner_lo = split2(band(source - z))
    e = lax.broadcasted_iota(jnp.int32, (16, SZ), 0)
    z = lax.broadcasted_iota(jnp.int32, (16, SZ), 1)
    face_hi, face_lo = split2(band(jnp.where(e < 8, SZ + e - z, z + 16 - e)))
    first[...] = jnp.concatenate([inner_hi, inner_hi], axis=0)
    unused = jnp.zeros((SZ - 48, SZ), BF16)
    second[...] = jnp.concatenate([inner_lo, face_hi, face_hi, face_lo, unused], axis=0)


def any_specs(count):
    return [pl.BlockSpec(memory_space=pl.ANY)] * count


def vmem_specs(count):
    return [pl.BlockSpec(memory_space=pltpu.VMEM)] * count


PARAMS = pltpu.CompilerParams(vmem_limit_bytes=VMEM_LIMIT)


def z_faces(rows):
    turned = jnp.concatenate(rows, axis=0).T
    return jnp.concatenate([turned[:8], turned[SZ - 8 :]], axis=0)


BLOCK = jax.ShapeDtypeStruct((ROWS, NB, SZ), F32)
X_FACE = jax.ShapeDtypeStruct((FACE, NB, SZ), F32)
Y_FACE = jax.ShapeDtypeStruct((SX, REACH, NB, SZ), F32)
MESSAGE = jax.ShapeDtypeStruct((ZROWS + TGT, LANES), F32)
FRAME = jax.ShapeDtypeStruct((TGT, LANES), F32)
MATRIX = jax.ShapeDtypeStruct((PAIRS, 2 * CH, 2 * SZ), BF16)


def write_faces(x, rows, x_low, x_high, y_low, y_high):
    for i in range(REACH):
        y_low[x, i] = rows[i]
        y_high[x, i] = rows[SY - REACH + i]

    if x < REACH:
        for i in range(SY):
            x_low[x * SY + i] = rows[i]

    if x >= SX - REACH:
        for i in range(SY):
            x_high[(x - (SX - REACH)) * SY + i] = rows[i]


def rearrange_kernel(src, *refs):
    field, faces, in_sem = refs[0], refs[1:5], refs[5]
    for row in range(ROWS):
        pltpu.make_async_copy(src.at[:, row, :], field.at[row], in_sem.at[row]).start()

    for x in range(SX):
        for y in range(SY):
            row = x * SY + y
            pltpu.make_async_copy(src.at[:, row, :], field.at[row], in_sem.at[row]).wait()
        rows = [field[x * SY + y] for y in range(SY)]
        write_faces(x, rows, *faces)


def rearrange(orbitals):
    return pl.pallas_call(
        rearrange_kernel,
        out_shape=[BLOCK, X_FACE, X_FACE, Y_FACE, Y_FACE],
        in_specs=any_specs(1),
        out_specs=vmem_specs(5),
        scratch_shapes=[
            pltpu.SemaphoreType.DMA((ROWS,)),
        ],
        compiler_params=PARAMS,
        name="rearrange",
    )(orbitals)


def build_kernel(starts, points, out, held, sem):
    full = pl.ds(0, SLOTS // LANES)
    load = pltpu.make_async_copy(points, held.at[:, full], sem)
    load.start()
    held[0, pl.ds(SLOTS // LANES, 8), :] = jnp.full((8, LANES), ROWS * SZ * 64, F32)
    for j in range(NPJ):
        held[1 + j, pl.ds(SLOTS // LANES, 8), :] = jnp.zeros((8, LANES), F32)
    load.wait()
    target_at = lax.broadcasted_iota(jnp.int32, (TGT, 2 * LANES), 0)
    z_at = lax.broadcasted_iota(jnp.int32, (SZ, 2 * LANES), 0)

    def window(row, block):
        def window_of(i):
            return jnp.concatenate([held[i, pl.ds(block, 1), :], held[i, pl.ds(block + 1, 1), :]], axis=1)

        key = window_of(0).astype(jnp.int32)
        target = jnp.where((key >> 13) == row, key & 63, 63)
        chosen = target_at == target
        parts = []
        for j in range(NPJ):
            parts.append(jnp.where(chosen, window_of(1 + j), 0.0))
        hi, lo = split2(jnp.concatenate(parts, axis=0))
        place = jnp.where(z_at == ((key >> 6) & 127), 1.0, 0.0).astype(BF16)
        both = dot(jnp.concatenate([hi, lo], axis=0), place, NT)
        return both[:CH] + both[CH:]

    @pl.loop(0, ROWS // BATCH)
    def _(step):
        first_row = step * BATCH
        bases = [starts[first_row + i] // LANES for i in range(BATCH)]
        for i in range(BATCH):
            hi, lo = split2(window(first_row + i, bases[i]))
            at = (step * (BATCH // 2) + i // 2, slice(None), pl.ds((i % 2) * SZ, SZ))
            out[at] = jnp.concatenate([hi, lo], axis=0)

        for i in range(BATCH):
            row = first_row + i
            windows = (starts[row + 1] - bases[i] * LANES + 2 * LANES - 1) // (2 * LANES)

            @pl.when(windows > 1)
            def _():
                total = lax.fori_loop(
                    0,
                    windows,
                    lambda k, acc: acc + window(row, bases[i] + 2 * k),
                    jnp.zeros((CH, SZ), F32),
                )
                hi, lo = split2(total)
                at = (step * (BATCH // 2) + i // 2, slice(None), pl.ds((i % 2) * SZ, SZ))
                out[at] = jnp.concatenate([hi, lo], axis=0)


def build(starts, points):
    return pl.pallas_call(
        build_kernel,
        out_shape=MATRIX,
        in_specs=[pl.BlockSpec(memory_space=pltpu.SMEM)] + any_specs(1),
        out_specs=pl.BlockSpec(memory_space=pltpu.VMEM),
        scratch_shapes=[
            pltpu.VMEM((1 + NPJ, SLOTS // LANES + 8, LANES), F32),
            pltpu.SemaphoreType.DMA(()),
        ],
        compiler_params=PARAMS,
        name="build",
    )(starts, points)


def partial_of(mat, values):
    hi, lo = split2(values)
    return dot(mat, jnp.concatenate([hi, lo], axis=0), NT)


def packed_partial(total):
    joined = total[:CH, :NB] + total[:CH, NB:] + total[CH:, :NB]
    return jnp.concatenate([joined[j * TGT : (j + 1) * TGT] for j in range(NPJ)], axis=1)


def first_kernel(field, mat, own, out, total):
    for g in range(GROUPS):
        out[pl.ds(16 * g, 16), :] = z_faces([field[4 * g + i] for i in range(4)])
    total[...] = jnp.zeros_like(total)
    for pair in range(PAIRS):
        values = jnp.concatenate([field[2 * pair], field[2 * pair + 1]], axis=1)
        total[...] = total[...] + partial_of(mat[pair], values)
    out[pl.ds(ZROWS, TGT), :] = packed_partial(total[...])
    out[pl.ds(ZROWS + TGT, 8), :] = own[...]


def first(field, mat, own):
    return pl.pallas_call(
        first_kernel,
        out_shape=jax.ShapeDtypeStruct((ZROWS + TGT + 8, LANES), F32),
        in_specs=vmem_specs(3),
        out_specs=pl.BlockSpec(memory_space=pltpu.VMEM),
        scratch_shapes=[pltpu.VMEM(TOTAL, F32)],
        compiler_params=PARAMS,
        name="first",
    )(field, mat, own)


def spread(frame, axis, stride, along, out, at):
    me = lax.axis_index(axis)
    target = lax.broadcasted_iota(jnp.int32, frame.shape, along)
    digit = (target // stride) % 3
    for distance in range(-3, 5):
        if abs(distance) > 2:
            piece = jnp.zeros(frame.shape, F32)
        else:
            by = (-stride * distance) % frame.shape[along]
            moved = frame if distance == 0 else pltpu.roll(frame, by, along)
            valid = (digit + distance >= 0) & (digit + distance <= 2) & (target < 36)
            piece = jnp.where(valid, moved, 0.0)
        out[(me + distance + 8) % 8, at, :] = piece


def parts_of(rows):
    return ((0, TGT, 0),) if rows == TGT else ((0, TGT, 0), (TGT, 8, 1))


def spread_zy_kernel(mine, other, out):
    for start, size, along in parts_of(out.shape[1]):
        at = pl.ds(ZROWS + start, size)
        theirs = other[at, :]
        target = lax.broadcasted_iota(jnp.int32, theirs.shape, along)
        up = pltpu.roll(theirs, theirs.shape[along] - 2, along)
        swapped = jnp.where(target & 2 == 0, up, pltpu.roll(theirs, 2, along))
        spread(mine[at, :] + swapped, "gy", 4, along, out, pl.ds(start, size))


def spread_x_kernel(came, out):
    for start, size, along in parts_of(out.shape[1]):
        at = pl.ds(start, size)
        frame = came[0, at, :]
        for slot in range(1, 8):
            frame = frame + came[slot, at, :]
        spread(frame, "gx", 12, along, out, at)


def spread_call(kernel, rows, *arrays):
    return pl.pallas_call(
        kernel,
        out_shape=jax.ShapeDtypeStruct((8, rows, LANES), F32),
        in_specs=vmem_specs(len(arrays)),
        out_specs=pl.BlockSpec(memory_space=pltpu.VMEM),
        compiler_params=PARAMS,
        name="spread",
    )(*arrays)


def step_kernel(first_step, last_step, *refs):
    count = 9 if first_step else 11
    field, faces, x_left, x_right, y_left, y_right, potential, came, mat = refs[:9]
    if not first_step:
        previous, coupling = refs[9:11]
    refs = refs[count:]
    if last_step:
        (new, gram), refs = refs[:2], refs[2:]
    else:
        (new, x_low, x_high, y_low, y_high, message), refs = refs[:6], refs[6:]
        faces_out = (x_low, x_high, y_low, y_high)
        if first_step:
            coupling, refs = refs[0], refs[1:]
    total, coef, first_z, second_z = refs
    alpha = (1.0 if first_step else 2.0) / FILTER_HALF
    half = [0.0] + [-0.5 * c for c in STENCIL[1:]]
    diagonal = -1.5 * STENCIL[0] - FILTER_CENTRE
    write_z_matrices(first_z, second_z)

    def at(x, y):
        if x < 0:
            return x_left[(x + REACH) * SY + y]
        if x >= SX:
            return x_right[(x - SX) * SY + y]
        if y < 0:
            return y_left[x, y + REACH]
        if y >= SY:
            return y_right[x, y - SY]
        return field[x * SY + y]

    for g in range(GROUPS):
        rows = [field[4 * g + i] for i in range(4)]
        hi, lo = split2(jnp.concatenate(rows, axis=0))
        face = faces[pl.ds(g * 16, 16), :]
        face_hi = face.astype(BF16).astype(F32)
        side = jnp.concatenate(
            [face_hi, face - face_hi, face_hi, jnp.zeros((LANES - 48, LANES), F32)], axis=0
        ).T.astype(BF16)
        along_z = dot(jnp.concatenate([hi, lo], axis=1), first_z[...]) + dot(
            jnp.concatenate([hi, side], axis=1), second_z[...]
        )
        for i in range(4):
            x, y = divmod(4 * g + i, SY)
            summed = along_z[i * NB : (i + 1) * NB]
            for m in range(1, REACH + 1):
                around = (at(x + m, y) + at(x - m, y)) + (at(x, y + m) + at(x, y - m))
                summed = summed + half[m] * around
            summed = summed + (potential[pl.ds(4 * g + i, 1), :] + diagonal) * rows[i]
            result = alpha * summed
            if not first_step:
                result = result - previous[4 * g + i]
            new[4 * g + i] = result

    total[...] = jnp.zeros_like(total)
    frame = came[0]
    for slot in range(1, came.shape[0]):
        frame = frame + came[slot]
    if first_step:
        by_channel = jnp.concatenate([frame[TGT:], jnp.zeros((LANES - 8, LANES), F32)], axis=0).T
        columns = [jnp.broadcast_to(by_channel[:TGT, j : j + 1], (TGT, NB)) for j in range(NPJ)]
        coupling[...] = jnp.concatenate(columns, axis=1)
        frame = frame[:TGT]
    frame = frame * (alpha * coupling[...])
    stacked = jnp.concatenate([frame[:, j * NB : (j + 1) * NB] for j in range(NPJ)], axis=0)
    turned = stacked.T
    coef[...] = jnp.concatenate(split2(turned), axis=0)

    c_both = coef[...]
    for x in range(SX):
        acc = total[...]
        rows = []
        for p in range(4):
            pair_mat = mat[x * 4 + p]
            both = dot(c_both, pair_mat[:CH])
            added = both[:NB] + both[NB:] + dot(c_both[:NB], pair_mat[CH:])
            for q in range(2):
                here = x * SY + 2 * p + q
                rows.append(new[here] + added[:, q * SZ : (q + 1) * SZ])
                new[here] = rows[-1]
        if not last_step:
            write_faces(x, rows, *faces_out)
        for p in range(4):
            values = jnp.concatenate(rows[2 * p : 2 * p + 2], axis=1)
            if last_step:
                joined = jnp.concatenate(split3(values), axis=0)
                acc = acc + dot(joined, joined, NT)
            else:
                acc = acc + partial_of(mat[x * 4 + p], values)
        total[...] = acc
        if not last_step:
            for part in range(2):
                message[pl.ds((2 * x + part) * 16, 16), :] = z_faces(rows[4 * part : 4 * part + 4])

    if last_step:
        t = total[...]
        summed = t[2 * NB :, :NB] + t[:NB, 2 * NB :] + t[NB : 2 * NB, NB : 2 * NB]
        summed = summed + (t[NB : 2 * NB, :NB] + t[:NB, NB : 2 * NB]) + t[:NB, :NB]
        gram[...] = jnp.concatenate([summed[8 * q : 8 * q + 8] for q in range(4)], axis=1)
    else:
        message[pl.ds(ZROWS, TGT), :] = packed_partial(total[...])


def step(first_step, last_step, *arrays):
    total = (3 * NB, 3 * NB) if last_step else TOTAL
    if last_step:
        outs = [BLOCK, jax.ShapeDtypeStruct((8, LANES), F32)]
    else:
        outs = [BLOCK, X_FACE, X_FACE, Y_FACE, Y_FACE, MESSAGE] + ([FRAME] if first_step else [])
    return pl.pallas_call(
        functools.partial(step_kernel, first_step, last_step),
        out_shape=outs,
        in_specs=vmem_specs(len(arrays)),
        out_specs=vmem_specs(len(outs)),
        scratch_shapes=[
            pltpu.VMEM(total, F32),
            pltpu.VMEM((2 * NB, CH), BF16),
            pltpu.VMEM((2 * SZ, SZ), BF16),
            pltpu.VMEM((2 * SZ, SZ), BF16),
        ],
        compiler_params=PARAMS,
        name="step",
    )(*arrays)


def finish_kernel(scale, field, grams, out, made, inverse, out_sem):
    packed = grams[0]
    for slot in range(1, grams.shape[0]):
        packed = packed + grams[slot]
    packed = packed * scale
    gram = jnp.concatenate([packed[:, q * NB : (q + 1) * NB] for q in range(4)], axis=0)
    row = lax.broadcasted_iota(jnp.int32, (NB, NB), 0)
    column = lax.broadcasted_iota(jnp.int32, (NB, NB), 1)
    eye = jnp.where(row == column, 1.0, 0.0)
    work = jnp.concatenate([gram, eye], axis=1)
    below = lax.broadcasted_iota(jnp.int32, (NB, 2 * NB), 0)
    for k in range(NB):
        root = 1.0 / jnp.sqrt(work[k : k + 1, k : k + 1])
        line = work[k : k + 1, :] * root
        inverse[pl.ds(k, 1), :] = line[:, NB:]
        if k < NB - 1:
            factor = work[:, k : k + 1] * root
            work = work - jnp.where(below > k, factor * line, 0.0)
    hi, mid, lo = split3(inverse[...])
    left = jnp.concatenate([lo, mid, hi, mid, hi, hi], axis=1)

    for x in range(SX):
        for p in range(SY // 2):
            at = x * SY + 2 * p
            values = jnp.concatenate([field[at], field[at + 1]], axis=1)
            f_hi, f_mid, f_lo = split3(values)
            right = jnp.concatenate([f_hi, f_mid, f_lo, f_hi, f_mid, f_hi], axis=0)
            result = dot(left, right)
            made[at] = result[:, :SZ]
            made[at + 1] = result[:, SZ:]
            for q in range(2):
                pltpu.make_async_copy(made.at[at + q], out.at[:, at + q, :], out_sem.at[at + q]).start()

    for r in range(ROWS):
        pltpu.make_async_copy(made.at[r], out.at[:, r, :], out_sem.at[r]).wait()


def finish(scale, field, grams):
    return pl.pallas_call(
        functools.partial(finish_kernel, scale),
        out_shape=jax.ShapeDtypeStruct((NB, ROWS, SZ), F32),
        in_specs=vmem_specs(2),
        out_specs=pl.BlockSpec(memory_space=pl.ANY),
        scratch_shapes=[
            pltpu.VMEM((ROWS, NB, SZ), F32),
            pltpu.VMEM((NB, NB), F32),
            pltpu.SemaphoreType.DMA((ROWS,)),
        ],
        compiler_params=PARAMS,
        name="finish",
    )(field, grams)


def shift(value, axis, by):
    count = lax.axis_size(axis)
    return lax.ppermute(value, axis, [(i, (i + by) % count) for i in range(count)])


def local(orbitals, potential, projector, point_cell, target, point_count, coupling):
    bands, size_x, size_y, size_z = orbitals.shape
    field, x_low, x_high, y_low, y_high = rearrange(orbitals.reshape(NB, ROWS, SZ))
    pot = potential.reshape(ROWS, SZ)

    alive = lax.iota(jnp.int32, SLOTS) < point_count.reshape(())
    code = target // 2
    z_other = (code % 3 != 1).astype(jnp.int32)
    wanted = ((code // 3) * 2 + z_other) * 2 + target % 2
    key = jnp.where(alive, point_cell * 64 + wanted, ROWS * SZ * 64)
    starts = jnp.sum(
        (key[None, :] < (lax.iota(jnp.int32, ROWS + 1) * (SZ * 64))[:, None]).astype(jnp.int32), axis=1
    )
    ordered = lax.sort((key,) + tuple(projector[j] for j in range(NPJ)), num_keys=1, is_stable=False)
    points = jnp.stack([ordered[0].astype(F32), *ordered[1:]]).reshape(1 + NPJ, SLOTS // LANES, LANES)
    mat = build(starts, points)

    own = jnp.pad(coupling.T, ((0, 8 - NPJ), (16, LANES - 18)))
    other = ()
    for k in range(DEGREE):
        start, last = k == 0, k == DEGREE - 1
        if start:
            x_left = shift(x_high, "gx", 1)
            x_right = shift(x_low, "gx", -1)
            mat, field, x_left, x_right = lax.optimization_barrier((mat, field, x_left, x_right))
            message = first(field, mat, own)
            message, y_low, y_high = lax.optimization_barrier((message, y_low, y_high))
        faces = shift(message, "gz", 1)
        y_left = shift(y_high, "gy", 1)
        y_right = shift(y_low, "gy", -1)
        if not start:
            faces, x_low, x_high = lax.optimization_barrier((faces, x_low, x_high))
            x_left = shift(x_high, "gx", 1)
            x_right = shift(x_low, "gx", -1)
        rows = message.shape[0] - ZROWS
        came = lax.all_to_all(spread_call(spread_zy_kernel, rows, message, faces), "gy", 0, 0)
        came = lax.all_to_all(spread_call(spread_x_kernel, rows, came), "gx", 0, 0)
        outs = step(start, last, field, faces, x_left, x_right, y_left, y_right, pot, came, mat, *other)
        previous = field
        if last:
            field, gram = outs
        else:
            field, x_low, x_high, y_low, y_high, message = outs[:6]
            if start:
                scales = outs[6]
            other = (previous, scales)
    axes = ("gx", "gy", "gz")
    devices = 1
    for axis in axes:
        devices *= lax.axis_size(axis)
    grams = lax.all_to_all(jnp.broadcast_to(gram[None], (devices,) + gram.shape), axes, 0, 0)
    result = finish(1.0 / float(devices * ROWS * SZ), field, grams)
    return result.reshape(bands, size_x, size_y, size_z)


def solution(mesh):
    in_specs = (
        P(None, "gx", "gy", "gz"),
        P("gx", "gy", "gz"),
        P(None, ("gx", "gy", "gz")),
        P(("gx", "gy", "gz")),
        P(("gx", "gy", "gz")),
        P("gx", "gy", "gz"),
        P(("gx", "gy", "gz"), None),
    )
    out_specs = P(None, "gx", "gy", "gz")
    return jax.shard_map(local, mesh=mesh, in_specs=in_specs, out_specs=out_specs, check_vma=False)
```

```python
import functools

import jax
import jax.numpy as jnp
from jax import lax
from jax.experimental import pallas as pl
from jax.experimental.pallas import tpu as pltpu
from jax.sharding import PartitionSpec as P

DEGREE = 4
STENCIL = (
    -5369.0 / 1800.0,
    12.0 / 7.0,
    -15.0 / 56.0,
    10.0 / 189.0,
    -1.0 / 112.0,
    2.0 / 1925.0,
    -1.0 / 16632.0,
)
FILTER_CENTRE = 9.5
FILTER_HALF = 5.5
REACH = 6

NB = 32
SX = 8
SY = 8
SZ = 128
ROWS = SX * SY
PAIRS = ROWS // 2
FACE = REACH * SY
NPJ = 4
SLOTS = 8192
TGT = 40
CH = NPJ * TGT
GROUPS = ROWS // 4
TOTAL = (2 * CH, 2 * NB)
BATCH = 16
ZROWS = GROUPS * 16
LANES = 128
F32 = jnp.float32
BF16 = jnp.bfloat16
NN = (((1,), (0,)), ((), ()))
NT = (((1,), (1,)), ((), ()))
VMEM_LIMIT = 16 * 1024 * 1024


def dot(a, b, dims=NN):
    return lax.dot_general(a, b, dims, preferred_element_type=F32)


def split2(v):
    hi = v.astype(BF16)
    return hi, (v - hi.astype(F32)).astype(BF16)


def split3(v):
    hi = v.astype(BF16)
    rest = v - hi.astype(F32)
    mid = rest.astype(BF16)
    return hi, mid, (rest - mid.astype(F32)).astype(BF16)


def band(distance):
    found = jnp.zeros(distance.shape, F32)
    for m in range(1, REACH + 1):
        found = jnp.where(jnp.abs(distance) == m, -0.5 * STENCIL[m], found)
    return found


def write_z_matrices(first, second):
    source = lax.broadcasted_iota(jnp.int32, (SZ, SZ), 0)
    z = lax.broadcasted_iota(jnp.int32, (SZ, SZ), 1)
    inner_hi, inner_lo = split2(band(source - z))
    e = lax.broadcasted_iota(jnp.int32, (16, SZ), 0)
    z = lax.broadcasted_iota(jnp.int32, (16, SZ), 1)
    face_hi, face_lo = split2(band(jnp.where(e < 8, SZ + e - z, z + 16 - e)))
    first[...] = jnp.concatenate([inner_hi, inner_hi], axis=0)
    unused = jnp.zeros((SZ - 48, SZ), BF16)
    second[...] = jnp.concatenate([inner_lo, face_hi, face_hi, face_lo, unused], axis=0)


def any_specs(count):
    return [pl.BlockSpec(memory_space=pl.ANY)] * count


def vmem_specs(count):
    return [pl.BlockSpec(memory_space=pltpu.VMEM)] * count


PARAMS = pltpu.CompilerParams(vmem_limit_bytes=VMEM_LIMIT)


def z_faces(rows):
    turned = jnp.concatenate(rows, axis=0).T
    return jnp.concatenate([turned[:8], turned[SZ - 8 :]], axis=0)


BLOCK = jax.ShapeDtypeStruct((ROWS, NB, SZ), F32)
X_FACE = jax.ShapeDtypeStruct((FACE, NB, SZ), F32)
Y_FACE = jax.ShapeDtypeStruct((SX, REACH, NB, SZ), F32)
MESSAGE = jax.ShapeDtypeStruct((ZROWS + TGT, LANES), F32)
FRAME = jax.ShapeDtypeStruct((TGT, LANES), F32)
MATRIX = jax.ShapeDtypeStruct((PAIRS, 2 * CH, 2 * SZ), BF16)


def write_x_faces(x, rows, x_low, x_high):
    if x < REACH:
        for i in range(SY):
            x_low[x * SY + i] = rows[i]
    if x >= SX - REACH:
        for i in range(SY):
            x_high[(x - (SX - REACH)) * SY + i] = rows[i]


def write_y_faces(x, rows, y_low, y_high):
    for i in range(REACH):
        y_low[x, i] = rows[i]
        y_high[x, i] = rows[SY - REACH + i]


def prepare_kernel(count, coupling, src, cells, targets, projector, *refs):
    field, x_low, x_high, key, own = refs[:5]
    weights, in_sem = refs[5:-1], refs[-1]
    loads = [pltpu.make_async_copy(src.at[:, row, :], field.at[row], in_sem.at[row]) for row in range(ROWS)]
    for load in loads:
        load.start()
    slot = lax.broadcasted_iota(jnp.int32, (SLOTS // LANES, LANES), 0) * LANES
    slot = slot + lax.broadcasted_iota(jnp.int32, (SLOTS // LANES, LANES), 1)
    target = targets[...]
    code = target // 2
    z_other = jnp.where(code % 3 != 1, 1, 0)
    wanted = ((code // 3) * 2 + z_other) * 2 + target % 2
    key[...] = jnp.where(slot < count[0], cells[...] * 64 + wanted, ROWS * SZ * 64)
    for j in range(NPJ):
        for i in range(SLOTS // LANES):
            weights[j][pl.ds(i, 1), :] = projector[pl.ds(j, 1), pl.ds(i * LANES, LANES)]
    channel = lax.broadcasted_iota(jnp.int32, (8, LANES), 0)
    at = lax.broadcasted_iota(jnp.int32, (8, LANES), 1)
    placed = jnp.zeros((8, LANES), F32)
    for a in range(2):
        for j in range(NPJ):
            placed = jnp.where((channel == j) & (at == 16 + a), coupling[a, j], placed)
    own[...] = placed
    for x in range(SX):
        for y in range(SY):
            loads[x * SY + y].wait()
        write_x_faces(x, [field[x * SY + y] for y in range(SY)], x_low, x_high)


def prepare(count, coupling, orbitals, cells, targets, projector):
    lines = (SLOTS // LANES, LANES)
    return pl.pallas_call(
        prepare_kernel,
        out_shape=[
            BLOCK,
            X_FACE,
            X_FACE,
            jax.ShapeDtypeStruct(lines, jnp.int32),
            jax.ShapeDtypeStruct((8, LANES), F32),
        ]
        + [jax.ShapeDtypeStruct(lines, F32)] * NPJ,
        in_specs=[pl.BlockSpec(memory_space=pltpu.SMEM)] * 2 + any_specs(1) + vmem_specs(3),
        out_specs=vmem_specs(5 + NPJ),
        scratch_shapes=[pltpu.SemaphoreType.DMA((ROWS,))],
        compiler_params=PARAMS,
        name="prepare",
    )(count, coupling, orbitals, cells.reshape(lines), targets.reshape(lines), projector)


def build_kernel(starts, points, out, held, sem):
    load = pltpu.make_async_copy(points, held.at[:, pl.ds(0, SLOTS)], sem)
    load.start()
    row = lax.broadcasted_iota(jnp.int32, (1 + NPJ, 2 * LANES), 0)
    load.wait()
    held[:, pl.ds(SLOTS, 2 * LANES)] = jnp.where(row == 0, float(ROWS * SZ * 64), 0.0)
    target_at = lax.broadcasted_iota(jnp.int32, (TGT, 2 * LANES), 0)
    z_at = lax.broadcasted_iota(jnp.int32, (SZ, 2 * LANES), 0)

    def window(row, block):
        seen = held[:, pl.ds(pl.multiple_of(block * LANES, LANES), 2 * LANES)]
        key = seen[:1].astype(jnp.int32)
        target = jnp.where((key >> 13) == row, key & 63, 63)
        chosen = target_at == target
        parts = []
        for j in range(NPJ):
            parts.append(jnp.where(chosen, seen[1 + j : 2 + j], 0.0))
        hi, lo = split2(jnp.concatenate(parts, axis=0))
        place = jnp.where(z_at == ((key >> 6) & 127), 1.0, 0.0).astype(BF16)
        both = dot(jnp.concatenate([hi, lo], axis=0), place, NT)
        return both[:CH] + both[CH:]

    @pl.loop(0, ROWS // BATCH)
    def _(step):
        first_row = step * BATCH
        bases = [starts[first_row + i] // LANES for i in range(BATCH)]
        for i in range(BATCH):
            hi, lo = split2(window(first_row + i, bases[i]))
            at = (step * (BATCH // 2) + i // 2, slice(None), pl.ds((i % 2) * SZ, SZ))
            out[at] = jnp.concatenate([hi, lo], axis=0)

        for i in range(BATCH):
            row = first_row + i
            windows = (starts[row + 1] - bases[i] * LANES + 2 * LANES - 1) // (2 * LANES)

            @pl.when(windows > 1)
            def _():
                total = lax.fori_loop(
                    0,
                    windows,
                    lambda k, acc: acc + window(row, bases[i] + 2 * k),
                    jnp.zeros((CH, SZ), F32),
                )
                hi, lo = split2(total)
                at = (step * (BATCH // 2) + i // 2, slice(None), pl.ds((i % 2) * SZ, SZ))
                out[at] = jnp.concatenate([hi, lo], axis=0)


def build(starts, points):
    return pl.pallas_call(
        build_kernel,
        out_shape=MATRIX,
        in_specs=[pl.BlockSpec(memory_space=pltpu.SMEM)] + any_specs(1),
        out_specs=pl.BlockSpec(memory_space=pltpu.VMEM),
        scratch_shapes=[
            pltpu.VMEM((1 + NPJ, SLOTS + 2 * LANES), F32),
            pltpu.SemaphoreType.DMA(()),
        ],
        compiler_params=PARAMS,
        name="build",
    )(starts, points)


def partial_of(mat, values):
    hi, lo = split2(values)
    return dot(mat, jnp.concatenate([hi, lo], axis=0), NT)


def packed_partial(total):
    joined = total[:CH, :NB] + total[:CH, NB:] + total[CH:, :NB]
    return jnp.concatenate([joined[j * TGT : (j + 1) * TGT] for j in range(NPJ)], axis=1)


def first_kernel(field, mat, own, out, y_low, y_high, total):
    for g in range(GROUPS):
        out[pl.ds(16 * g, 16), :] = z_faces([field[4 * g + i] for i in range(4)])
    for x in range(SX):
        write_y_faces(x, [field[x * SY + y] for y in range(SY)], y_low, y_high)
    total[...] = jnp.zeros_like(total)
    for pair in range(PAIRS):
        values = jnp.concatenate([field[2 * pair], field[2 * pair + 1]], axis=1)
        total[...] = total[...] + partial_of(mat[pair], values)
    out[pl.ds(ZROWS, TGT), :] = packed_partial(total[...])
    out[pl.ds(ZROWS + TGT, 8), :] = own[...]


def first(field, mat, own):
    return pl.pallas_call(
        first_kernel,
        out_shape=[jax.ShapeDtypeStruct((ZROWS + TGT + 8, LANES), F32), Y_FACE, Y_FACE],
        in_specs=vmem_specs(3),
        out_specs=vmem_specs(3),
        scratch_shapes=[pltpu.VMEM(TOTAL, F32)],
        compiler_params=PARAMS,
        name="first",
    )(field, mat, own)


def spread(frame, axis, stride, along, out, at):
    me = lax.axis_index(axis)
    target = lax.broadcasted_iota(jnp.int32, frame.shape, along)
    digit = (target // stride) % 3
    for distance in range(-3, 5):
        if abs(distance) > 2:
            piece = jnp.zeros(frame.shape, F32)
        else:
            by = (-stride * distance) % frame.shape[along]
            moved = frame if distance == 0 else pltpu.roll(frame, by, along)
            valid = (digit + distance >= 0) & (digit + distance <= 2) & (target < 36)
            piece = jnp.where(valid, moved, 0.0)
        out[(me + distance + 8) % 8, at, :] = piece


def parts_of(rows):
    return ((0, TGT, 0),) if rows == TGT else ((0, TGT, 0), (TGT, 8, 1))


def spread_zy_kernel(mine, other, out):
    for start, size, along in parts_of(out.shape[1]):
        at = pl.ds(ZROWS + start, size)
        theirs = other[at, :]
        target = lax.broadcasted_iota(jnp.int32, theirs.shape, along)
        up = pltpu.roll(theirs, theirs.shape[along] - 2, along)
        swapped = jnp.where(target & 2 == 0, up, pltpu.roll(theirs, 2, along))
        spread(mine[at, :] + swapped, "gy", 4, along, out, pl.ds(start, size))


def spread_x_kernel(came, out):
    for start, size, along in parts_of(out.shape[1]):
        at = pl.ds(start, size)
        frame = came[0, at, :]
        for slot in range(1, 8):
            frame = frame + came[slot, at, :]
        spread(frame, "gx", 12, along, out, at)


def spread_call(kernel, rows, *arrays):
    return pl.pallas_call(
        kernel,
        out_shape=jax.ShapeDtypeStruct((8, rows, LANES), F32),
        in_specs=vmem_specs(len(arrays)),
        out_specs=pl.BlockSpec(memory_space=pltpu.VMEM),
        compiler_params=PARAMS,
        name="spread",
    )(*arrays)


def step_kernel(first_step, last_step, *refs):
    count = 9 if first_step else 11
    field, faces, x_left, x_right, y_left, y_right, potential, came, mat = refs[:9]
    if not first_step:
        previous, coupling = refs[9:11]
    refs = refs[count:]
    if last_step:
        (new, gram), refs = refs[:2], refs[2:]
    else:
        (new, x_low, x_high, y_low, y_high, message), refs = refs[:6], refs[6:]
        if first_step:
            coupling, refs = refs[0], refs[1:]
    total, coef, first_z, second_z = refs
    alpha = (1.0 if first_step else 2.0) / FILTER_HALF
    half = [0.0] + [-0.5 * c for c in STENCIL[1:]]
    diagonal = -1.5 * STENCIL[0] - FILTER_CENTRE
    write_z_matrices(first_z, second_z)

    def at(x, y):
        if x < 0:
            return x_left[(x + REACH) * SY + y]
        if x >= SX:
            return x_right[(x - SX) * SY + y]
        if y < 0:
            return y_left[x, y + REACH]
        if y >= SY:
            return y_right[x, y - SY]
        return field[x * SY + y]

    for g in range(GROUPS):
        rows = [field[4 * g + i] for i in range(4)]
        hi, lo = split2(jnp.concatenate(rows, axis=0))
        face = faces[pl.ds(g * 16, 16), :]
        face_hi = face.astype(BF16).astype(F32)
        side = jnp.concatenate(
            [face_hi, face - face_hi, face_hi, jnp.zeros((LANES - 48, LANES), F32)], axis=0
        ).T.astype(BF16)
        along_z = dot(jnp.concatenate([hi, lo], axis=1), first_z[...]) + dot(
            jnp.concatenate([hi, side], axis=1), second_z[...]
        )
        for i in range(4):
            x, y = divmod(4 * g + i, SY)
            summed = along_z[i * NB : (i + 1) * NB]
            for m in range(1, REACH + 1):
                around = (at(x + m, y) + at(x - m, y)) + (at(x, y + m) + at(x, y - m))
                summed = summed + half[m] * around
            summed = summed + (potential[pl.ds(4 * g + i, 1), :] + diagonal) * rows[i]
            result = alpha * summed
            if not first_step:
                result = result - previous[4 * g + i]
            new[4 * g + i] = result

    total[...] = jnp.zeros_like(total)
    frame = came[0]
    for slot in range(1, came.shape[0]):
        frame = frame + came[slot]
    if first_step:
        by_channel = jnp.concatenate([frame[TGT:], jnp.zeros((LANES - 8, LANES), F32)], axis=0).T
        columns = [jnp.broadcast_to(by_channel[:TGT, j : j + 1], (TGT, NB)) for j in range(NPJ)]
        coupling[...] = jnp.concatenate(columns, axis=1)
        frame = frame[:TGT]
    frame = frame * (alpha * coupling[...])
    stacked = jnp.concatenate([frame[:, j * NB : (j + 1) * NB] for j in range(NPJ)], axis=0)
    turned = stacked.T
    coef[...] = jnp.concatenate(split2(turned), axis=0)

    c_both = coef[...]
    for x in range(SX):
        acc = total[...]
        rows = []
        for p in range(4):
            pair_mat = mat[x * 4 + p]
            both = dot(c_both, pair_mat[:CH])
            added = both[:NB] + both[NB:] + dot(c_both[:NB], pair_mat[CH:])
            for q in range(2):
                here = x * SY + 2 * p + q
                rows.append(new[here] + added[:, q * SZ : (q + 1) * SZ])
                new[here] = rows[-1]
        if not last_step:
            write_x_faces(x, rows, x_low, x_high)
            write_y_faces(x, rows, y_low, y_high)
        for p in range(4):
            values = jnp.concatenate(rows[2 * p : 2 * p + 2], axis=1)
            if last_step:
                joined = jnp.concatenate(split3(values), axis=0)
                acc = acc + dot(joined, joined, NT)
            else:
                acc = acc + partial_of(mat[x * 4 + p], values)
        total[...] = acc
        if not last_step:
            for part in range(2):
                message[pl.ds((2 * x + part) * 16, 16), :] = z_faces(rows[4 * part : 4 * part + 4])

    if last_step:
        t = total[...]
        summed = t[2 * NB :, :NB] + t[:NB, 2 * NB :] + t[NB : 2 * NB, NB : 2 * NB]
        summed = summed + (t[NB : 2 * NB, :NB] + t[:NB, NB : 2 * NB]) + t[:NB, :NB]
        gram[...] = jnp.concatenate([summed[8 * q : 8 * q + 8] for q in range(4)], axis=1)
    else:
        message[pl.ds(ZROWS, TGT), :] = packed_partial(total[...])


def step(first_step, last_step, *arrays):
    total = (3 * NB, 3 * NB) if last_step else TOTAL
    if last_step:
        outs = [BLOCK, jax.ShapeDtypeStruct((8, LANES), F32)]
    else:
        outs = [BLOCK, X_FACE, X_FACE, Y_FACE, Y_FACE, MESSAGE] + ([FRAME] if first_step else [])
    return pl.pallas_call(
        functools.partial(step_kernel, first_step, last_step),
        out_shape=outs,
        in_specs=vmem_specs(len(arrays)),
        out_specs=vmem_specs(len(outs)),
        scratch_shapes=[
            pltpu.VMEM(total, F32),
            pltpu.VMEM((2 * NB, CH), BF16),
            pltpu.VMEM((2 * SZ, SZ), BF16),
            pltpu.VMEM((2 * SZ, SZ), BF16),
        ],
        compiler_params=PARAMS,
        name="step",
    )(*arrays)


def finish_kernel(scale, field, grams, out, made, inverse, out_sem):
    packed = grams[0]
    for slot in range(1, grams.shape[0]):
        packed = packed + grams[slot]
    packed = packed * scale
    gram = jnp.concatenate([packed[:, q * NB : (q + 1) * NB] for q in range(4)], axis=0)
    row = lax.broadcasted_iota(jnp.int32, (NB, NB), 0)
    column = lax.broadcasted_iota(jnp.int32, (NB, NB), 1)
    eye = jnp.where(row == column, 1.0, 0.0)
    work = jnp.concatenate([gram, eye], axis=1)
    below = lax.broadcasted_iota(jnp.int32, (NB, 2 * NB), 0)
    for k in range(NB):
        root = 1.0 / jnp.sqrt(work[k : k + 1, k : k + 1])
        line = work[k : k + 1, :] * root
        inverse[pl.ds(k, 1), :] = line[:, NB:]
        if k < NB - 1:
            factor = work[:, k : k + 1] * root
            work = work - jnp.where(below > k, factor * line, 0.0)
    hi, mid, lo = split3(inverse[...])
    left = jnp.concatenate([lo, mid, hi, mid, hi, hi], axis=1)

    for x in range(SX):
        for p in range(SY // 2):
            at = x * SY + 2 * p
            values = jnp.concatenate([field[at], field[at + 1]], axis=1)
            f_hi, f_mid, f_lo = split3(values)
            right = jnp.concatenate([f_hi, f_mid, f_lo, f_hi, f_mid, f_hi], axis=0)
            result = dot(left, right)
            made[at] = result[:, :SZ]
            made[at + 1] = result[:, SZ:]
            for q in range(2):
                pltpu.make_async_copy(made.at[at + q], out.at[:, at + q, :], out_sem.at[at + q]).start()

    for r in range(ROWS):
        pltpu.make_async_copy(made.at[r], out.at[:, r, :], out_sem.at[r]).wait()


def finish(scale, field, grams):
    return pl.pallas_call(
        functools.partial(finish_kernel, scale),
        out_shape=jax.ShapeDtypeStruct((NB, ROWS, SZ), F32),
        in_specs=vmem_specs(2),
        out_specs=pl.BlockSpec(memory_space=pl.ANY),
        scratch_shapes=[
            pltpu.VMEM((ROWS, NB, SZ), F32),
            pltpu.VMEM((NB, NB), F32),
            pltpu.SemaphoreType.DMA((ROWS,)),
        ],
        compiler_params=PARAMS,
        name="finish",
    )(field, grams)


def shift(value, axis, by):
    count = lax.axis_size(axis)
    return lax.ppermute(value, axis, [(i, (i + by) % count) for i in range(count)])


def local(orbitals, potential, projector, point_cell, target, point_count, coupling):
    bands, size_x, size_y, size_z = orbitals.shape
    field, x_low, x_high, key, own, *weights = prepare(
        point_count.reshape(1), coupling, orbitals.reshape(NB, ROWS, SZ), point_cell, target, projector
    )
    pot = potential.reshape(ROWS, SZ)
    key = key.reshape(SLOTS)
    starts = jnp.sum(
        (key[None, :] < (lax.iota(jnp.int32, ROWS + 1) * (SZ * 64))[:, None]).astype(jnp.int32), axis=1
    )
    ordered = lax.sort((key, *[w.reshape(SLOTS) for w in weights]), num_keys=1, is_stable=False)
    points = jnp.stack([ordered[0].astype(F32), *ordered[1:]])
    mat = build(starts, points)

    other = ()
    for k in range(DEGREE):
        start, last = k == 0, k == DEGREE - 1
        if start:
            x_left = shift(x_high, "gx", 1)
            x_right = shift(x_low, "gx", -1)
            mat, field, x_left, x_right = lax.optimization_barrier((mat, field, x_left, x_right))
            message, y_low, y_high = first(field, mat, own)
        faces = shift(message, "gz", 1)
        y_left = shift(y_high, "gy", 1)
        y_right = shift(y_low, "gy", -1)
        if not start:
            faces, x_low, x_high = lax.optimization_barrier((faces, x_low, x_high))
            x_left = shift(x_high, "gx", 1)
            x_right = shift(x_low, "gx", -1)
        rows = message.shape[0] - ZROWS
        came = lax.all_to_all(spread_call(spread_zy_kernel, rows, message, faces), "gy", 0, 0)
        came = lax.all_to_all(spread_call(spread_x_kernel, rows, came), "gx", 0, 0)
        outs = step(start, last, field, faces, x_left, x_right, y_left, y_right, pot, came, mat, *other)
        previous = field
        if last:
            field, gram = outs
        else:
            field, x_low, x_high, y_low, y_high, message = outs[:6]
            if start:
                scales = outs[6]
            other = (previous, scales)
    axes = ("gx", "gy", "gz")
    devices = 1
    for axis in axes:
        devices *= lax.axis_size(axis)
    grams = lax.all_to_all(jnp.broadcast_to(gram[None], (devices,) + gram.shape), axes, 0, 0)
    result = finish(1.0 / float(devices * ROWS * SZ), field, grams)
    return result.reshape(bands, size_x, size_y, size_z)


def solution(mesh):
    in_specs = (
        P(None, "gx", "gy", "gz"),
        P("gx", "gy", "gz"),
        P(None, ("gx", "gy", "gz")),
        P(("gx", "gy", "gz")),
        P(("gx", "gy", "gz")),
        P("gx", "gy", "gz"),
        P(("gx", "gy", "gz"), None),
    )
    out_specs = P(None, "gx", "gy", "gz")
    return jax.shard_map(local, mesh=mesh, in_specs=in_specs, out_specs=out_specs, check_vma=False)
```

```python
import functools

import jax
import jax.numpy as jnp
from jax import lax
from jax.experimental import pallas as pl
from jax.experimental.pallas import tpu as pltpu
from jax.sharding import PartitionSpec as P

DEGREE = 4
STENCIL = (
    -5369.0 / 1800.0,
    12.0 / 7.0,
    -15.0 / 56.0,
    10.0 / 189.0,
    -1.0 / 112.0,
    2.0 / 1925.0,
    -1.0 / 16632.0,
)
FILTER_CENTRE = 9.5
FILTER_HALF = 5.5
REACH = 6

NB = 32
SX = 8
SY = 8
SZ = 128
ROWS = SX * SY
PAIRS = ROWS // 2
FACE = REACH * SY
NPJ = 4
SLOTS = 8192
TGT = 40
CH = NPJ * TGT
GROUPS = ROWS // 4
TOTAL = (2 * CH, 2 * NB)
BATCH = 16
ZROWS = GROUPS * 16
LANES = 128
F32 = jnp.float32
BF16 = jnp.bfloat16
NN = (((1,), (0,)), ((), ()))
NT = (((1,), (1,)), ((), ()))
VMEM_LIMIT = 16 * 1024 * 1024
PREPARE_LIMIT = 64256 * 1024


def dot(a, b, dims=NN):
    return lax.dot_general(a, b, dims, preferred_element_type=F32)


def split2(v):
    hi = v.astype(BF16)
    return hi, (v - hi.astype(F32)).astype(BF16)


def split3(v):
    hi = v.astype(BF16)
    rest = v - hi.astype(F32)
    mid = rest.astype(BF16)
    return hi, mid, (rest - mid.astype(F32)).astype(BF16)


def band(distance):
    found = jnp.zeros(distance.shape, F32)
    for m in range(1, REACH + 1):
        found = jnp.where(jnp.abs(distance) == m, -0.5 * STENCIL[m], found)
    return found


def write_z_matrices(first, second):
    source = lax.broadcasted_iota(jnp.int32, (SZ, SZ), 0)
    z = lax.broadcasted_iota(jnp.int32, (SZ, SZ), 1)
    inner_hi, inner_lo = split2(band(source - z))
    e = lax.broadcasted_iota(jnp.int32, (16, SZ), 0)
    z = lax.broadcasted_iota(jnp.int32, (16, SZ), 1)
    face_hi, face_lo = split2(band(jnp.where(e < 8, SZ + e - z, z + 16 - e)))
    first[...] = jnp.concatenate([inner_hi, inner_hi], axis=0)
    unused = jnp.zeros((SZ - 48, SZ), BF16)
    second[...] = jnp.concatenate([inner_lo, face_hi, face_hi, face_lo, unused], axis=0)


def any_specs(count):
    return [pl.BlockSpec(memory_space=pl.ANY)] * count


def vmem_specs(count):
    return [pl.BlockSpec(memory_space=pltpu.VMEM)] * count


PARAMS = pltpu.CompilerParams(vmem_limit_bytes=VMEM_LIMIT)


def z_faces(rows):
    turned = jnp.concatenate(rows, axis=0).T
    return jnp.concatenate([turned[:8], turned[SZ - 8 :]], axis=0)


BLOCK = jax.ShapeDtypeStruct((ROWS, NB, SZ), F32)
X_FACE = jax.ShapeDtypeStruct((FACE, NB, SZ), F32)
Y_FACE = jax.ShapeDtypeStruct((SX, REACH, NB, SZ), F32)
MESSAGE = jax.ShapeDtypeStruct((ZROWS + TGT, LANES), F32)
FRAME = jax.ShapeDtypeStruct((TGT, LANES), F32)
MATRIX = jax.ShapeDtypeStruct((PAIRS, 2 * CH, 2 * SZ), BF16)


def write_x_faces(x, rows, x_low, x_high):
    if x < REACH:
        for i in range(SY):
            x_low[x * SY + i] = rows[i]
    if x >= SX - REACH:
        for i in range(SY):
            x_high[(x - (SX - REACH)) * SY + i] = rows[i]


def write_y_faces(x, rows, y_low, y_high):
    for i in range(REACH):
        y_low[x, i] = rows[i]
        y_high[x, i] = rows[SY - REACH + i]


def prepare_kernel(count, coupling, src, cells, targets, projector, *refs):
    field, key, own = refs[:3]
    weights = refs[3 : 3 + NPJ]
    coupling_v, cells_v, targets_v, projector_v, in_sem, row_sem = refs[3 + NPJ :]
    pairs = ((cells, cells_v), (targets, targets_v), (projector, projector_v), (coupling, coupling_v))
    loads = [pltpu.make_async_copy(a, b, in_sem.at[i]) for i, (a, b) in enumerate(pairs)]
    rows = [pltpu.make_async_copy(src.at[:, row, :], field.at[row], row_sem.at[row]) for row in range(ROWS)]
    for load in loads + rows:
        load.start()
    for load in loads:
        load.wait()
    slot = lax.broadcasted_iota(jnp.int32, (SLOTS // LANES, LANES), 0) * LANES
    slot = slot + lax.broadcasted_iota(jnp.int32, (SLOTS // LANES, LANES), 1)
    target = targets_v[...]
    code = target // 2
    z_other = jnp.where(code % 3 != 1, 1, 0)
    wanted = ((code // 3) * 2 + z_other) * 2 + target % 2
    key[...] = jnp.where(slot < count[0], cells_v[...] * 64 + wanted, ROWS * SZ * 64)
    for j in range(NPJ):
        for i in range(SLOTS // LANES):
            weights[j][pl.ds(i, 1), :] = projector_v[pl.ds(j, 1), pl.ds(i * LANES, LANES)]
    channel = lax.broadcasted_iota(jnp.int32, (8, LANES), 0)
    at = lax.broadcasted_iota(jnp.int32, (8, LANES), 1)
    placed = jnp.zeros((8, LANES), F32)
    for a in range(2):
        for j in range(NPJ):
            value = jnp.broadcast_to(coupling_v[a : a + 1, j : j + 1], (8, LANES))
            placed = jnp.where((channel == j) & (at == 16 + a), value, placed)
    own[...] = placed
    for row in rows:
        row.wait()


def prepare(count, coupling, orbitals, cells, targets, projector):
    lines = (SLOTS // LANES, LANES)
    return pl.pallas_call(
        prepare_kernel,
        out_shape=[BLOCK, jax.ShapeDtypeStruct(lines, jnp.int32), jax.ShapeDtypeStruct((8, LANES), F32)]
        + [jax.ShapeDtypeStruct(lines, F32)] * NPJ,
        in_specs=[pl.BlockSpec(memory_space=pltpu.SMEM)] + any_specs(5),
        out_specs=vmem_specs(3 + NPJ),
        scratch_shapes=[
            pltpu.VMEM(coupling.shape, F32),
            pltpu.VMEM(lines, jnp.int32),
            pltpu.VMEM(lines, jnp.int32),
            pltpu.VMEM(projector.shape, F32),
            pltpu.SemaphoreType.DMA((4,)),
            pltpu.SemaphoreType.DMA((ROWS,)),
        ],
        compiler_params=pltpu.CompilerParams(vmem_limit_bytes=PREPARE_LIMIT),
        name="prepare",
    )(count, coupling, orbitals, cells.reshape(lines), targets.reshape(lines), projector)


def build_kernel(starts, points, out, held, sem):
    load = pltpu.make_async_copy(points, held.at[:, pl.ds(0, SLOTS)], sem)
    load.start()
    row = lax.broadcasted_iota(jnp.int32, (1 + NPJ, 2 * LANES), 0)
    load.wait()
    held[:, pl.ds(SLOTS, 2 * LANES)] = jnp.where(row == 0, float(ROWS * SZ * 64), 0.0)
    target_at = lax.broadcasted_iota(jnp.int32, (TGT, 2 * LANES), 0)
    z_at = lax.broadcasted_iota(jnp.int32, (SZ, 2 * LANES), 0)

    def window(row, block):
        seen = held[:, pl.ds(pl.multiple_of(block * LANES, LANES), 2 * LANES)]
        key = seen[:1].astype(jnp.int32)
        target = jnp.where((key >> 13) == row, key & 63, 63)
        chosen = target_at == target
        parts = []
        for j in range(NPJ):
            parts.append(jnp.where(chosen, seen[1 + j : 2 + j], 0.0))
        hi, lo = split2(jnp.concatenate(parts, axis=0))
        place = jnp.where(z_at == ((key >> 6) & 127), 1.0, 0.0).astype(BF16)
        both = dot(jnp.concatenate([hi, lo], axis=0), place, NT)
        return both[:CH] + both[CH:]

    @pl.loop(0, ROWS // BATCH)
    def _(step):
        first_row = step * BATCH
        bases = [starts[first_row + i] // LANES for i in range(BATCH)]
        for i in range(BATCH):
            hi, lo = split2(window(first_row + i, bases[i]))
            at = (step * (BATCH // 2) + i // 2, slice(None), pl.ds((i % 2) * SZ, SZ))
            out[at] = jnp.concatenate([hi, lo], axis=0)

        for i in range(BATCH):
            row = first_row + i
            windows = (starts[row + 1] - bases[i] * LANES + 2 * LANES - 1) // (2 * LANES)

            @pl.when(windows > 1)
            def _():
                total = lax.fori_loop(
                    0,
                    windows,
                    lambda k, acc: acc + window(row, bases[i] + 2 * k),
                    jnp.zeros((CH, SZ), F32),
                )
                hi, lo = split2(total)
                at = (step * (BATCH // 2) + i // 2, slice(None), pl.ds((i % 2) * SZ, SZ))
                out[at] = jnp.concatenate([hi, lo], axis=0)


def build(starts, points):
    return pl.pallas_call(
        build_kernel,
        out_shape=MATRIX,
        in_specs=[pl.BlockSpec(memory_space=pltpu.SMEM)] + any_specs(1),
        out_specs=pl.BlockSpec(memory_space=pltpu.VMEM),
        scratch_shapes=[
            pltpu.VMEM((1 + NPJ, SLOTS + 2 * LANES), F32),
            pltpu.SemaphoreType.DMA(()),
        ],
        compiler_params=PARAMS,
        name="build",
    )(starts, points)


def partial_of(mat, values):
    hi, lo = split2(values)
    return dot(mat, jnp.concatenate([hi, lo], axis=0), NT)


def packed_partial(total):
    joined = total[:CH, :NB] + total[:CH, NB:] + total[CH:, :NB]
    return jnp.concatenate([joined[j * TGT : (j + 1) * TGT] for j in range(NPJ)], axis=1)


def first_kernel(field, mat, own, out, x_low, x_high, y_low, y_high, total):
    for g in range(GROUPS):
        out[pl.ds(16 * g, 16), :] = z_faces([field[4 * g + i] for i in range(4)])
    for x in range(SX):
        rows = [field[x * SY + y] for y in range(SY)]
        write_x_faces(x, rows, x_low, x_high)
        write_y_faces(x, rows, y_low, y_high)
    total[...] = jnp.zeros_like(total)
    for pair in range(PAIRS):
        values = jnp.concatenate([field[2 * pair], field[2 * pair + 1]], axis=1)
        total[...] = total[...] + partial_of(mat[pair], values)
    out[pl.ds(ZROWS, TGT), :] = packed_partial(total[...])
    out[pl.ds(ZROWS + TGT, 8), :] = own[...]


def first(field, mat, own):
    return pl.pallas_call(
        first_kernel,
        out_shape=[jax.ShapeDtypeStruct((ZROWS + TGT + 8, LANES), F32), X_FACE, X_FACE, Y_FACE, Y_FACE],
        in_specs=vmem_specs(3),
        out_specs=vmem_specs(5),
        scratch_shapes=[pltpu.VMEM(TOTAL, F32)],
        compiler_params=PARAMS,
        name="first",
    )(field, mat, own)


def spread(frame, axis, stride, along, out, at):
    me = lax.axis_index(axis)
    target = lax.broadcasted_iota(jnp.int32, frame.shape, along)
    digit = (target // stride) % 3
    for distance in range(-3, 5):
        if abs(distance) > 2:
            piece = jnp.zeros(frame.shape, F32)
        else:
            by = (-stride * distance) % frame.shape[along]
            moved = frame if distance == 0 else pltpu.roll(frame, by, along)
            valid = (digit + distance >= 0) & (digit + distance <= 2) & (target < 36)
            piece = jnp.where(valid, moved, 0.0)
        out[(me + distance + 8) % 8, at, :] = piece


def parts_of(rows):
    return ((0, TGT, 0),) if rows == TGT else ((0, TGT, 0), (TGT, 8, 1))


def spread_zy_kernel(mine, other, out):
    for start, size, along in parts_of(out.shape[1]):
        at = pl.ds(ZROWS + start, size)
        theirs = other[at, :]
        target = lax.broadcasted_iota(jnp.int32, theirs.shape, along)
        up = pltpu.roll(theirs, theirs.shape[along] - 2, along)
        swapped = jnp.where(target & 2 == 0, up, pltpu.roll(theirs, 2, along))
        spread(mine[at, :] + swapped, "gy", 4, along, out, pl.ds(start, size))


def spread_x_kernel(came, out):
    for start, size, along in parts_of(out.shape[1]):
        at = pl.ds(start, size)
        frame = came[0, at, :]
        for slot in range(1, 8):
            frame = frame + came[slot, at, :]
        spread(frame, "gx", 12, along, out, at)


def spread_call(kernel, rows, *arrays):
    return pl.pallas_call(
        kernel,
        out_shape=jax.ShapeDtypeStruct((8, rows, LANES), F32),
        in_specs=vmem_specs(len(arrays)),
        out_specs=pl.BlockSpec(memory_space=pltpu.VMEM),
        compiler_params=PARAMS,
        name="spread",
    )(*arrays)


def step_kernel(first_step, last_step, *refs):
    count = 9 if first_step else 11
    field, faces, x_left, x_right, y_left, y_right, potential, came, mat = refs[:9]
    if not first_step:
        previous, coupling = refs[9:11]
    refs = refs[count:]
    if last_step:
        (new, gram), refs = refs[:2], refs[2:]
    else:
        (new, x_low, x_high, y_low, y_high, message), refs = refs[:6], refs[6:]
        if first_step:
            coupling, refs = refs[0], refs[1:]
    total, coef, first_z, second_z = refs
    alpha = (1.0 if first_step else 2.0) / FILTER_HALF
    half = [0.0] + [-0.5 * c for c in STENCIL[1:]]
    diagonal = -1.5 * STENCIL[0] - FILTER_CENTRE
    write_z_matrices(first_z, second_z)

    def at(x, y):
        if x < 0:
            return x_left[(x + REACH) * SY + y]
        if x >= SX:
            return x_right[(x - SX) * SY + y]
        if y < 0:
            return y_left[x, y + REACH]
        if y >= SY:
            return y_right[x, y - SY]
        return field[x * SY + y]

    for g in range(GROUPS):
        rows = [field[4 * g + i] for i in range(4)]
        hi, lo = split2(jnp.concatenate(rows, axis=0))
        face = faces[pl.ds(g * 16, 16), :]
        face_hi = face.astype(BF16).astype(F32)
        side = jnp.concatenate(
            [face_hi, face - face_hi, face_hi, jnp.zeros((LANES - 48, LANES), F32)], axis=0
        ).T.astype(BF16)
        along_z = dot(jnp.concatenate([hi, lo], axis=1), first_z[...]) + dot(
            jnp.concatenate([hi, side], axis=1), second_z[...]
        )
        for i in range(4):
            x, y = divmod(4 * g + i, SY)
            summed = along_z[i * NB : (i + 1) * NB]
            for m in range(1, REACH + 1):
                around = (at(x + m, y) + at(x - m, y)) + (at(x, y + m) + at(x, y - m))
                summed = summed + half[m] * around
            summed = summed + (potential[pl.ds(4 * g + i, 1), :] + diagonal) * rows[i]
            result = alpha * summed
            if not first_step:
                result = result - previous[4 * g + i]
            new[4 * g + i] = result

    total[...] = jnp.zeros_like(total)
    frame = came[0]
    for slot in range(1, came.shape[0]):
        frame = frame + came[slot]
    if first_step:
        by_channel = jnp.concatenate([frame[TGT:], jnp.zeros((LANES - 8, LANES), F32)], axis=0).T
        columns = [jnp.broadcast_to(by_channel[:TGT, j : j + 1], (TGT, NB)) for j in range(NPJ)]
        coupling[...] = jnp.concatenate(columns, axis=1)
        frame = frame[:TGT]
    frame = frame * (alpha * coupling[...])
    stacked = jnp.concatenate([frame[:, j * NB : (j + 1) * NB] for j in range(NPJ)], axis=0)
    turned = stacked.T
    coef[...] = jnp.concatenate(split2(turned), axis=0)

    c_both = coef[...]
    for x in range(SX):
        acc = total[...]
        rows = []
        for p in range(4):
            pair_mat = mat[x * 4 + p]
            both = dot(c_both, pair_mat[:CH])
            added = both[:NB] + both[NB:] + dot(c_both[:NB], pair_mat[CH:])
            for q in range(2):
                here = x * SY + 2 * p + q
                rows.append(new[here] + added[:, q * SZ : (q + 1) * SZ])
                new[here] = rows[-1]
        if not last_step:
            write_x_faces(x, rows, x_low, x_high)
            write_y_faces(x, rows, y_low, y_high)
        for p in range(4):
            values = jnp.concatenate(rows[2 * p : 2 * p + 2], axis=1)
            if last_step:
                joined = jnp.concatenate(split3(values), axis=0)
                acc = acc + dot(joined, joined, NT)
            else:
                acc = acc + partial_of(mat[x * 4 + p], values)
        total[...] = acc
        if not last_step:
            for part in range(2):
                message[pl.ds((2 * x + part) * 16, 16), :] = z_faces(rows[4 * part : 4 * part + 4])

    if last_step:
        t = total[...]
        summed = t[2 * NB :, :NB] + t[:NB, 2 * NB :] + t[NB : 2 * NB, NB : 2 * NB]
        summed = summed + (t[NB : 2 * NB, :NB] + t[:NB, NB : 2 * NB]) + t[:NB, :NB]
        gram[...] = jnp.concatenate([summed[8 * q : 8 * q + 8] for q in range(4)], axis=1)
    else:
        message[pl.ds(ZROWS, TGT), :] = packed_partial(total[...])


def step(first_step, last_step, *arrays):
    total = (3 * NB, 3 * NB) if last_step else TOTAL
    if last_step:
        outs = [BLOCK, jax.ShapeDtypeStruct((8, LANES), F32)]
    else:
        outs = [BLOCK, X_FACE, X_FACE, Y_FACE, Y_FACE, MESSAGE] + ([FRAME] if first_step else [])
    return pl.pallas_call(
        functools.partial(step_kernel, first_step, last_step),
        out_shape=outs,
        in_specs=vmem_specs(len(arrays)),
        out_specs=vmem_specs(len(outs)),
        scratch_shapes=[
            pltpu.VMEM(total, F32),
            pltpu.VMEM((2 * NB, CH), BF16),
            pltpu.VMEM((2 * SZ, SZ), BF16),
            pltpu.VMEM((2 * SZ, SZ), BF16),
        ],
        compiler_params=PARAMS,
        name="step",
    )(*arrays)


def finish_kernel(scale, field, grams, out, made, inverse, out_sem):
    packed = grams[0]
    for slot in range(1, grams.shape[0]):
        packed = packed + grams[slot]
    packed = packed * scale
    gram = jnp.concatenate([packed[:, q * NB : (q + 1) * NB] for q in range(4)], axis=0)
    row = lax.broadcasted_iota(jnp.int32, (NB, NB), 0)
    column = lax.broadcasted_iota(jnp.int32, (NB, NB), 1)
    eye = jnp.where(row == column, 1.0, 0.0)
    work = jnp.concatenate([gram, eye], axis=1)
    below = lax.broadcasted_iota(jnp.int32, (NB, 2 * NB), 0)
    for k in range(NB):
        root = 1.0 / jnp.sqrt(work[k : k + 1, k : k + 1])
        line = work[k : k + 1, :] * root
        inverse[pl.ds(k, 1), :] = line[:, NB:]
        if k < NB - 1:
            factor = work[:, k : k + 1] * root
            work = work - jnp.where(below > k, factor * line, 0.0)
    hi, mid, lo = split3(inverse[...])
    left = jnp.concatenate([lo, mid, hi, mid, hi, hi], axis=1)

    for x in range(SX):
        for p in range(SY // 2):
            at = x * SY + 2 * p
            values = jnp.concatenate([field[at], field[at + 1]], axis=1)
            f_hi, f_mid, f_lo = split3(values)
            right = jnp.concatenate([f_hi, f_mid, f_lo, f_hi, f_mid, f_hi], axis=0)
            result = dot(left, right)
            made[at] = result[:, :SZ]
            made[at + 1] = result[:, SZ:]
            for q in range(2):
                pltpu.make_async_copy(made.at[at + q], out.at[:, at + q, :], out_sem.at[at + q]).start()

    for r in range(ROWS):
        pltpu.make_async_copy(made.at[r], out.at[:, r, :], out_sem.at[r]).wait()


def finish(scale, field, grams):
    return pl.pallas_call(
        functools.partial(finish_kernel, scale),
        out_shape=jax.ShapeDtypeStruct((NB, ROWS, SZ), F32),
        in_specs=vmem_specs(2),
        out_specs=pl.BlockSpec(memory_space=pl.ANY),
        scratch_shapes=[
            pltpu.VMEM((ROWS, NB, SZ), F32),
            pltpu.VMEM((NB, NB), F32),
            pltpu.SemaphoreType.DMA((ROWS,)),
        ],
        compiler_params=PARAMS,
        name="finish",
    )(field, grams)


def shift(value, axis, by):
    count = lax.axis_size(axis)
    return lax.ppermute(value, axis, [(i, (i + by) % count) for i in range(count)])


def local(orbitals, potential, projector, point_cell, target, point_count, coupling):
    bands, size_x, size_y, size_z = orbitals.shape
    field, key, own, *weights = prepare(
        point_count.reshape(1), coupling, orbitals.reshape(NB, ROWS, SZ), point_cell, target, projector
    )
    pot = potential.reshape(ROWS, SZ)
    key = key.reshape(SLOTS)
    starts = jnp.sum(
        (key[None, :] < (lax.iota(jnp.int32, ROWS + 1) * (SZ * 64))[:, None]).astype(jnp.int32), axis=1
    )
    ordered = lax.sort((key, *[w.reshape(SLOTS) for w in weights]), num_keys=1, is_stable=False)
    points = jnp.stack([ordered[0].astype(F32), *ordered[1:]])
    mat = build(starts, points)

    other = ()
    for k in range(DEGREE):
        start, last = k == 0, k == DEGREE - 1
        if start:
            message, x_low, x_high, y_low, y_high = first(field, mat, own)
        faces = shift(message, "gz", 1)
        y_left = shift(y_high, "gy", 1)
        y_right = shift(y_low, "gy", -1)
        faces, x_low, x_high = lax.optimization_barrier((faces, x_low, x_high))
        x_left = shift(x_high, "gx", 1)
        x_right = shift(x_low, "gx", -1)
        rows = message.shape[0] - ZROWS
        came = lax.all_to_all(spread_call(spread_zy_kernel, rows, message, faces), "gy", 0, 0)
        came = lax.all_to_all(spread_call(spread_x_kernel, rows, came), "gx", 0, 0)
        outs = step(start, last, field, faces, x_left, x_right, y_left, y_right, pot, came, mat, *other)
        previous = field
        if last:
            field, gram = outs
        else:
            field, x_low, x_high, y_low, y_high, message = outs[:6]
            if start:
                scales = outs[6]
            other = (previous, scales)
    axes = ("gx", "gy", "gz")
    devices = 1
    for axis in axes:
        devices *= lax.axis_size(axis)
    grams = lax.all_to_all(jnp.broadcast_to(gram[None], (devices,) + gram.shape), axes, 0, 0)
    result = finish(1.0 / float(devices * ROWS * SZ), field, grams)
    return result.reshape(bands, size_x, size_y, size_z)


def solution(mesh):
    in_specs = (
        P(None, "gx", "gy", "gz"),
        P("gx", "gy", "gz"),
        P(None, ("gx", "gy", "gz")),
        P(("gx", "gy", "gz")),
        P(("gx", "gy", "gz")),
        P("gx", "gy", "gz"),
        P(("gx", "gy", "gz"), None),
    )
    out_specs = P(None, "gx", "gy", "gz")
    return jax.shard_map(local, mesh=mesh, in_specs=in_specs, out_specs=out_specs, check_vma=False)
```

```python
import functools

import jax
import jax.numpy as jnp
from jax import lax
from jax.experimental import pallas as pl
from jax.experimental.pallas import tpu as pltpu
from jax.sharding import PartitionSpec as P

DEGREE = 4
STENCIL = (
    -5369.0 / 1800.0,
    12.0 / 7.0,
    -15.0 / 56.0,
    10.0 / 189.0,
    -1.0 / 112.0,
    2.0 / 1925.0,
    -1.0 / 16632.0,
)
FILTER_CENTRE = 9.5
FILTER_HALF = 5.5
REACH = 6

NB = 32
SX = 8
SY = 8
SZ = 128
ROWS = SX * SY
PAIRS = ROWS // 2
FACE = REACH * SY
NPJ = 4
SLOTS = 8192
TGT = 40
CH = NPJ * TGT
GROUPS = ROWS // 4
TOTAL = (NB, CH)
BATCH = 16
ZROWS = GROUPS * 16
PACK = 24
LANES = 128
F32 = jnp.float32
BF16 = jnp.bfloat16
NN = (((1,), (0,)), ((), ()))
NT = (((1,), (1,)), ((), ()))
VMEM_LIMIT = 16 * 1024 * 1024
PREPARE_LIMIT = 64256 * 1024


def dot(a, b, dims=NN):
    return lax.dot_general(a, b, dims, preferred_element_type=F32)


def split2(v):
    hi = v.astype(BF16)
    return hi, (v - hi.astype(F32)).astype(BF16)


def split3(v):
    hi = v.astype(BF16)
    rest = v - hi.astype(F32)
    mid = rest.astype(BF16)
    return hi, mid, (rest - mid.astype(F32)).astype(BF16)


def band(distance):
    found = jnp.zeros(distance.shape, F32)
    for m in range(1, REACH + 1):
        found = jnp.where(jnp.abs(distance) == m, -0.5 * STENCIL[m], found)
    return found


def write_z_matrices(first, second):
    source = lax.broadcasted_iota(jnp.int32, (SZ, SZ), 0)
    z = lax.broadcasted_iota(jnp.int32, (SZ, SZ), 1)
    inner_hi, inner_lo = split2(band(source - z))
    e = lax.broadcasted_iota(jnp.int32, (16, SZ), 0)
    z = lax.broadcasted_iota(jnp.int32, (16, SZ), 1)
    face_hi, face_lo = split2(band(jnp.where(e < 8, SZ + e - z, z + 16 - e)))
    first[...] = jnp.concatenate([inner_hi, inner_hi], axis=0)
    unused = jnp.zeros((SZ - 48, SZ), BF16)
    second[...] = jnp.concatenate([inner_lo, face_hi, face_hi, face_lo, unused], axis=0)


def any_specs(count):
    return [pl.BlockSpec(memory_space=pl.ANY)] * count


def vmem_specs(count):
    return [pl.BlockSpec(memory_space=pltpu.VMEM)] * count


PARAMS = pltpu.CompilerParams(vmem_limit_bytes=VMEM_LIMIT)


def z_faces(rows):
    turned = jnp.concatenate(rows, axis=0).T
    return jnp.concatenate([turned[:8], turned[SZ - 8 :]], axis=0)


BLOCK = jax.ShapeDtypeStruct((ROWS, NB, SZ), F32)
X_FACE = jax.ShapeDtypeStruct((FACE, NB, SZ), F32)
Y_FACE = jax.ShapeDtypeStruct((SX, REACH, NB, SZ), F32)
MESSAGE = jax.ShapeDtypeStruct((ZROWS + TGT, LANES), F32)
FRAME = jax.ShapeDtypeStruct((TGT, LANES), F32)
MATRIX = jax.ShapeDtypeStruct((PAIRS, 2 * CH, 2 * SZ), BF16)


def write_x_faces(x, rows, x_low, x_high):
    if x < REACH:
        for i in range(SY):
            x_low[x * SY + i] = rows[i]
    if x >= SX - REACH:
        for i in range(SY):
            x_high[(x - (SX - REACH)) * SY + i] = rows[i]


def write_y_faces(x, rows, y_low, y_high):
    for i in range(REACH):
        y_low[x, i] = rows[i]
        y_high[x, i] = rows[SY - REACH + i]


def prepare_kernel(count, coupling, src, cells, targets, projector, *refs):
    field, key, own = refs[:3]
    weights = refs[3 : 3 + NPJ]
    coupling_v, cells_v, targets_v, projector_v, in_sem, row_sem = refs[3 + NPJ :]
    pairs = ((cells, cells_v), (targets, targets_v), (projector, projector_v), (coupling, coupling_v))
    loads = [pltpu.make_async_copy(a, b, in_sem.at[i]) for i, (a, b) in enumerate(pairs)]
    rows = [pltpu.make_async_copy(src.at[:, row, :], field.at[row], row_sem.at[row]) for row in range(ROWS)]
    for load in loads + rows:
        load.start()
    for load in loads:
        load.wait()
    slot = lax.broadcasted_iota(jnp.int32, (SLOTS // LANES, LANES), 0) * LANES
    slot = slot + lax.broadcasted_iota(jnp.int32, (SLOTS // LANES, LANES), 1)
    target = targets_v[...]
    code = target // 2
    z_other = jnp.where(code % 3 != 1, 1, 0)
    wanted = ((code // 3) * 2 + z_other) * 2 + target % 2
    key[...] = jnp.where(slot < count[0], cells_v[...] * 64 + wanted, ROWS * SZ * 64)
    for j in range(NPJ):
        for i in range(SLOTS // LANES):
            weights[j][pl.ds(i, 1), :] = projector_v[pl.ds(j, 1), pl.ds(i * LANES, LANES)]
    channel = lax.broadcasted_iota(jnp.int32, (8, LANES), 0)
    at = lax.broadcasted_iota(jnp.int32, (8, LANES), 1)
    placed = jnp.zeros((8, LANES), F32)
    for a in range(2):
        for j in range(NPJ):
            value = jnp.broadcast_to(coupling_v[a : a + 1, j : j + 1], (8, LANES))
            placed = jnp.where((channel == j) & (at == 16 + a), value, placed)
    own[...] = placed
    for row in rows:
        row.wait()


def prepare(count, coupling, orbitals, cells, targets, projector):
    lines = (SLOTS // LANES, LANES)
    return pl.pallas_call(
        prepare_kernel,
        out_shape=[BLOCK, jax.ShapeDtypeStruct(lines, jnp.int32), jax.ShapeDtypeStruct((8, LANES), F32)]
        + [jax.ShapeDtypeStruct(lines, F32)] * NPJ,
        in_specs=[pl.BlockSpec(memory_space=pltpu.SMEM)] + any_specs(5),
        out_specs=vmem_specs(3 + NPJ),
        scratch_shapes=[
            pltpu.VMEM(coupling.shape, F32),
            pltpu.VMEM(lines, jnp.int32),
            pltpu.VMEM(lines, jnp.int32),
            pltpu.VMEM(projector.shape, F32),
            pltpu.SemaphoreType.DMA((4,)),
            pltpu.SemaphoreType.DMA((ROWS,)),
        ],
        compiler_params=pltpu.CompilerParams(vmem_limit_bytes=PREPARE_LIMIT),
        name="prepare",
    )(count, coupling, orbitals, cells.reshape(lines), targets.reshape(lines), projector)


def build_kernel(starts, points, out, held, sem):
    load = pltpu.make_async_copy(points, held.at[:, pl.ds(0, SLOTS)], sem)
    load.start()
    row = lax.broadcasted_iota(jnp.int32, (1 + NPJ, 2 * LANES), 0)
    load.wait()
    held[:, pl.ds(SLOTS, 2 * LANES)] = jnp.where(row == 0, float(ROWS * SZ * 64), 0.0)
    target_at = lax.broadcasted_iota(jnp.int32, (TGT, 2 * LANES), 0)
    z_at = lax.broadcasted_iota(jnp.int32, (SZ, 2 * LANES), 0)

    def window(row, block):
        seen = held[:, pl.ds(pl.multiple_of(block * LANES, LANES), 2 * LANES)]
        key = seen[:1].astype(jnp.int32)
        target = jnp.where((key >> 13) == row, key & 63, 63)
        chosen = target_at == target
        parts = []
        for j in range(NPJ):
            parts.append(jnp.where(chosen, seen[1 + j : 2 + j], 0.0))
        hi, lo = split2(jnp.concatenate(parts, axis=0))
        place = jnp.where(z_at == ((key >> 6) & 127), 1.0, 0.0).astype(BF16)
        both = dot(jnp.concatenate([hi, lo], axis=0), place, NT)
        return both[:CH] + both[CH:]

    @pl.loop(0, ROWS // BATCH)
    def _(step):
        first_row = step * BATCH
        bases = [starts[first_row + i] // LANES for i in range(BATCH)]
        for i in range(BATCH):
            hi, lo = split2(window(first_row + i, bases[i]))
            at = (step * (BATCH // 2) + i // 2, slice(None), pl.ds((i % 2) * SZ, SZ))
            out[at] = jnp.concatenate([hi, lo], axis=0)

        for i in range(BATCH):
            row = first_row + i
            windows = (starts[row + 1] - bases[i] * LANES + 2 * LANES - 1) // (2 * LANES)

            @pl.when(windows > 1)
            def _():
                total = lax.fori_loop(
                    0,
                    windows,
                    lambda k, acc: acc + window(row, bases[i] + 2 * k),
                    jnp.zeros((CH, SZ), F32),
                )
                hi, lo = split2(total)
                at = (step * (BATCH // 2) + i // 2, slice(None), pl.ds((i % 2) * SZ, SZ))
                out[at] = jnp.concatenate([hi, lo], axis=0)


def build(starts, points):
    return pl.pallas_call(
        build_kernel,
        out_shape=MATRIX,
        in_specs=[pl.BlockSpec(memory_space=pltpu.SMEM)] + any_specs(1),
        out_specs=pl.BlockSpec(memory_space=pltpu.VMEM),
        scratch_shapes=[
            pltpu.VMEM((1 + NPJ, SLOTS + 2 * LANES), F32),
            pltpu.SemaphoreType.DMA(()),
        ],
        compiler_params=PARAMS,
        name="build",
    )(starts, points)


def partial_of(mat, values):
    hi, lo = split2(values)
    both = dot(jnp.concatenate([hi, lo], axis=0), mat[:CH], NT)
    return both[:NB] + both[NB:] + dot(hi, mat[CH:], NT)


def packed_partial(total):
    joined = total.T
    return jnp.concatenate([joined[j * TGT : (j + 1) * TGT] for j in range(NPJ)], axis=1)


def first_kernel(field, mat, own, out, x_low, x_high, y_low, y_high, total):
    for g in range(GROUPS):
        out[pl.ds(16 * g, 16), :] = z_faces([field[4 * g + i] for i in range(4)])
    for x in range(SX):
        rows = [field[x * SY + y] for y in range(SY)]
        write_x_faces(x, rows, x_low, x_high)
        write_y_faces(x, rows, y_low, y_high)
    total[...] = jnp.zeros_like(total)
    for pair in range(PAIRS):
        values = jnp.concatenate([field[2 * pair], field[2 * pair + 1]], axis=1)
        total[...] = total[...] + partial_of(mat[pair], values)
    out[pl.ds(ZROWS, TGT), :] = packed_partial(total[...])
    out[pl.ds(ZROWS + TGT, 8), :] = own[...]


def first(field, mat, own):
    return pl.pallas_call(
        first_kernel,
        out_shape=[jax.ShapeDtypeStruct((ZROWS + TGT + 8, LANES), F32), X_FACE, X_FACE, Y_FACE, Y_FACE],
        in_specs=vmem_specs(3),
        out_specs=vmem_specs(5),
        scratch_shapes=[pltpu.VMEM(TOTAL, F32)],
        compiler_params=PARAMS,
        name="first",
    )(field, mat, own)


def neighbours(axis):
    me = lax.axis_index(axis)
    return [(d, (me + d + 8) % 8, (me - d + 8) % 8) for d in (-2, -1, 1, 2)]


def packed(frame, stride, d):
    found = []
    for start in range(0, 36, 3 * stride):
        rows = frame[start : start + 3 * stride]
        gap = jnp.zeros((stride, LANES), F32)
        if d == 1:
            found.append(rows[stride:])
        elif d == -1:
            found.append(rows[: 2 * stride])
        elif d == 2:
            found += [rows[2 * stride :], gap]
        else:
            found += [gap, rows[:stride]]
    return jnp.concatenate(found, axis=0)


def shifted(frame, stride, d):
    target = lax.broadcasted_iota(jnp.int32, frame.shape, 1)
    digit = (target // stride) % 3
    valid = (digit + d >= 0) & (digit + d <= 2) & (target < 36)
    return jnp.where(valid, pltpu.roll(frame, (-stride * d) % LANES, 1), 0.0)


def send(axis, stride, frame, out):
    me = lax.axis_index(axis)
    for d in (-3, 0, 3, 4):
        out[(me + d + 8) % 8] = jnp.zeros(out.shape[1:], F32)
    for d, to, _ in neighbours(axis):
        out[to, pl.ds(0, PACK), :] = packed(frame[:TGT], stride, d)
        if frame.shape[0] > TGT:
            out[to, pl.ds(PACK, 8), :] = shifted(frame[TGT:], stride, d)


def received(axis, stride, frame, came):
    below = above = couplings = 0.0
    for d, _, source in neighbours(axis):
        block = came[source]
        if d > 0:
            below = below + block[:PACK]
        else:
            above = above + block[:PACK]
        if frame.shape[0] > TGT:
            couplings = couplings + block[PACK:]
    gap = jnp.zeros((stride, LANES), F32)
    first, last = [], []
    for start in range(0, PACK, 2 * stride):
        first += [below[start : start + 2 * stride], gap]
        last += [gap, above[start : start + 2 * stride]]
    rest = [jnp.zeros((TGT - 36, LANES), F32)]
    added = jnp.concatenate(first + rest, axis=0) + jnp.concatenate(last + rest, axis=0)
    if frame.shape[0] == TGT:
        return frame + added
    return frame + jnp.concatenate([added, couplings], axis=0)


def swap_z(theirs, along):
    target = lax.broadcasted_iota(jnp.int32, theirs.shape, along)
    up = pltpu.roll(theirs, theirs.shape[along] - 2, along)
    return jnp.where(target & 2 == 0, up, pltpu.roll(theirs, 2, along))


def spread_zy_kernel(mine, other, out, kept):
    frame = mine[pl.ds(ZROWS, TGT), :] + swap_z(other[pl.ds(ZROWS, TGT), :], 0)
    if kept.shape[0] > TGT:
        at = pl.ds(ZROWS + TGT, 8)
        frame = jnp.concatenate([frame, mine[at, :] + swap_z(other[at, :], 1)], axis=0)
    kept[...] = frame
    send("gy", 4, frame, out)


def spread_x_kernel(held, came, out, kept):
    frame = received("gy", 4, held[...], came)
    kept[...] = frame
    send("gx", 12, frame, out)


def spread_call(kernel, rows, *arrays):
    return pl.pallas_call(
        kernel,
        out_shape=[
            jax.ShapeDtypeStruct((8, rows - TGT + PACK, LANES), F32),
            jax.ShapeDtypeStruct((rows, LANES), F32),
        ],
        in_specs=vmem_specs(len(arrays)),
        out_specs=vmem_specs(2),
        compiler_params=PARAMS,
        name="spread",
    )(*arrays)


def step_kernel(first_step, last_step, *refs):
    count = 10 if first_step else 12
    field, faces, x_left, x_right, y_left, y_right, potential, kept, came, mat = refs[:10]
    if not first_step:
        previous, coupling = refs[10:12]
    refs = refs[count:]
    if last_step:
        (new, gram), refs = refs[:2], refs[2:]
    else:
        (new, x_low, x_high, y_low, y_high, message), refs = refs[:6], refs[6:]
        if first_step:
            coupling, refs = refs[0], refs[1:]
    total, coef, first_z, second_z = refs
    alpha = (1.0 if first_step else 2.0) / FILTER_HALF
    half = [0.0] + [-0.5 * c for c in STENCIL[1:]]
    diagonal = -1.5 * STENCIL[0] - FILTER_CENTRE
    write_z_matrices(first_z, second_z)

    def at(x, y):
        if x < 0:
            return x_left[(x + REACH) * SY + y]
        if x >= SX:
            return x_right[(x - SX) * SY + y]
        if y < 0:
            return y_left[x, y + REACH]
        if y >= SY:
            return y_right[x, y - SY]
        return field[x * SY + y]

    for g in range(GROUPS):
        rows = [field[4 * g + i] for i in range(4)]
        hi, lo = split2(jnp.concatenate(rows, axis=0))
        face = faces[pl.ds(g * 16, 16), :]
        face_hi = face.astype(BF16).astype(F32)
        side = jnp.concatenate(
            [face_hi, face - face_hi, face_hi, jnp.zeros((LANES - 48, LANES), F32)], axis=0
        ).T.astype(BF16)
        along_z = dot(jnp.concatenate([hi, lo], axis=1), first_z[...]) + dot(
            jnp.concatenate([hi, side], axis=1), second_z[...]
        )
        for i in range(4):
            x, y = divmod(4 * g + i, SY)
            summed = along_z[i * NB : (i + 1) * NB]
            for m in range(1, REACH + 1):
                around = (at(x + m, y) + at(x - m, y)) + (at(x, y + m) + at(x, y - m))
                summed = summed + half[m] * around
            summed = summed + (potential[pl.ds(4 * g + i, 1), :] + diagonal) * rows[i]
            result = alpha * summed
            if not first_step:
                result = result - previous[4 * g + i]
            new[4 * g + i] = result

    total[...] = jnp.zeros_like(total)
    frame = received("gx", 12, kept[...], came)
    if first_step:
        by_channel = jnp.concatenate([frame[TGT:], jnp.zeros((LANES - 8, LANES), F32)], axis=0).T
        columns = [jnp.broadcast_to(by_channel[:TGT, j : j + 1], (TGT, NB)) for j in range(NPJ)]
        coupling[...] = jnp.concatenate(columns, axis=1)
        frame = frame[:TGT]
    frame = frame * (alpha * coupling[...])
    stacked = jnp.concatenate([frame[:, j * NB : (j + 1) * NB] for j in range(NPJ)], axis=0)
    turned = stacked.T
    coef[...] = jnp.concatenate(split2(turned), axis=0)

    c_both = coef[...]
    for x in range(SX):
        acc = total[...]
        rows = []
        for p in range(4):
            pair_mat = mat[x * 4 + p]
            both = dot(c_both, pair_mat[:CH])
            added = both[:NB] + both[NB:] + dot(c_both[:NB], pair_mat[CH:])
            for q in range(2):
                here = x * SY + 2 * p + q
                rows.append(new[here] + added[:, q * SZ : (q + 1) * SZ])
                new[here] = rows[-1]
        if not last_step:
            write_x_faces(x, rows, x_low, x_high)
            write_y_faces(x, rows, y_low, y_high)
        for p in range(4):
            values = jnp.concatenate(rows[2 * p : 2 * p + 2], axis=1)
            if last_step:
                joined = jnp.concatenate(split3(values), axis=0)
                acc = acc + dot(joined, joined, NT)
            else:
                acc = acc + partial_of(mat[x * 4 + p], values)
        total[...] = acc
        if not last_step:
            for part in range(2):
                message[pl.ds((2 * x + part) * 16, 16), :] = z_faces(rows[4 * part : 4 * part + 4])

    if last_step:
        t = total[...]
        summed = t[2 * NB :, :NB] + t[:NB, 2 * NB :] + t[NB : 2 * NB, NB : 2 * NB]
        summed = summed + (t[NB : 2 * NB, :NB] + t[:NB, NB : 2 * NB]) + t[:NB, :NB]
        gram[...] = jnp.concatenate([summed[8 * q : 8 * q + 8] for q in range(4)], axis=1)
    else:
        message[pl.ds(ZROWS, TGT), :] = packed_partial(total[...])


def step(first_step, last_step, *arrays):
    total = (3 * NB, 3 * NB) if last_step else TOTAL
    if last_step:
        outs = [BLOCK, jax.ShapeDtypeStruct((8, LANES), F32)]
    else:
        outs = [BLOCK, X_FACE, X_FACE, Y_FACE, Y_FACE, MESSAGE] + ([FRAME] if first_step else [])
    return pl.pallas_call(
        functools.partial(step_kernel, first_step, last_step),
        out_shape=outs,
        in_specs=vmem_specs(len(arrays)),
        out_specs=vmem_specs(len(outs)),
        scratch_shapes=[
            pltpu.VMEM(total, F32),
            pltpu.VMEM((2 * NB, CH), BF16),
            pltpu.VMEM((2 * SZ, SZ), BF16),
            pltpu.VMEM((2 * SZ, SZ), BF16),
        ],
        compiler_params=PARAMS,
        name="step",
    )(*arrays)


def finish_kernel(scale, field, grams, out, made, inverse, out_sem):
    packed = grams[0]
    for slot in range(1, grams.shape[0]):
        packed = packed + grams[slot]
    packed = packed * scale
    gram = jnp.concatenate([packed[:, q * NB : (q + 1) * NB] for q in range(4)], axis=0)
    row = lax.broadcasted_iota(jnp.int32, (NB, NB), 0)
    column = lax.broadcasted_iota(jnp.int32, (NB, NB), 1)
    eye = jnp.where(row == column, 1.0, 0.0)
    work = jnp.concatenate([gram, eye], axis=1)
    below = lax.broadcasted_iota(jnp.int32, (NB, 2 * NB), 0)
    for k in range(NB):
        root = lax.rsqrt(work[k : k + 1, k : k + 1])
        line = work[k : k + 1, :] * root
        inverse[pl.ds(k, 1), :] = line[:, NB:]
        if k < NB - 1:
            factor = work[:, k : k + 1] * root
            work = work - jnp.where(below > k, factor * line, 0.0)
    hi, mid, lo = split3(inverse[...])
    left = jnp.concatenate([lo, mid, hi, mid, hi, hi], axis=1)

    for x in range(SX):
        for p in range(SY // 2):
            at = x * SY + 2 * p
            values = jnp.concatenate([field[at], field[at + 1]], axis=1)
            f_hi, f_mid, f_lo = split3(values)
            right = jnp.concatenate([f_hi, f_mid, f_lo, f_hi, f_mid, f_hi], axis=0)
            result = dot(left, right)
            made[at] = result[:, :SZ]
            made[at + 1] = result[:, SZ:]
            for q in range(2):
                pltpu.make_async_copy(made.at[at + q], out.at[:, at + q, :], out_sem.at[at + q]).start()

    for r in range(ROWS):
        pltpu.make_async_copy(made.at[r], out.at[:, r, :], out_sem.at[r]).wait()


def finish(scale, field, grams):
    return pl.pallas_call(
        functools.partial(finish_kernel, scale),
        out_shape=jax.ShapeDtypeStruct((NB, ROWS, SZ), F32),
        in_specs=vmem_specs(2),
        out_specs=pl.BlockSpec(memory_space=pl.ANY),
        scratch_shapes=[
            pltpu.VMEM((ROWS, NB, SZ), F32),
            pltpu.VMEM((NB, NB), F32),
            pltpu.SemaphoreType.DMA((ROWS,)),
        ],
        compiler_params=PARAMS,
        name="finish",
    )(field, grams)


def shift(value, axis, by):
    count = lax.axis_size(axis)
    return lax.ppermute(value, axis, [(i, (i + by) % count) for i in range(count)])


def local(orbitals, potential, projector, point_cell, target, point_count, coupling):
    bands, size_x, size_y, size_z = orbitals.shape
    field, key, own, *weights = prepare(
        point_count.reshape(1), coupling, orbitals.reshape(NB, ROWS, SZ), point_cell, target, projector
    )
    pot = potential.reshape(ROWS, SZ)
    key = key.reshape(SLOTS)
    starts = jnp.sum(
        (key[None, :] < (lax.iota(jnp.int32, ROWS + 1) * (SZ * 64))[:, None]).astype(jnp.int32), axis=1
    )
    ordered = lax.sort((key, *[w.reshape(SLOTS) for w in weights]), num_keys=1, is_stable=False)
    points = jnp.stack([ordered[0].astype(F32), *ordered[1:]])
    mat = build(starts, points)

    other = ()
    for k in range(DEGREE):
        start, last = k == 0, k == DEGREE - 1
        if start:
            message, x_low, x_high, y_low, y_high = first(field, mat, own)
        faces = shift(message, "gz", 1)
        y_left = shift(y_high, "gy", 1)
        y_right = shift(y_low, "gy", -1)
        faces, x_low, x_high = lax.optimization_barrier((faces, x_low, x_high))
        x_left = shift(x_high, "gx", 1)
        x_right = shift(x_low, "gx", -1)
        rows = message.shape[0] - ZROWS
        sends, kept = spread_call(spread_zy_kernel, rows, message, faces)
        came = lax.all_to_all(sends, "gy", 0, 0)
        sends, kept = spread_call(spread_x_kernel, rows, kept, came)
        came = lax.all_to_all(sends, "gx", 0, 0)
        outs = step(start, last, field, faces, x_left, x_right, y_left, y_right, pot, kept, came, mat, *other)
        previous = field
        if last:
            field, gram = outs
        else:
            field, x_low, x_high, y_low, y_high, message = outs[:6]
            if start:
                scales = outs[6]
            other = (previous, scales)
    axes = ("gx", "gy", "gz")
    devices = 1
    for axis in axes:
        devices *= lax.axis_size(axis)
    grams = lax.all_to_all(jnp.broadcast_to(gram[None], (devices,) + gram.shape), axes, 0, 0)
    result = finish(1.0 / float(devices * ROWS * SZ), field, grams)
    return result.reshape(bands, size_x, size_y, size_z)


def solution(mesh):
    in_specs = (
        P(None, "gx", "gy", "gz"),
        P("gx", "gy", "gz"),
        P(None, ("gx", "gy", "gz")),
        P(("gx", "gy", "gz")),
        P(("gx", "gy", "gz")),
        P("gx", "gy", "gz"),
        P(("gx", "gy", "gz"), None),
    )
    out_specs = P(None, "gx", "gy", "gz")
    return jax.shard_map(local, mesh=mesh, in_specs=in_specs, out_specs=out_specs, check_vma=False)
```

```python
import functools

import jax
import jax.numpy as jnp
from jax import lax
from jax.experimental import pallas as pl
from jax.experimental.pallas import tpu as pltpu
from jax.sharding import PartitionSpec as P

DEGREE = 4
STENCIL = (
    -5369.0 / 1800.0,
    12.0 / 7.0,
    -15.0 / 56.0,
    10.0 / 189.0,
    -1.0 / 112.0,
    2.0 / 1925.0,
    -1.0 / 16632.0,
)
FILTER_CENTRE = 9.5
FILTER_HALF = 5.5
REACH = 6

NB = 32
SX = 8
SY = 8
SZ = 128
ROWS = SX * SY
PAIRS = ROWS // 2
FACE = REACH * SY
NPJ = 4
SLOTS = 8192
TGT = 40
CH = NPJ * TGT
GROUPS = ROWS // 4
TOTAL = (NB, CH)
BATCH = 16
ZROWS = GROUPS * 16
PACK = 24
LANES = 128
LOWER = [(i, j) for i in range(4) for j in range(i + 1)]
F32 = jnp.float32
BF16 = jnp.bfloat16
NN = (((1,), (0,)), ((), ()))
NT = (((1,), (1,)), ((), ()))
VMEM_LIMIT = 16 * 1024 * 1024
PREPARE_LIMIT = 64256 * 1024


def dot(a, b, dims=NN):
    return lax.dot_general(a, b, dims, preferred_element_type=F32)


def split2(v):
    hi = v.astype(BF16)
    return hi, (v - hi.astype(F32)).astype(BF16)


def split3(v):
    hi = v.astype(BF16)
    rest = v - hi.astype(F32)
    mid = rest.astype(BF16)
    return hi, mid, (rest - mid.astype(F32)).astype(BF16)


def band(distance):
    found = jnp.zeros(distance.shape, F32)
    for m in range(1, REACH + 1):
        found = jnp.where(jnp.abs(distance) == m, -0.5 * STENCIL[m], found)
    return found


def write_z_matrices(first, second):
    source = lax.broadcasted_iota(jnp.int32, (SZ, SZ), 0)
    z = lax.broadcasted_iota(jnp.int32, (SZ, SZ), 1)
    inner_hi, inner_lo = split2(band(source - z))
    e = lax.broadcasted_iota(jnp.int32, (16, SZ), 0)
    z = lax.broadcasted_iota(jnp.int32, (16, SZ), 1)
    face_hi, face_lo = split2(band(jnp.where(e < 8, SZ + e - z, z + 16 - e)))
    first[...] = jnp.concatenate([inner_hi, inner_hi], axis=0)
    unused = jnp.zeros((SZ - 48, SZ), BF16)
    second[...] = jnp.concatenate([inner_lo, face_hi, face_hi, face_lo, unused], axis=0)


def any_specs(count):
    return [pl.BlockSpec(memory_space=pl.ANY)] * count


def vmem_specs(count):
    return [pl.BlockSpec(memory_space=pltpu.VMEM)] * count


PARAMS = pltpu.CompilerParams(vmem_limit_bytes=VMEM_LIMIT)


def z_faces(rows):
    turned = jnp.concatenate(rows, axis=0).T
    return jnp.concatenate([turned[:8], turned[SZ - 8 :]], axis=0)


BLOCK = jax.ShapeDtypeStruct((ROWS, NB, SZ), F32)
X_FACE = jax.ShapeDtypeStruct((FACE, NB, SZ), F32)
Y_FACE = jax.ShapeDtypeStruct((SX, REACH, NB, SZ), F32)
MESSAGE = jax.ShapeDtypeStruct((ZROWS + TGT, LANES), F32)
FRAME = jax.ShapeDtypeStruct((TGT, LANES), F32)
MATRIX = jax.ShapeDtypeStruct((PAIRS, 2 * CH, 2 * SZ), BF16)


def write_x_faces(x, rows, x_low, x_high):
    if x < REACH:
        for i in range(SY):
            x_low[x * SY + i] = rows[i]
    if x >= SX - REACH:
        for i in range(SY):
            x_high[(x - (SX - REACH)) * SY + i] = rows[i]


def write_y_faces(x, rows, y_low, y_high):
    for i in range(REACH):
        y_low[x, i] = rows[i]
        y_high[x, i] = rows[SY - REACH + i]


def prepare_kernel(count, coupling, src, cells, targets, projector, *refs):
    field, key, own = refs[:3]
    weights = refs[3 : 3 + NPJ]
    coupling_v, cells_v, targets_v, projector_v, in_sem, row_sem = refs[3 + NPJ :]
    pairs = ((cells, cells_v), (targets, targets_v), (projector, projector_v), (coupling, coupling_v))
    loads = [pltpu.make_async_copy(a, b, in_sem.at[i]) for i, (a, b) in enumerate(pairs)]
    rows = [pltpu.make_async_copy(src.at[:, row, :], field.at[row], row_sem.at[row]) for row in range(ROWS)]
    for load in loads + rows:
        load.start()
    for load in loads:
        load.wait()
    slot = lax.broadcasted_iota(jnp.int32, (SLOTS // LANES, LANES), 0) * LANES
    slot = slot + lax.broadcasted_iota(jnp.int32, (SLOTS // LANES, LANES), 1)
    target = targets_v[...]
    code = target // 2
    z_other = jnp.where(code % 3 != 1, 1, 0)
    wanted = ((code // 3) * 2 + z_other) * 2 + target % 2
    key[...] = jnp.where(slot < count[0], cells_v[...] * 64 + wanted, ROWS * SZ * 64)
    for j in range(NPJ):
        for i in range(SLOTS // LANES):
            weights[j][pl.ds(i, 1), :] = projector_v[pl.ds(j, 1), pl.ds(i * LANES, LANES)]
    channel = lax.broadcasted_iota(jnp.int32, (8, LANES), 0)
    at = lax.broadcasted_iota(jnp.int32, (8, LANES), 1)
    placed = jnp.zeros((8, LANES), F32)
    for a in range(2):
        for j in range(NPJ):
            value = jnp.broadcast_to(coupling_v[a : a + 1, j : j + 1], (8, LANES))
            placed = jnp.where((channel == j) & (at == 16 + a), value, placed)
    own[...] = placed
    for row in rows:
        row.wait()


def prepare(count, coupling, orbitals, cells, targets, projector):
    lines = (SLOTS // LANES, LANES)
    return pl.pallas_call(
        prepare_kernel,
        out_shape=[BLOCK, jax.ShapeDtypeStruct(lines, jnp.int32), jax.ShapeDtypeStruct((8, LANES), F32)]
        + [jax.ShapeDtypeStruct(lines, F32)] * NPJ,
        in_specs=[pl.BlockSpec(memory_space=pltpu.SMEM)] + any_specs(5),
        out_specs=vmem_specs(3 + NPJ),
        scratch_shapes=[
            pltpu.VMEM(coupling.shape, F32),
            pltpu.VMEM(lines, jnp.int32),
            pltpu.VMEM(lines, jnp.int32),
            pltpu.VMEM(projector.shape, F32),
            pltpu.SemaphoreType.DMA((4,)),
            pltpu.SemaphoreType.DMA((ROWS,)),
        ],
        compiler_params=pltpu.CompilerParams(vmem_limit_bytes=PREPARE_LIMIT),
        name="prepare",
    )(count, coupling, orbitals, cells.reshape(lines), targets.reshape(lines), projector)


def build_kernel(starts, points, out, held, sem):
    load = pltpu.make_async_copy(points, held.at[:, pl.ds(0, SLOTS)], sem)
    load.start()
    row = lax.broadcasted_iota(jnp.int32, (1 + NPJ, 2 * LANES), 0)
    load.wait()
    held[:, pl.ds(SLOTS, 2 * LANES)] = jnp.where(row == 0, float(ROWS * SZ * 64), 0.0)
    target_at = lax.broadcasted_iota(jnp.int32, (TGT, 2 * LANES), 0)
    z_at = lax.broadcasted_iota(jnp.int32, (SZ, 2 * LANES), 0)

    def window(row, block):
        seen = held[:, pl.ds(pl.multiple_of(block * LANES, LANES), 2 * LANES)]
        key = seen[:1].astype(jnp.int32)
        target = jnp.where((key >> 13) == row, key & 63, 63)
        chosen = target_at == target
        parts = []
        for j in range(NPJ):
            parts.append(jnp.where(chosen, seen[1 + j : 2 + j], 0.0))
        hi, lo = split2(jnp.concatenate(parts, axis=0))
        place = jnp.where(z_at == ((key >> 6) & 127), 1.0, 0.0).astype(BF16)
        both = dot(jnp.concatenate([hi, lo], axis=0), place, NT)
        return both[:CH] + both[CH:]

    @pl.loop(0, ROWS // BATCH)
    def _(step):
        first_row = step * BATCH
        bases = [starts[first_row + i] // LANES for i in range(BATCH)]
        for i in range(BATCH):
            hi, lo = split2(window(first_row + i, bases[i]))
            at = (step * (BATCH // 2) + i // 2, slice(None), pl.ds((i % 2) * SZ, SZ))
            out[at] = jnp.concatenate([hi, lo], axis=0)

        for i in range(BATCH):
            row = first_row + i
            windows = (starts[row + 1] - bases[i] * LANES + 2 * LANES - 1) // (2 * LANES)

            @pl.when(windows > 1)
            def _():
                total = lax.fori_loop(
                    0,
                    windows,
                    lambda k, acc: acc + window(row, bases[i] + 2 * k),
                    jnp.zeros((CH, SZ), F32),
                )
                hi, lo = split2(total)
                at = (step * (BATCH // 2) + i // 2, slice(None), pl.ds((i % 2) * SZ, SZ))
                out[at] = jnp.concatenate([hi, lo], axis=0)


def build(starts, points):
    return pl.pallas_call(
        build_kernel,
        out_shape=MATRIX,
        in_specs=[pl.BlockSpec(memory_space=pltpu.SMEM)] + any_specs(1),
        out_specs=pl.BlockSpec(memory_space=pltpu.VMEM),
        scratch_shapes=[
            pltpu.VMEM((1 + NPJ, SLOTS + 2 * LANES), F32),
            pltpu.SemaphoreType.DMA(()),
        ],
        compiler_params=PARAMS,
        name="build",
    )(starts, points)


def partial_of(mat, values):
    hi, lo = split2(values)
    both = dot(jnp.concatenate([hi, lo], axis=0), mat[:CH], NT)
    return both[:NB] + both[NB:] + dot(hi, mat[CH:], NT)


def packed_partial(total):
    joined = total.T
    return jnp.concatenate([joined[j * TGT : (j + 1) * TGT] for j in range(NPJ)], axis=1)


def first_kernel(field, mat, own, out, x_low, x_high, y_low, y_high, total):
    for g in range(GROUPS):
        out[pl.ds(16 * g, 16), :] = z_faces([field[4 * g + i] for i in range(4)])
    for x in range(SX):
        rows = [field[x * SY + y] for y in range(SY)]
        write_x_faces(x, rows, x_low, x_high)
        write_y_faces(x, rows, y_low, y_high)
    total[...] = jnp.zeros_like(total)
    for pair in range(PAIRS):
        values = jnp.concatenate([field[2 * pair], field[2 * pair + 1]], axis=1)
        total[...] = total[...] + partial_of(mat[pair], values)
    out[pl.ds(ZROWS, TGT), :] = packed_partial(total[...])
    out[pl.ds(ZROWS + TGT, 8), :] = own[...]


def first(field, mat, own):
    return pl.pallas_call(
        first_kernel,
        out_shape=[jax.ShapeDtypeStruct((ZROWS + TGT + 8, LANES), F32), X_FACE, X_FACE, Y_FACE, Y_FACE],
        in_specs=vmem_specs(3),
        out_specs=vmem_specs(5),
        scratch_shapes=[pltpu.VMEM(TOTAL, F32)],
        compiler_params=PARAMS,
        name="first",
    )(field, mat, own)


def neighbours(axis):
    me = lax.axis_index(axis)
    return [(d, (me + d + 8) % 8, (me - d + 8) % 8) for d in (-2, -1, 1, 2)]


def packed(frame, stride, d):
    found = []
    for start in range(0, 36, 3 * stride):
        rows = frame[start : start + 3 * stride]
        gap = jnp.zeros((stride, LANES), F32)
        if d == 1:
            found.append(rows[stride:])
        elif d == -1:
            found.append(rows[: 2 * stride])
        elif d == 2:
            found += [rows[2 * stride :], gap]
        else:
            found += [gap, rows[:stride]]
    return jnp.concatenate(found, axis=0)


def shifted(frame, stride, d):
    target = lax.broadcasted_iota(jnp.int32, frame.shape, 1)
    digit = (target // stride) % 3
    valid = (digit + d >= 0) & (digit + d <= 2) & (target < 36)
    return jnp.where(valid, pltpu.roll(frame, (-stride * d) % LANES, 1), 0.0)


def send(axis, stride, frame, out):
    me = lax.axis_index(axis)
    for d in (-3, 0, 3, 4):
        out[(me + d + 8) % 8] = jnp.zeros(out.shape[1:], F32)
    for d, to, _ in neighbours(axis):
        out[to, pl.ds(0, PACK), :] = packed(frame[:TGT], stride, d)
        if frame.shape[0] > TGT:
            out[to, pl.ds(PACK, 8), :] = shifted(frame[TGT:], stride, d)


def received(axis, stride, frame, came):
    below = above = couplings = 0.0
    for d, _, source in neighbours(axis):
        block = came[source]
        if d > 0:
            below = below + block[:PACK]
        else:
            above = above + block[:PACK]
        if frame.shape[0] > TGT:
            couplings = couplings + block[PACK:]
    gap = jnp.zeros((stride, LANES), F32)
    first, last = [], []
    for start in range(0, PACK, 2 * stride):
        first += [below[start : start + 2 * stride], gap]
        last += [gap, above[start : start + 2 * stride]]
    rest = [jnp.zeros((TGT - 36, LANES), F32)]
    added = jnp.concatenate(first + rest, axis=0) + jnp.concatenate(last + rest, axis=0)
    if frame.shape[0] == TGT:
        return frame + added
    return frame + jnp.concatenate([added, couplings], axis=0)


def swap_z(theirs, along):
    target = lax.broadcasted_iota(jnp.int32, theirs.shape, along)
    up = pltpu.roll(theirs, theirs.shape[along] - 2, along)
    return jnp.where(target & 2 == 0, up, pltpu.roll(theirs, 2, along))


def spread_zy_kernel(mine, other, out, kept):
    frame = mine[pl.ds(ZROWS, TGT), :] + swap_z(other[pl.ds(ZROWS, TGT), :], 0)
    if kept.shape[0] > TGT:
        at = pl.ds(ZROWS + TGT, 8)
        frame = jnp.concatenate([frame, mine[at, :] + swap_z(other[at, :], 1)], axis=0)
    kept[...] = frame
    send("gy", 4, frame, out)


def spread_x_kernel(held, came, out, kept):
    frame = received("gy", 4, held[...], came)
    kept[...] = frame
    send("gx", 12, frame, out)


def spread_call(kernel, rows, *arrays):
    return pl.pallas_call(
        kernel,
        out_shape=[
            jax.ShapeDtypeStruct((8, rows - TGT + PACK, LANES), F32),
            jax.ShapeDtypeStruct((rows, LANES), F32),
        ],
        in_specs=vmem_specs(len(arrays)),
        out_specs=vmem_specs(2),
        compiler_params=PARAMS,
        name="spread",
    )(*arrays)


def step_kernel(first_step, last_step, *refs):
    count = 10 if first_step else 12
    field, faces, x_left, x_right, y_left, y_right, potential, kept, came, mat = refs[:10]
    if not first_step:
        previous, coupling = refs[10:12]
    refs = refs[count:]
    if last_step:
        (new, gram), refs = refs[:2], refs[2:]
    else:
        (new, x_low, x_high, y_low, y_high, message), refs = refs[:6], refs[6:]
        if first_step:
            coupling, refs = refs[0], refs[1:]
    total, coef, first_z, second_z = refs
    alpha = (1.0 if first_step else 2.0) / FILTER_HALF
    half = [0.0] + [-0.5 * c for c in STENCIL[1:]]
    diagonal = -1.5 * STENCIL[0] - FILTER_CENTRE
    write_z_matrices(first_z, second_z)

    def at(x, y):
        if x < 0:
            return x_left[(x + REACH) * SY + y]
        if x >= SX:
            return x_right[(x - SX) * SY + y]
        if y < 0:
            return y_left[x, y + REACH]
        if y >= SY:
            return y_right[x, y - SY]
        return field[x * SY + y]

    for g in range(GROUPS):
        rows = [field[4 * g + i] for i in range(4)]
        hi, lo = split2(jnp.concatenate(rows, axis=0))
        face = faces[pl.ds(g * 16, 16), :]
        face_hi = face.astype(BF16).astype(F32)
        side = jnp.concatenate(
            [face_hi, face - face_hi, face_hi, jnp.zeros((LANES - 48, LANES), F32)], axis=0
        ).T.astype(BF16)
        along_z = dot(jnp.concatenate([hi, lo], axis=1), first_z[...]) + dot(
            jnp.concatenate([hi, side], axis=1), second_z[...]
        )
        for i in range(4):
            x, y = divmod(4 * g + i, SY)
            summed = along_z[i * NB : (i + 1) * NB]
            for m in range(1, REACH + 1):
                around = (at(x + m, y) + at(x - m, y)) + (at(x, y + m) + at(x, y - m))
                summed = summed + half[m] * around
            summed = summed + (potential[pl.ds(4 * g + i, 1), :] + diagonal) * rows[i]
            result = alpha * summed
            if not first_step:
                result = result - previous[4 * g + i]
            new[4 * g + i] = result

    total[...] = jnp.zeros_like(total)
    frame = received("gx", 12, kept[...], came)
    if first_step:
        by_channel = jnp.concatenate([frame[TGT:], jnp.zeros((LANES - 8, LANES), F32)], axis=0).T
        columns = [jnp.broadcast_to(by_channel[:TGT, j : j + 1], (TGT, NB)) for j in range(NPJ)]
        coupling[...] = jnp.concatenate(columns, axis=1)
        frame = frame[:TGT]
    frame = frame * (alpha * coupling[...])
    stacked = jnp.concatenate([frame[:, j * NB : (j + 1) * NB] for j in range(NPJ)], axis=0)
    turned = stacked.T
    coef[...] = jnp.concatenate(split2(turned), axis=0)

    c_both = coef[...]
    for x in range(SX):
        acc = total[...]
        rows = []
        for p in range(4):
            pair_mat = mat[x * 4 + p]
            both = dot(c_both, pair_mat[:CH])
            added = both[:NB] + both[NB:] + dot(c_both[:NB], pair_mat[CH:])
            for q in range(2):
                here = x * SY + 2 * p + q
                rows.append(new[here] + added[:, q * SZ : (q + 1) * SZ])
                new[here] = rows[-1]
        if not last_step:
            write_x_faces(x, rows, x_low, x_high)
            write_y_faces(x, rows, y_low, y_high)
        for p in range(4):
            values = jnp.concatenate(rows[2 * p : 2 * p + 2], axis=1)
            if last_step:
                joined = jnp.concatenate(split3(values), axis=0)
                acc = acc + dot(joined, joined, NT)
            else:
                acc = acc + partial_of(mat[x * 4 + p], values)
        total[...] = acc
        if not last_step:
            for part in range(2):
                message[pl.ds((2 * x + part) * 16, 16), :] = z_faces(rows[4 * part : 4 * part + 4])

    if last_step:
        t = total[...]
        summed = t[2 * NB :, :NB] + t[:NB, 2 * NB :] + t[NB : 2 * NB, NB : 2 * NB]
        summed = summed + (t[NB : 2 * NB, :NB] + t[:NB, NB : 2 * NB]) + t[:NB, :NB]
        blocks = [summed[8 * i : 8 * i + 8, 8 * j : 8 * j + 8] for i, j in LOWER]
        blocks = jnp.concatenate(blocks, axis=1)
        for r in range(8):
            gram[:, pl.ds(r * 8 * len(LOWER), 8 * len(LOWER))] = blocks[r : r + 1]
    else:
        message[pl.ds(ZROWS, TGT), :] = packed_partial(total[...])


def step(first_step, last_step, *arrays):
    total = (3 * NB, 3 * NB) if last_step else TOTAL
    if last_step:
        outs = [BLOCK, jax.ShapeDtypeStruct((1, 64 * len(LOWER)), F32)]
    else:
        outs = [BLOCK, X_FACE, X_FACE, Y_FACE, Y_FACE, MESSAGE] + ([FRAME] if first_step else [])
    return pl.pallas_call(
        functools.partial(step_kernel, first_step, last_step),
        out_shape=outs,
        in_specs=vmem_specs(len(arrays)),
        out_specs=vmem_specs(len(outs)),
        scratch_shapes=[
            pltpu.VMEM(total, F32),
            pltpu.VMEM((2 * NB, CH), BF16),
            pltpu.VMEM((2 * SZ, SZ), BF16),
            pltpu.VMEM((2 * SZ, SZ), BF16),
        ],
        compiler_params=PARAMS,
        name="step",
    )(*arrays)


def finish_kernel(scale, field, grams, out, made, inverse, out_sem):
    packed = grams[0]
    for slot in range(1, grams.shape[0]):
        packed = packed + grams[slot]
    packed = packed * scale
    width = 8 * len(LOWER)
    blocks = jnp.concatenate([packed[:, r * width : (r + 1) * width] for r in range(8)], axis=0)
    lower = []
    for i in range(4):
        found = [blocks[:, 8 * b : 8 * b + 8] for b, (k, _) in enumerate(LOWER) if k == i]
        lower.append(jnp.concatenate(found + [jnp.zeros((8, NB - 8 * i - 8), F32)] * (i < 3), axis=1))
    lower = jnp.concatenate(lower, axis=0)
    row = lax.broadcasted_iota(jnp.int32, (NB, NB), 0)
    column = lax.broadcasted_iota(jnp.int32, (NB, NB), 1)
    gram = jnp.where(row // 8 >= column // 8, lower, lower.T)
    eye = jnp.where(row == column, 1.0, 0.0)
    work = jnp.concatenate([gram, eye], axis=1)
    below = lax.broadcasted_iota(jnp.int32, (NB, 2 * NB), 0)
    for k in range(NB):
        column = jnp.broadcast_to(work[:, k : k + 1], work.shape)
        root = lax.rsqrt(column[k : k + 1])
        line = work[k : k + 1] * root
        inverse[pl.ds(k, 1), :] = line[:, NB:]
        if k < NB - 1:
            work = work - jnp.where(below > k, column, 0.0) * (line * root)
    hi, mid, lo = split3(inverse[...])
    left = jnp.concatenate([lo, mid, hi, mid, hi, hi], axis=1)

    for x in range(SX):
        for p in range(SY // 2):
            at = x * SY + 2 * p
            values = jnp.concatenate([field[at], field[at + 1]], axis=1)
            f_hi, f_mid, f_lo = split3(values)
            right = jnp.concatenate([f_hi, f_mid, f_lo, f_hi, f_mid, f_hi], axis=0)
            result = dot(left, right)
            made[at] = result[:, :SZ]
            made[at + 1] = result[:, SZ:]
            for q in range(2):
                pltpu.make_async_copy(made.at[at + q], out.at[:, at + q, :], out_sem.at[at + q]).start()

    for r in range(ROWS):
        pltpu.make_async_copy(made.at[r], out.at[:, r, :], out_sem.at[r]).wait()


def finish(scale, field, grams):
    return pl.pallas_call(
        functools.partial(finish_kernel, scale),
        out_shape=jax.ShapeDtypeStruct((NB, ROWS, SZ), F32),
        in_specs=vmem_specs(2),
        out_specs=pl.BlockSpec(memory_space=pl.ANY),
        scratch_shapes=[
            pltpu.VMEM((ROWS, NB, SZ), F32),
            pltpu.VMEM((NB, NB), F32),
            pltpu.SemaphoreType.DMA((ROWS,)),
        ],
        compiler_params=PARAMS,
        name="finish",
    )(field, grams)


def shift(value, axis, by):
    count = lax.axis_size(axis)
    return lax.ppermute(value, axis, [(i, (i + by) % count) for i in range(count)])


def local(orbitals, potential, projector, point_cell, target, point_count, coupling):
    bands, size_x, size_y, size_z = orbitals.shape
    field, key, own, *weights = prepare(
        point_count.reshape(1), coupling, orbitals.reshape(NB, ROWS, SZ), point_cell, target, projector
    )
    pot = potential.reshape(ROWS, SZ)
    key = key.reshape(SLOTS)
    starts = jnp.sum(
        (key[None, :] < (lax.iota(jnp.int32, ROWS + 1) * (SZ * 64))[:, None]).astype(jnp.int32), axis=1
    )
    ordered = lax.sort((key, *[w.reshape(SLOTS) for w in weights]), num_keys=1, is_stable=False)
    points = jnp.stack([ordered[0].astype(F32), *ordered[1:]])
    mat = build(starts, points)

    other = ()
    for k in range(DEGREE):
        start, last = k == 0, k == DEGREE - 1
        if start:
            message, x_low, x_high, y_low, y_high = first(field, mat, own)
        faces = shift(message, "gz", 1)
        y_left = shift(y_high, "gy", 1)
        y_right = shift(y_low, "gy", -1)
        faces, x_low, x_high = lax.optimization_barrier((faces, x_low, x_high))
        x_left = shift(x_high, "gx", 1)
        x_right = shift(x_low, "gx", -1)
        rows = message.shape[0] - ZROWS
        sends, kept = spread_call(spread_zy_kernel, rows, message, faces)
        came = lax.all_to_all(sends, "gy", 0, 0)
        sends, kept = spread_call(spread_x_kernel, rows, kept, came)
        came = lax.all_to_all(sends, "gx", 0, 0)
        outs = step(start, last, field, faces, x_left, x_right, y_left, y_right, pot, kept, came, mat, *other)
        previous = field
        if last:
            field, gram = outs
        else:
            field, x_low, x_high, y_low, y_high, message = outs[:6]
            if start:
                scales = outs[6]
            other = (previous, scales)
    axes = ("gx", "gy", "gz")
    devices = 1
    for axis in axes:
        devices *= lax.axis_size(axis)
    grams = lax.all_to_all(jnp.broadcast_to(gram[None], (devices,) + gram.shape), axes, 0, 0)
    result = finish(1.0 / float(devices * ROWS * SZ), field, grams)
    return result.reshape(bands, size_x, size_y, size_z)


def solution(mesh):
    in_specs = (
        P(None, "gx", "gy", "gz"),
        P("gx", "gy", "gz"),
        P(None, ("gx", "gy", "gz")),
        P(("gx", "gy", "gz")),
        P(("gx", "gy", "gz")),
        P("gx", "gy", "gz"),
        P(("gx", "gy", "gz"), None),
    )
    out_specs = P(None, "gx", "gy", "gz")
    return jax.shard_map(local, mesh=mesh, in_specs=in_specs, out_specs=out_specs, check_vma=False)
```

```python
import functools

import jax
import jax.numpy as jnp
from jax import lax
from jax.experimental import pallas as pl
from jax.experimental.pallas import tpu as pltpu
from jax.sharding import PartitionSpec as P

DEGREE = 4
STENCIL = (
    -5369.0 / 1800.0,
    12.0 / 7.0,
    -15.0 / 56.0,
    10.0 / 189.0,
    -1.0 / 112.0,
    2.0 / 1925.0,
    -1.0 / 16632.0,
)
FILTER_CENTRE = 9.5
FILTER_HALF = 5.5
REACH = 6

NB = 32
SX = 8
SY = 8
SZ = 128
ROWS = SX * SY
PAIRS = ROWS // 2
FACE = REACH * SY
NPJ = 4
SLOTS = 8192
TGT = 40
CH = NPJ * TGT
GROUPS = ROWS // 4
TOTAL = (NB, CH)
BATCH = 16
EDGE = 2 * REACH
ZROWS = GROUPS * EDGE
PACK = 24
LANES = 128
LOWER = [(i, j) for i in range(4) for j in range(i + 1)]
F32 = jnp.float32
BF16 = jnp.bfloat16
NN = (((1,), (0,)), ((), ()))
NT = (((1,), (1,)), ((), ()))
VMEM_LIMIT = 16 * 1024 * 1024
PREPARE_LIMIT = 64256 * 1024


def dot(a, b, dims=NN):
    return lax.dot_general(a, b, dims, preferred_element_type=F32)


def split2(v):
    hi = v.astype(BF16)
    return hi, (v - hi.astype(F32)).astype(BF16)


def split3(v):
    hi = v.astype(BF16)
    rest = v - hi.astype(F32)
    mid = rest.astype(BF16)
    return hi, mid, (rest - mid.astype(F32)).astype(BF16)


def band(distance):
    found = jnp.zeros(distance.shape, F32)
    for m in range(1, REACH + 1):
        found = jnp.where(jnp.abs(distance) == m, -0.5 * STENCIL[m], found)
    return found


def write_z_matrices(first, second):
    source = lax.broadcasted_iota(jnp.int32, (SZ, SZ), 0)
    z = lax.broadcasted_iota(jnp.int32, (SZ, SZ), 1)
    inner_hi, inner_lo = split2(band(source - z))
    e = lax.broadcasted_iota(jnp.int32, (EDGE, SZ), 0)
    z = lax.broadcasted_iota(jnp.int32, (EDGE, SZ), 1)
    face = band(jnp.where(e < REACH, SZ + e - z, z + EDGE - e))
    face_hi = face.astype(BF16).astype(F32)
    first[...] = jnp.concatenate([inner_hi, inner_hi], axis=0)
    unused = jnp.zeros((SZ - 3 * EDGE, SZ), F32)
    sides = jnp.concatenate([face_hi, face_hi, face - face_hi, unused], axis=0).astype(BF16)
    second[...] = jnp.concatenate([inner_lo, sides], axis=0)


def any_specs(count):
    return [pl.BlockSpec(memory_space=pl.ANY)] * count


def vmem_specs(count):
    return [pl.BlockSpec(memory_space=pltpu.VMEM)] * count


PARAMS = pltpu.CompilerParams(vmem_limit_bytes=VMEM_LIMIT)


def z_faces(rows):
    turned = jnp.concatenate(rows, axis=0).T
    return jnp.concatenate([turned[:REACH], turned[SZ - REACH :]], axis=0)


BLOCK = jax.ShapeDtypeStruct((ROWS, NB, SZ), F32)
X_FACE = jax.ShapeDtypeStruct((FACE, NB, SZ), F32)
Y_FACE = jax.ShapeDtypeStruct((SX, REACH, NB, SZ), F32)
MESSAGE = jax.ShapeDtypeStruct((ZROWS + TGT, LANES), F32)
FRAME = jax.ShapeDtypeStruct((TGT, LANES), F32)
MATRIX = jax.ShapeDtypeStruct((PAIRS, 2 * CH, 2 * SZ), BF16)


def write_x_faces(x, rows, x_low, x_high):
    if x < REACH:
        for i in range(SY):
            x_low[x * SY + i] = rows[i]
    if x >= SX - REACH:
        for i in range(SY):
            x_high[(x - (SX - REACH)) * SY + i] = rows[i]


def write_y_faces(x, rows, y_low, y_high):
    for i in range(REACH):
        y_low[x, i] = rows[i]
        y_high[x, i] = rows[SY - REACH + i]


def prepare_kernel(count, coupling, src, cells, targets, projector, *refs):
    field, key, own = refs[:3]
    weights = refs[3 : 3 + NPJ]
    coupling_v, cells_v, targets_v, projector_v, in_sem, row_sem = refs[3 + NPJ :]
    pairs = ((cells, cells_v), (targets, targets_v), (projector, projector_v), (coupling, coupling_v))
    loads = [pltpu.make_async_copy(a, b, in_sem.at[i]) for i, (a, b) in enumerate(pairs)]
    rows = [pltpu.make_async_copy(src.at[:, row, :], field.at[row], row_sem.at[row]) for row in range(ROWS)]
    for load in loads + rows:
        load.start()
    for load in loads:
        load.wait()
    slot = lax.broadcasted_iota(jnp.int32, (SLOTS // LANES, LANES), 0) * LANES
    slot = slot + lax.broadcasted_iota(jnp.int32, (SLOTS // LANES, LANES), 1)
    target = targets_v[...]
    code = target // 2
    z_other = jnp.where(code % 3 != 1, 1, 0)
    wanted = ((code // 3) * 2 + z_other) * 2 + target % 2
    key[...] = jnp.where(slot < count[0], cells_v[...] * 64 + wanted, ROWS * SZ * 64)
    for j in range(NPJ):
        for i in range(SLOTS // LANES):
            weights[j][pl.ds(i, 1), :] = projector_v[pl.ds(j, 1), pl.ds(i * LANES, LANES)]
    channel = lax.broadcasted_iota(jnp.int32, (8, LANES), 0)
    at = lax.broadcasted_iota(jnp.int32, (8, LANES), 1)
    placed = jnp.zeros((8, LANES), F32)
    for a in range(2):
        for j in range(NPJ):
            value = jnp.broadcast_to(coupling_v[a : a + 1, j : j + 1], (8, LANES))
            placed = jnp.where((channel == j) & (at == 16 + a), value, placed)
    own[...] = placed
    for row in rows:
        row.wait()


def prepare(count, coupling, orbitals, cells, targets, projector):
    lines = (SLOTS // LANES, LANES)
    return pl.pallas_call(
        prepare_kernel,
        out_shape=[BLOCK, jax.ShapeDtypeStruct(lines, jnp.int32), jax.ShapeDtypeStruct((8, LANES), F32)]
        + [jax.ShapeDtypeStruct(lines, F32)] * NPJ,
        in_specs=[pl.BlockSpec(memory_space=pltpu.SMEM)] + any_specs(5),
        out_specs=vmem_specs(3 + NPJ),
        scratch_shapes=[
            pltpu.VMEM(coupling.shape, F32),
            pltpu.VMEM(lines, jnp.int32),
            pltpu.VMEM(lines, jnp.int32),
            pltpu.VMEM(projector.shape, F32),
            pltpu.SemaphoreType.DMA((4,)),
            pltpu.SemaphoreType.DMA((ROWS,)),
        ],
        compiler_params=pltpu.CompilerParams(vmem_limit_bytes=PREPARE_LIMIT),
        name="prepare",
    )(count, coupling, orbitals, cells.reshape(lines), targets.reshape(lines), projector)


def build_kernel(starts, points, out, held, sem):
    load = pltpu.make_async_copy(points, held.at[:, pl.ds(0, SLOTS)], sem)
    load.start()
    row = lax.broadcasted_iota(jnp.int32, (1 + NPJ, 2 * LANES), 0)
    load.wait()
    held[:, pl.ds(SLOTS, 2 * LANES)] = jnp.where(row == 0, float(ROWS * SZ * 64), 0.0)
    target_at = lax.broadcasted_iota(jnp.int32, (TGT, 2 * LANES), 0)
    z_at = lax.broadcasted_iota(jnp.int32, (SZ, 2 * LANES), 0)

    def window(row, block):
        seen = held[:, pl.ds(pl.multiple_of(block * LANES, LANES), 2 * LANES)]
        key = seen[:1].astype(jnp.int32)
        target = jnp.where((key >> 13) == row, key & 63, 63)
        chosen = target_at == target
        parts = []
        for j in range(NPJ):
            parts.append(jnp.where(chosen, seen[1 + j : 2 + j], 0.0))
        hi, lo = split2(jnp.concatenate(parts, axis=0))
        place = jnp.where(z_at == ((key >> 6) & 127), 1.0, 0.0).astype(BF16)
        both = dot(jnp.concatenate([hi, lo], axis=0), place, NT)
        return both[:CH] + both[CH:]

    @pl.loop(0, ROWS // BATCH)
    def _(step):
        first_row = step * BATCH
        bases = [starts[first_row + i] // LANES for i in range(BATCH)]
        for i in range(BATCH):
            hi, lo = split2(window(first_row + i, bases[i]))
            at = (step * (BATCH // 2) + i // 2, slice(None), pl.ds((i % 2) * SZ, SZ))
            out[at] = jnp.concatenate([hi, lo], axis=0)

        for i in range(BATCH):
            row = first_row + i
            windows = (starts[row + 1] - bases[i] * LANES + 2 * LANES - 1) // (2 * LANES)

            @pl.when(windows > 1)
            def _():
                at = (step * (BATCH // 2) + i // 2, slice(None), pl.ds((i % 2) * SZ, SZ))
                both = out[at].astype(F32)
                total = lax.fori_loop(
                    1,
                    windows,
                    lambda k, acc: acc + window(row, bases[i] + 2 * k),
                    both[:CH] + both[CH:],
                )
                hi, lo = split2(total)
                out[at] = jnp.concatenate([hi, lo], axis=0)


def build(starts, points):
    return pl.pallas_call(
        build_kernel,
        out_shape=MATRIX,
        in_specs=[pl.BlockSpec(memory_space=pltpu.SMEM)] + any_specs(1),
        out_specs=pl.BlockSpec(memory_space=pltpu.VMEM),
        scratch_shapes=[
            pltpu.VMEM((1 + NPJ, SLOTS + 2 * LANES), F32),
            pltpu.SemaphoreType.DMA(()),
        ],
        compiler_params=PARAMS,
        name="build",
    )(starts, points)


def partial_of(mat, values):
    hi, lo = split2(values)
    both = dot(jnp.concatenate([hi, lo], axis=0), mat[:CH], NT)
    return both[:NB] + both[NB:] + dot(hi, mat[CH:], NT)


def packed_partial(total):
    joined = total.T
    return jnp.concatenate([joined[j * TGT : (j + 1) * TGT] for j in range(NPJ)], axis=1)


def first_kernel(field, mat, own, out, x_low, x_high, y_low, y_high, total):
    for g in range(GROUPS):
        out[pl.ds(EDGE * g, EDGE), :] = z_faces([field[4 * g + i] for i in range(4)])
    for x in range(SX):
        rows = [field[x * SY + y] for y in range(SY)]
        write_x_faces(x, rows, x_low, x_high)
        write_y_faces(x, rows, y_low, y_high)
    total[...] = jnp.zeros_like(total)
    for pair in range(PAIRS):
        values = jnp.concatenate([field[2 * pair], field[2 * pair + 1]], axis=1)
        total[...] = total[...] + partial_of(mat[pair], values)
    out[pl.ds(ZROWS, TGT), :] = packed_partial(total[...])
    out[pl.ds(ZROWS + TGT, 8), :] = own[...]


def first(field, mat, own):
    return pl.pallas_call(
        first_kernel,
        out_shape=[jax.ShapeDtypeStruct((ZROWS + TGT + 8, LANES), F32), X_FACE, X_FACE, Y_FACE, Y_FACE],
        in_specs=vmem_specs(3),
        out_specs=vmem_specs(5),
        scratch_shapes=[pltpu.VMEM(TOTAL, F32)],
        compiler_params=PARAMS,
        name="first",
    )(field, mat, own)


def neighbours(axis):
    me = lax.axis_index(axis)
    return [(d, (me + d + 8) % 8, (me - d + 8) % 8) for d in (-2, -1, 1, 2)]


def packed(frame, stride, d):
    found = []
    for start in range(0, 36, 3 * stride):
        rows = frame[start : start + 3 * stride]
        gap = jnp.zeros((stride, LANES), F32)
        if d == 1:
            found.append(rows[stride:])
        elif d == -1:
            found.append(rows[: 2 * stride])
        elif d == 2:
            found += [rows[2 * stride :], gap]
        else:
            found += [gap, rows[:stride]]
    return jnp.concatenate(found, axis=0)


def shifted(frame, stride, d):
    target = lax.broadcasted_iota(jnp.int32, frame.shape, 1)
    digit = (target // stride) % 3
    valid = (digit + d >= 0) & (digit + d <= 2) & (target < 36)
    return jnp.where(valid, pltpu.roll(frame, (-stride * d) % LANES, 1), 0.0)


def send(axis, stride, frame, out):
    me = lax.axis_index(axis)
    for d in (-3, 0, 3, 4):
        out[(me + d + 8) % 8] = jnp.zeros(out.shape[1:], F32)
    for d, to, _ in neighbours(axis):
        out[to, pl.ds(0, PACK), :] = packed(frame[:TGT], stride, d)
        if frame.shape[0] > TGT:
            out[to, pl.ds(PACK, 8), :] = shifted(frame[TGT:], stride, d)


def received(axis, stride, frame, came):
    below = above = couplings = 0.0
    for d, _, source in neighbours(axis):
        block = came[source]
        if d > 0:
            below = below + block[:PACK]
        else:
            above = above + block[:PACK]
        if frame.shape[0] > TGT:
            couplings = couplings + block[PACK:]
    gap = jnp.zeros((stride, LANES), F32)
    first, last = [], []
    for start in range(0, PACK, 2 * stride):
        first += [below[start : start + 2 * stride], gap]
        last += [gap, above[start : start + 2 * stride]]
    rest = [jnp.zeros((TGT - 36, LANES), F32)]
    added = jnp.concatenate(first + rest, axis=0) + jnp.concatenate(last + rest, axis=0)
    if frame.shape[0] == TGT:
        return frame + added
    return frame + jnp.concatenate([added, couplings], axis=0)


def swap_z(theirs, along):
    target = lax.broadcasted_iota(jnp.int32, theirs.shape, along)
    up = pltpu.roll(theirs, theirs.shape[along] - 2, along)
    return jnp.where(target & 2 == 0, up, pltpu.roll(theirs, 2, along))


def spread_zy_kernel(mine, other, out, kept):
    frame = mine[pl.ds(ZROWS, TGT), :] + swap_z(other[pl.ds(ZROWS, TGT), :], 0)
    if kept.shape[0] > TGT:
        at = pl.ds(ZROWS + TGT, 8)
        frame = jnp.concatenate([frame, mine[at, :] + swap_z(other[at, :], 1)], axis=0)
    kept[...] = frame
    send("gy", 4, frame, out)


def spread_x_kernel(held, came, out, kept):
    frame = received("gy", 4, held[...], came)
    kept[...] = frame
    send("gx", 12, frame, out)


def spread_call(kernel, rows, *arrays):
    return pl.pallas_call(
        kernel,
        out_shape=[
            jax.ShapeDtypeStruct((8, rows - TGT + PACK, LANES), F32),
            jax.ShapeDtypeStruct((rows, LANES), F32),
        ],
        in_specs=vmem_specs(len(arrays)),
        out_specs=vmem_specs(2),
        compiler_params=PARAMS,
        name="spread",
    )(*arrays)


def step_kernel(first_step, last_step, *refs):
    count = 10 if first_step else 12
    field, faces, x_left, x_right, y_left, y_right, potential, kept, came, mat = refs[:10]
    if not first_step:
        previous, coupling = refs[10:12]
    refs = refs[count:]
    if last_step:
        (new, gram), refs = refs[:2], refs[2:]
    else:
        (new, x_low, x_high, y_low, y_high, message), refs = refs[:6], refs[6:]
        if first_step:
            coupling, refs = refs[0], refs[1:]
    total, coef, first_z, second_z = refs
    alpha = (1.0 if first_step else 2.0) / FILTER_HALF
    half = [0.0] + [-0.5 * c for c in STENCIL[1:]]
    diagonal = -1.5 * STENCIL[0] - FILTER_CENTRE
    write_z_matrices(first_z, second_z)

    def at(x, y):
        if x < 0:
            return x_left[(x + REACH) * SY + y]
        if x >= SX:
            return x_right[(x - SX) * SY + y]
        if y < 0:
            return y_left[x, y + REACH]
        if y >= SY:
            return y_right[x, y - SY]
        return field[x * SY + y]

    for g in range(GROUPS):
        rows = [field[4 * g + i] for i in range(4)]
        hi, lo = split2(jnp.concatenate(rows, axis=0))
        face = faces[pl.ds(g * EDGE, EDGE), :]
        face_hi = face.astype(BF16).astype(F32)
        side = jnp.concatenate(
            [face_hi, face - face_hi, face_hi, jnp.zeros((LANES - 3 * EDGE, LANES), F32)], axis=0
        ).T.astype(BF16)
        along_z = dot(jnp.concatenate([hi, lo], axis=1), first_z[...]) + dot(
            jnp.concatenate([hi, side], axis=1), second_z[...]
        )
        for i in range(4):
            x, y = divmod(4 * g + i, SY)
            summed = along_z[i * NB : (i + 1) * NB]
            for m in range(1, REACH + 1):
                around = (at(x + m, y) + at(x - m, y)) + (at(x, y + m) + at(x, y - m))
                summed = summed + half[m] * around
            summed = summed + (potential[pl.ds(4 * g + i, 1), :] + diagonal) * rows[i]
            result = alpha * summed
            if not first_step:
                result = result - previous[4 * g + i]
            new[4 * g + i] = result

    total[...] = jnp.zeros_like(total)
    frame = received("gx", 12, kept[...], came)
    if first_step:
        by_channel = jnp.concatenate([frame[TGT:], jnp.zeros((LANES - 8, LANES), F32)], axis=0).T
        columns = [jnp.broadcast_to(by_channel[:TGT, j : j + 1], (TGT, NB)) for j in range(NPJ)]
        coupling[...] = jnp.concatenate(columns, axis=1)
        frame = frame[:TGT]
    frame = frame * (alpha * coupling[...])
    stacked = jnp.concatenate([frame[:, j * NB : (j + 1) * NB] for j in range(NPJ)], axis=0)
    turned = stacked.T
    coef[...] = jnp.concatenate(split2(turned), axis=0)

    c_both = coef[...]
    for x in range(SX):
        acc = total[...]
        rows = []
        for p in range(4):
            pair_mat = mat[x * 4 + p]
            both = dot(c_both, pair_mat[:CH])
            added = both[:NB] + both[NB:] + dot(c_both[:NB], pair_mat[CH:])
            for q in range(2):
                here = x * SY + 2 * p + q
                rows.append(new[here] + added[:, q * SZ : (q + 1) * SZ])
                new[here] = rows[-1]
        if not last_step:
            write_x_faces(x, rows, x_low, x_high)
            write_y_faces(x, rows, y_low, y_high)
        for p in range(4):
            values = jnp.concatenate(rows[2 * p : 2 * p + 2], axis=1)
            if last_step:
                joined = jnp.concatenate(split3(values), axis=0)
                acc = acc + dot(joined, joined, NT)
            else:
                acc = acc + partial_of(mat[x * 4 + p], values)
        total[...] = acc
        if not last_step:
            for part in range(2):
                message[pl.ds((2 * x + part) * EDGE, EDGE), :] = z_faces(rows[4 * part : 4 * part + 4])

    if last_step:
        t = total[...]
        summed = t[2 * NB :, :NB] + t[:NB, 2 * NB :] + t[NB : 2 * NB, NB : 2 * NB]
        summed = summed + (t[NB : 2 * NB, :NB] + t[:NB, NB : 2 * NB]) + t[:NB, :NB]
        blocks = [summed[8 * i : 8 * i + 8, 8 * j : 8 * j + 8] for i, j in LOWER]
        blocks = jnp.concatenate(blocks, axis=1)
        for r in range(8):
            gram[:, pl.ds(r * 8 * len(LOWER), 8 * len(LOWER))] = blocks[r : r + 1]
    else:
        message[pl.ds(ZROWS, TGT), :] = packed_partial(total[...])


def step(first_step, last_step, *arrays):
    total = (3 * NB, 3 * NB) if last_step else TOTAL
    if last_step:
        outs = [BLOCK, jax.ShapeDtypeStruct((1, 64 * len(LOWER)), F32)]
    else:
        outs = [BLOCK, X_FACE, X_FACE, Y_FACE, Y_FACE, MESSAGE] + ([FRAME] if first_step else [])
    return pl.pallas_call(
        functools.partial(step_kernel, first_step, last_step),
        out_shape=outs,
        in_specs=vmem_specs(len(arrays)),
        out_specs=vmem_specs(len(outs)),
        scratch_shapes=[
            pltpu.VMEM(total, F32),
            pltpu.VMEM((2 * NB, CH), BF16),
            pltpu.VMEM((2 * SZ, SZ), BF16),
            pltpu.VMEM((2 * SZ, SZ), BF16),
        ],
        compiler_params=PARAMS,
        name="step",
    )(*arrays)


def finish_kernel(scale, field, grams, out, made, inverse, out_sem):
    packed = grams[0]
    for slot in range(1, grams.shape[0]):
        packed = packed + grams[slot]
    packed = packed * scale
    width = 8 * len(LOWER)
    blocks = jnp.concatenate([packed[:, r * width : (r + 1) * width] for r in range(8)], axis=0)
    lower = []
    for i in range(4):
        found = [blocks[:, 8 * b : 8 * b + 8] for b, (k, _) in enumerate(LOWER) if k == i]
        lower.append(jnp.concatenate(found + [jnp.zeros((8, NB - 8 * i - 8), F32)] * (i < 3), axis=1))
    lower = jnp.concatenate(lower, axis=0)
    row = lax.broadcasted_iota(jnp.int32, (NB, NB), 0)
    column = lax.broadcasted_iota(jnp.int32, (NB, NB), 1)
    gram = jnp.where(row // 8 >= column // 8, lower, lower.T)
    eye = jnp.where(row == column, 1.0, 0.0)
    work = jnp.concatenate([gram, eye], axis=1)
    below = lax.broadcasted_iota(jnp.int32, (NB, 2 * NB), 0)
    for k in range(0, NB, 2):
        left = jnp.broadcast_to(work[:, k : k + 1], work.shape)
        right = jnp.broadcast_to(work[:, k + 1 : k + 2], work.shape)
        root = lax.rsqrt(left[k : k + 1])
        beside = left[k + 1 : k + 2] * root
        next_root = lax.rsqrt(right[k + 1 : k + 2] - beside * beside)
        line = work[k : k + 1] * root
        next_line = (work[k + 1 : k + 2] - beside * line) * next_root
        inverse[pl.ds(k, 1), :] = line[:, NB:]
        inverse[pl.ds(k + 1, 1), :] = next_line[:, NB:]
        if k < NB - 2:
            factor = left * root
            next_factor = (right - factor * beside) * next_root
            work = work - jnp.where(below > k + 1, factor * line + next_factor * next_line, 0.0)
    hi, mid, lo = split3(inverse[...])
    left = jnp.concatenate([lo, mid, hi, mid, hi, hi], axis=1)

    for x in range(SX):
        for p in range(SY // 2):
            at = x * SY + 2 * p
            values = jnp.concatenate([field[at], field[at + 1]], axis=1)
            f_hi, f_mid, f_lo = split3(values)
            right = jnp.concatenate([f_hi, f_mid, f_lo, f_hi, f_mid, f_hi], axis=0)
            result = dot(left, right)
            made[at] = result[:, :SZ]
            made[at + 1] = result[:, SZ:]
            for q in range(2):
                pltpu.make_async_copy(made.at[at + q], out.at[:, at + q, :], out_sem.at[at + q]).start()

    for r in range(ROWS):
        pltpu.make_async_copy(made.at[r], out.at[:, r, :], out_sem.at[r]).wait()


def finish(scale, field, grams):
    return pl.pallas_call(
        functools.partial(finish_kernel, scale),
        out_shape=jax.ShapeDtypeStruct((NB, ROWS, SZ), F32),
        in_specs=vmem_specs(2),
        out_specs=pl.BlockSpec(memory_space=pl.ANY),
        scratch_shapes=[
            pltpu.VMEM((ROWS, NB, SZ), F32),
            pltpu.VMEM((NB, NB), F32),
            pltpu.SemaphoreType.DMA((ROWS,)),
        ],
        compiler_params=PARAMS,
        name="finish",
    )(field, grams)


def shift(value, axis, by):
    count = lax.axis_size(axis)
    return lax.ppermute(value, axis, [(i, (i + by) % count) for i in range(count)])


def local(orbitals, potential, projector, point_cell, target, point_count, coupling):
    bands, size_x, size_y, size_z = orbitals.shape
    field, key, own, *weights = prepare(
        point_count.reshape(1), coupling, orbitals.reshape(NB, ROWS, SZ), point_cell, target, projector
    )
    pot = potential.reshape(ROWS, SZ)
    key = key.reshape(SLOTS)
    starts = jnp.sum(
        (key[None, :] < (lax.iota(jnp.int32, ROWS + 1) * (SZ * 64))[:, None]).astype(jnp.int32), axis=1
    )
    ordered = lax.sort((key, *[w.reshape(SLOTS) for w in weights]), num_keys=1, is_stable=False)
    points = jnp.stack([ordered[0].astype(F32), *ordered[1:]])
    mat = build(starts, points)

    other = ()
    for k in range(DEGREE):
        start, last = k == 0, k == DEGREE - 1
        if start:
            message, x_low, x_high, y_low, y_high = first(field, mat, own)
        faces = shift(message, "gz", 1)
        y_left = shift(y_high, "gy", 1)
        y_right = shift(y_low, "gy", -1)
        faces, x_low, x_high = lax.optimization_barrier((faces, x_low, x_high))
        x_left = shift(x_high, "gx", 1)
        x_right = shift(x_low, "gx", -1)
        rows = message.shape[0] - ZROWS
        sends, kept = spread_call(spread_zy_kernel, rows, message, faces)
        came = lax.all_to_all(sends, "gy", 0, 0)
        sends, kept = spread_call(spread_x_kernel, rows, kept, came)
        came = lax.all_to_all(sends, "gx", 0, 0)
        outs = step(start, last, field, faces, x_left, x_right, y_left, y_right, pot, kept, came, mat, *other)
        previous = field
        if last:
            field, gram = outs
        else:
            field, x_low, x_high, y_low, y_high, message = outs[:6]
            if start:
                scales = outs[6]
            other = (previous, scales)
    axes = ("gx", "gy", "gz")
    devices = 1
    for axis in axes:
        devices *= lax.axis_size(axis)
    grams = lax.all_to_all(jnp.broadcast_to(gram[None], (devices,) + gram.shape), axes, 0, 0)
    result = finish(1.0 / float(devices * ROWS * SZ), field, grams)
    return result.reshape(bands, size_x, size_y, size_z)


def solution(mesh):
    in_specs = (
        P(None, "gx", "gy", "gz"),
        P("gx", "gy", "gz"),
        P(None, ("gx", "gy", "gz")),
        P(("gx", "gy", "gz")),
        P(("gx", "gy", "gz")),
        P("gx", "gy", "gz"),
        P(("gx", "gy", "gz"), None),
    )
    out_specs = P(None, "gx", "gy", "gz")
    return jax.shard_map(local, mesh=mesh, in_specs=in_specs, out_specs=out_specs, check_vma=False)
```

```python
import functools

import jax
import jax.numpy as jnp
from jax import lax
from jax.experimental import pallas as pl
from jax.experimental.pallas import tpu as pltpu
from jax.sharding import PartitionSpec as P

DEGREE = 4
STENCIL = (
    -5369.0 / 1800.0,
    12.0 / 7.0,
    -15.0 / 56.0,
    10.0 / 189.0,
    -1.0 / 112.0,
    2.0 / 1925.0,
    -1.0 / 16632.0,
)
FILTER_CENTRE = 9.5
FILTER_HALF = 5.5
REACH = 6

NB = 32
SX = 8
SY = 8
SZ = 128
ROWS = SX * SY
PAIRS = ROWS // 2
FACE = REACH * SY
NPJ = 4
SLOTS = 8192
TGT = 40
CH = NPJ * TGT
GROUPS = ROWS // 4
TOTAL = (NB, CH)
BATCH = 16
EDGE = 2 * REACH
ZROWS = GROUPS * EDGE
PACK = 24
LANES = 128
STRIP = 8
LOWER = [(i, j) for i in range(4) for j in range(i + 1)]
F32 = jnp.float32
BF16 = jnp.bfloat16
NN = (((1,), (0,)), ((), ()))
NT = (((1,), (1,)), ((), ()))
VMEM_LIMIT = 16 * 1024 * 1024
PREPARE_LIMIT = 64256 * 1024


def dot(a, b, dims=NN):
    return lax.dot_general(a, b, dims, preferred_element_type=F32)


def split2(v):
    hi = v.astype(BF16)
    return hi, (v - hi.astype(F32)).astype(BF16)


def split3(v):
    hi = v.astype(BF16)
    rest = v - hi.astype(F32)
    mid = rest.astype(BF16)
    return hi, mid, (rest - mid.astype(F32)).astype(BF16)


def band(distance):
    found = jnp.zeros(distance.shape, F32)
    for m in range(1, REACH + 1):
        found = jnp.where(jnp.abs(distance) == m, -0.5 * STENCIL[m], found)
    return found


def write_z_matrices(first, second):
    source = lax.broadcasted_iota(jnp.int32, (SZ, SZ), 0)
    z = lax.broadcasted_iota(jnp.int32, (SZ, SZ), 1)
    inner_hi, inner_lo = split2(band(source - z))
    e = lax.broadcasted_iota(jnp.int32, (EDGE, SZ), 0)
    z = lax.broadcasted_iota(jnp.int32, (EDGE, SZ), 1)
    face = band(jnp.where(e < REACH, SZ + e - z, z + EDGE - e))
    face_hi = face.astype(BF16).astype(F32)
    first[...] = jnp.concatenate([inner_hi, inner_hi], axis=0)
    unused = jnp.zeros((SZ - 3 * EDGE, SZ), F32)
    sides = jnp.concatenate([face_hi, face_hi, face - face_hi, unused], axis=0).astype(BF16)
    second[...] = jnp.concatenate([inner_lo, sides], axis=0)


def any_specs(count):
    return [pl.BlockSpec(memory_space=pl.ANY)] * count


def vmem_specs(count):
    return [pl.BlockSpec(memory_space=pltpu.VMEM)] * count


PARAMS = pltpu.CompilerParams(vmem_limit_bytes=VMEM_LIMIT)


def z_faces(rows):
    turned = jnp.concatenate(rows, axis=0).T
    return jnp.concatenate([turned[:REACH], turned[SZ - REACH :]], axis=0)


BLOCK = jax.ShapeDtypeStruct((ROWS, NB, SZ), F32)
X_FACE = jax.ShapeDtypeStruct((FACE, NB, SZ), F32)
Y_FACE = jax.ShapeDtypeStruct((SX, REACH, NB, SZ), F32)
MESSAGE = jax.ShapeDtypeStruct((ZROWS + TGT, LANES), F32)
FRAME = jax.ShapeDtypeStruct((TGT, LANES), F32)
MATRIX = jax.ShapeDtypeStruct((PAIRS, 2 * CH, 2 * SZ), BF16)


def write_x_faces(x, rows, x_low, x_high):
    if x < REACH:
        for i in range(SY):
            x_low[x * SY + i] = rows[i]
    if x >= SX - REACH:
        for i in range(SY):
            x_high[(x - (SX - REACH)) * SY + i] = rows[i]


def write_y_faces(x, rows, y_low, y_high):
    for i in range(REACH):
        y_low[x, i] = rows[i]
        y_high[x, i] = rows[SY - REACH + i]


def prepare_kernel(count, coupling, src, cells, targets, projector, *refs):
    field, key, own = refs[:3]
    weights = refs[3 : 3 + NPJ]
    coupling_v, cells_v, targets_v, projector_v, in_sem, row_sem = refs[3 + NPJ :]
    pairs = ((cells, cells_v), (targets, targets_v), (projector, projector_v), (coupling, coupling_v))
    loads = [pltpu.make_async_copy(a, b, in_sem.at[i]) for i, (a, b) in enumerate(pairs)]
    rows = [pltpu.make_async_copy(src.at[:, row, :], field.at[row], row_sem.at[row]) for row in range(ROWS)]
    for load in loads + rows:
        load.start()
    for load in loads:
        load.wait()
    slot = lax.broadcasted_iota(jnp.int32, (SLOTS // LANES, LANES), 0) * LANES
    slot = slot + lax.broadcasted_iota(jnp.int32, (SLOTS // LANES, LANES), 1)
    target = targets_v[...]
    code = target // 2
    z_other = jnp.where(code % 3 != 1, 1, 0)
    wanted = ((code // 3) * 2 + z_other) * 2 + target % 2
    key[...] = jnp.where(slot < count[0], cells_v[...] * 64 + wanted, ROWS * SZ * 64)
    for j in range(NPJ):
        for i in range(SLOTS // LANES):
            weights[j][pl.ds(i, 1), :] = projector_v[pl.ds(j, 1), pl.ds(i * LANES, LANES)]
    channel = lax.broadcasted_iota(jnp.int32, (8, LANES), 0)
    at = lax.broadcasted_iota(jnp.int32, (8, LANES), 1)
    placed = jnp.zeros((8, LANES), F32)
    for a in range(2):
        for j in range(NPJ):
            value = jnp.broadcast_to(coupling_v[a : a + 1, j : j + 1], (8, LANES))
            placed = jnp.where((channel == j) & (at == 16 + a), value, placed)
    own[...] = placed
    for row in rows:
        row.wait()


def prepare(count, coupling, orbitals, cells, targets, projector):
    lines = (SLOTS // LANES, LANES)
    return pl.pallas_call(
        prepare_kernel,
        out_shape=[BLOCK, jax.ShapeDtypeStruct(lines, jnp.int32), jax.ShapeDtypeStruct((8, LANES), F32)]
        + [jax.ShapeDtypeStruct(lines, F32)] * NPJ,
        in_specs=[pl.BlockSpec(memory_space=pltpu.SMEM)] + any_specs(5),
        out_specs=vmem_specs(3 + NPJ),
        scratch_shapes=[
            pltpu.VMEM(coupling.shape, F32),
            pltpu.VMEM(lines, jnp.int32),
            pltpu.VMEM(lines, jnp.int32),
            pltpu.VMEM(projector.shape, F32),
            pltpu.SemaphoreType.DMA((4,)),
            pltpu.SemaphoreType.DMA((ROWS,)),
        ],
        compiler_params=pltpu.CompilerParams(vmem_limit_bytes=PREPARE_LIMIT),
        name="prepare",
    )(count, coupling, orbitals, cells.reshape(lines), targets.reshape(lines), projector)


def build_kernel(starts, points, out, held, sem):
    load = pltpu.make_async_copy(points, held.at[:, pl.ds(0, SLOTS)], sem)
    load.start()
    row = lax.broadcasted_iota(jnp.int32, (1 + NPJ, 2 * LANES), 0)
    load.wait()
    held[:, pl.ds(SLOTS, 2 * LANES)] = jnp.where(row == 0, float(ROWS * SZ * 64), 0.0)
    target_at = lax.broadcasted_iota(jnp.int32, (TGT, 2 * LANES), 0)
    z_at = lax.broadcasted_iota(jnp.int32, (SZ, 2 * LANES), 0)

    def window(row, block):
        seen = held[:, pl.ds(pl.multiple_of(block * LANES, LANES), 2 * LANES)]
        key = seen[:1].astype(jnp.int32)
        target = jnp.where((key >> 13) == row, key & 63, 63)
        chosen = target_at == target
        parts = []
        for j in range(NPJ):
            parts.append(jnp.where(chosen, seen[1 + j : 2 + j], 0.0))
        hi, lo = split2(jnp.concatenate(parts, axis=0))
        place = jnp.where(z_at == ((key >> 6) & 127), 1.0, 0.0).astype(BF16)
        both = dot(jnp.concatenate([hi, lo], axis=0), place, NT)
        return both[:CH] + both[CH:]

    @pl.loop(0, ROWS // BATCH)
    def _(step):
        first_row = step * BATCH
        bases = [starts[first_row + i] // LANES for i in range(BATCH)]
        for i in range(BATCH):
            hi, lo = split2(window(first_row + i, bases[i]))
            at = (step * (BATCH // 2) + i // 2, slice(None), pl.ds((i % 2) * SZ, SZ))
            out[at] = jnp.concatenate([hi, lo], axis=0)

        for i in range(BATCH):
            row = first_row + i
            windows = (starts[row + 1] - bases[i] * LANES + 2 * LANES - 1) // (2 * LANES)

            @pl.when(windows > 1)
            def _():
                at = (step * (BATCH // 2) + i // 2, slice(None), pl.ds((i % 2) * SZ, SZ))
                both = out[at].astype(F32)
                total = lax.fori_loop(
                    1,
                    windows,
                    lambda k, acc: acc + window(row, bases[i] + 2 * k),
                    both[:CH] + both[CH:],
                )
                hi, lo = split2(total)
                out[at] = jnp.concatenate([hi, lo], axis=0)


def build(starts, points):
    return pl.pallas_call(
        build_kernel,
        out_shape=MATRIX,
        in_specs=[pl.BlockSpec(memory_space=pltpu.SMEM)] + any_specs(1),
        out_specs=pl.BlockSpec(memory_space=pltpu.VMEM),
        scratch_shapes=[
            pltpu.VMEM((1 + NPJ, SLOTS + 2 * LANES), F32),
            pltpu.SemaphoreType.DMA(()),
        ],
        compiler_params=PARAMS,
        name="build",
    )(starts, points)


def partial_of(mat, values):
    hi, lo = split2(values)
    both = dot(jnp.concatenate([hi, lo], axis=0), mat[:CH], NT)
    return both[:NB] + both[NB:] + dot(hi, mat[CH:], NT)


def packed_partial(total):
    joined = total.T
    return jnp.concatenate([joined[j * TGT : (j + 1) * TGT] for j in range(NPJ)], axis=1)


def first_kernel(field, mat, own, out, x_low, x_high, y_low, y_high, total):
    for g in range(GROUPS):
        out[pl.ds(EDGE * g, EDGE), :] = z_faces([field[4 * g + i] for i in range(4)])
    for x in range(SX):
        rows = [field[x * SY + y] for y in range(SY)]
        write_x_faces(x, rows, x_low, x_high)
        write_y_faces(x, rows, y_low, y_high)
    total[...] = jnp.zeros_like(total)
    for pair in range(PAIRS):
        values = jnp.concatenate([field[2 * pair], field[2 * pair + 1]], axis=1)
        total[...] = total[...] + partial_of(mat[pair], values)
    out[pl.ds(ZROWS, TGT), :] = packed_partial(total[...])
    out[pl.ds(ZROWS + TGT, 8), :] = own[...]


def first(field, mat, own):
    return pl.pallas_call(
        first_kernel,
        out_shape=[jax.ShapeDtypeStruct((ZROWS + TGT + 8, LANES), F32), X_FACE, X_FACE, Y_FACE, Y_FACE],
        in_specs=vmem_specs(3),
        out_specs=vmem_specs(5),
        scratch_shapes=[pltpu.VMEM(TOTAL, F32)],
        compiler_params=PARAMS,
        name="first",
    )(field, mat, own)


def neighbours(axis):
    me = lax.axis_index(axis)
    return [(d, (me + d + 8) % 8, (me - d + 8) % 8) for d in (-2, -1, 1, 2)]


def packed(frame, stride, d):
    found = []
    for start in range(0, 36, 3 * stride):
        rows = frame[start : start + 3 * stride]
        gap = jnp.zeros((stride, LANES), F32)
        if d == 1:
            found.append(rows[stride:])
        elif d == -1:
            found.append(rows[: 2 * stride])
        elif d == 2:
            found += [rows[2 * stride :], gap]
        else:
            found += [gap, rows[:stride]]
    return jnp.concatenate(found, axis=0)


def shifted(frame, stride, d):
    target = lax.broadcasted_iota(jnp.int32, frame.shape, 1)
    digit = (target // stride) % 3
    valid = (digit + d >= 0) & (digit + d <= 2) & (target < 36)
    return jnp.where(valid, pltpu.roll(frame, (-stride * d) % LANES, 1), 0.0)


def send(axis, stride, frame, out):
    me = lax.axis_index(axis)
    for d in (-3, 0, 3, 4):
        out[(me + d + 8) % 8] = jnp.zeros(out.shape[1:], F32)
    for d, to, _ in neighbours(axis):
        out[to, pl.ds(0, PACK), :] = packed(frame[:TGT], stride, d)
        if frame.shape[0] > TGT:
            out[to, pl.ds(PACK, 8), :] = shifted(frame[TGT:], stride, d)


def received(axis, stride, frame, came):
    below = above = couplings = 0.0
    for d, _, source in neighbours(axis):
        block = came[source]
        if d > 0:
            below = below + block[:PACK]
        else:
            above = above + block[:PACK]
        if frame.shape[0] > TGT:
            couplings = couplings + block[PACK:]
    gap = jnp.zeros((stride, LANES), F32)
    first, last = [], []
    for start in range(0, PACK, 2 * stride):
        first += [below[start : start + 2 * stride], gap]
        last += [gap, above[start : start + 2 * stride]]
    rest = [jnp.zeros((TGT - 36, LANES), F32)]
    added = jnp.concatenate(first + rest, axis=0) + jnp.concatenate(last + rest, axis=0)
    if frame.shape[0] == TGT:
        return frame + added
    return frame + jnp.concatenate([added, couplings], axis=0)


def swap_z(theirs, along):
    target = lax.broadcasted_iota(jnp.int32, theirs.shape, along)
    up = pltpu.roll(theirs, theirs.shape[along] - 2, along)
    return jnp.where(target & 2 == 0, up, pltpu.roll(theirs, 2, along))


def spread_zy_kernel(mine, other, out, kept):
    frame = mine[pl.ds(ZROWS, TGT), :] + swap_z(other[pl.ds(ZROWS, TGT), :], 0)
    if kept.shape[0] > TGT:
        at = pl.ds(ZROWS + TGT, 8)
        frame = jnp.concatenate([frame, mine[at, :] + swap_z(other[at, :], 1)], axis=0)
    kept[...] = frame
    send("gy", 4, frame, out)


def spread_x_kernel(held, came, out, kept):
    frame = received("gy", 4, held[...], came)
    kept[...] = frame
    send("gx", 12, frame, out)


def spread_call(kernel, rows, *arrays):
    return pl.pallas_call(
        kernel,
        out_shape=[
            jax.ShapeDtypeStruct((8, rows - TGT + PACK, LANES), F32),
            jax.ShapeDtypeStruct((rows, LANES), F32),
        ],
        in_specs=vmem_specs(len(arrays)),
        out_specs=vmem_specs(2),
        compiler_params=PARAMS,
        name="spread",
    )(*arrays)


def step_kernel(first_step, last_step, *refs):
    count = 10 if first_step else 12
    field, faces, x_left, x_right, y_left, y_right, potential, kept, came, mat = refs[:10]
    if not first_step:
        previous, coupling = refs[10:12]
    refs = refs[count:]
    if last_step:
        (new, gram), refs = refs[:2], refs[2:]
    else:
        (new, x_low, x_high, y_low, y_high, message), refs = refs[:6], refs[6:]
        if first_step:
            coupling, refs = refs[0], refs[1:]
    total, coef, first_z, second_z = refs
    alpha = (1.0 if first_step else 2.0) / FILTER_HALF
    half = [0.0] + [-0.5 * c for c in STENCIL[1:]]
    diagonal = -1.5 * STENCIL[0] - FILTER_CENTRE
    write_z_matrices(first_z, second_z)

    def at(x, y, b):
        some = pl.ds(b, 8)
        if x < 0:
            return x_left[(x + REACH) * SY + y, some, :]
        if x >= SX:
            return x_right[(x - SX) * SY + y, some, :]
        if y < 0:
            return y_left[x, y + REACH, some, :]
        if y >= SY:
            return y_right[x, y - SY, some, :]
        return field[x * SY + y, some, :]

    for x in range(SX):
        along_z = []
        for g in (2 * x, 2 * x + 1):
            block = jnp.concatenate([field[4 * g + i] for i in range(4)], axis=0)
            hi, lo = split2(block)
            face = faces[pl.ds(g * EDGE, EDGE), :]
            face_hi = face.astype(BF16).astype(F32)
            side = jnp.concatenate(
                [face_hi, face - face_hi, face_hi, jnp.zeros((LANES - 3 * EDGE, LANES), F32)], axis=0
            ).T.astype(BF16)
            along_z.append(
                dot(jnp.concatenate([hi, lo], axis=1), first_z[...])
                + dot(jnp.concatenate([hi, side], axis=1), second_z[...])
            )
        for b in range(0, NB, 8):
            line = [at(x, y, b) for y in range(-REACH, SY + REACH)]
            for y in range(SY):
                part, i = divmod(y, 4)
                summed = along_z[part][i * NB + b : i * NB + b + 8]
                for m in range(1, REACH + 1):
                    around = (at(x + m, y, b) + at(x - m, y, b)) + (line[y + REACH + m] + line[y + REACH - m])
                    summed = summed + half[m] * around
                summed = summed + (potential[pl.ds(x * SY + y, 1), :] + diagonal) * line[y + REACH]
                result = alpha * summed
                if not first_step:
                    result = result - previous[x * SY + y, pl.ds(b, 8), :]
                new[x * SY + y, pl.ds(b, 8), :] = result

    total[...] = jnp.zeros_like(total)
    frame = received("gx", 12, kept[...], came)
    if first_step:
        by_channel = jnp.concatenate([frame[TGT:], jnp.zeros((LANES - 8, LANES), F32)], axis=0).T
        columns = [jnp.broadcast_to(by_channel[:TGT, j : j + 1], (TGT, NB)) for j in range(NPJ)]
        coupling[...] = jnp.concatenate(columns, axis=1)
        frame = frame[:TGT]
    frame = frame * (alpha * coupling[...])
    stacked = jnp.concatenate([frame[:, j * NB : (j + 1) * NB] for j in range(NPJ)], axis=0)
    turned = stacked.T
    coef[...] = jnp.concatenate(split2(turned), axis=0)

    c_both = coef[...]
    for x in range(SX):
        acc = total[...]
        rows = []
        for p in range(4):
            pair_mat = mat[x * 4 + p]
            both = dot(c_both, pair_mat[:CH])
            added = both[:NB] + both[NB:] + dot(c_both[:NB], pair_mat[CH:])
            for q in range(2):
                here = x * SY + 2 * p + q
                rows.append(new[here] + added[:, q * SZ : (q + 1) * SZ])
                new[here] = rows[-1]
        if not last_step:
            write_x_faces(x, rows, x_low, x_high)
            write_y_faces(x, rows, y_low, y_high)
        for p in range(4):
            values = jnp.concatenate(rows[2 * p : 2 * p + 2], axis=1)
            if last_step:
                joined = jnp.concatenate(split3(values), axis=0)
                acc = acc + dot(joined, joined, NT)
            else:
                acc = acc + partial_of(mat[x * 4 + p], values)
        total[...] = acc
        if not last_step:
            for part in range(2):
                message[pl.ds((2 * x + part) * EDGE, EDGE), :] = z_faces(rows[4 * part : 4 * part + 4])

    if last_step:
        t = total[...]
        summed = t[2 * NB :, :NB] + t[:NB, 2 * NB :] + t[NB : 2 * NB, NB : 2 * NB]
        summed = summed + (t[NB : 2 * NB, :NB] + t[:NB, NB : 2 * NB]) + t[:NB, :NB]
        blocks = [summed[8 * i : 8 * i + 8, 8 * j : 8 * j + 8] for i, j in LOWER]
        blocks = jnp.concatenate(blocks, axis=1)
        for r in range(8):
            gram[:, pl.ds(r * 8 * len(LOWER), 8 * len(LOWER))] = blocks[r : r + 1]
    else:
        message[pl.ds(ZROWS, TGT), :] = packed_partial(total[...])


def step(first_step, last_step, *arrays):
    total = (3 * NB, 3 * NB) if last_step else TOTAL
    if last_step:
        outs = [BLOCK, jax.ShapeDtypeStruct((1, 64 * len(LOWER)), F32)]
    else:
        outs = [BLOCK, X_FACE, X_FACE, Y_FACE, Y_FACE, MESSAGE] + ([FRAME] if first_step else [])
    return pl.pallas_call(
        functools.partial(step_kernel, first_step, last_step),
        out_shape=outs,
        in_specs=vmem_specs(len(arrays)),
        out_specs=vmem_specs(len(outs)),
        scratch_shapes=[
            pltpu.VMEM(total, F32),
            pltpu.VMEM((2 * NB, CH), BF16),
            pltpu.VMEM((2 * SZ, SZ), BF16),
            pltpu.VMEM((2 * SZ, SZ), BF16),
        ],
        compiler_params=PARAMS,
        name="step",
    )(*arrays)


def finish_kernel(scale, field, grams, out, made, inverse, out_sem):
    packed = grams[0]
    for slot in range(1, grams.shape[0]):
        packed = packed + grams[slot]
    packed = packed * scale
    width = 8 * len(LOWER)
    blocks = jnp.concatenate([packed[:, r * width : (r + 1) * width] for r in range(8)], axis=0)
    lower = []
    for i in range(4):
        found = [blocks[:, 8 * b : 8 * b + 8] for b, (k, _) in enumerate(LOWER) if k == i]
        lower.append(jnp.concatenate(found + [jnp.zeros((8, NB - 8 * i - 8), F32)] * (i < 3), axis=1))
    lower = jnp.concatenate(lower, axis=0)
    row = lax.broadcasted_iota(jnp.int32, (NB, NB), 0)
    column = lax.broadcasted_iota(jnp.int32, (NB, NB), 1)
    gram = jnp.where(row // 8 >= column // 8, lower, lower.T)
    eye = jnp.where(row == column, 1.0, 0.0)
    work = jnp.concatenate([gram, eye], axis=1)
    below = lax.broadcasted_iota(jnp.int32, (NB, 2 * NB), 0)
    for k in range(0, NB, STRIP):
        columns = [jnp.broadcast_to(work[:, k + i : k + i + 1], work.shape) for i in range(STRIP)]
        lines = [work[k + i : k + i + 1] for i in range(STRIP)]
        for i in range(STRIP):
            root = lax.rsqrt(columns[i][k + i : k + i + 1])
            columns[i] = columns[i] * root
            lines[i] = lines[i] * root
            inverse[pl.ds(k + i, 1), :] = lines[i][:, NB:]
            for j in range(i + 1, STRIP):
                beside = columns[i][k + j : k + j + 1]
                columns[j] = columns[j] - columns[i] * beside
                lines[j] = lines[j] - lines[i] * beside
        if k < NB - STRIP:
            removed = columns[0] * lines[0]
            for i in range(1, STRIP):
                removed = removed + columns[i] * lines[i]
            work = work - jnp.where(below >= k + STRIP, removed, 0.0)
    hi, mid, lo = split3(inverse[...])
    left = jnp.concatenate([lo, mid, hi, mid, hi, hi], axis=1)

    for x in range(SX):
        for p in range(SY // 2):
            at = x * SY + 2 * p
            values = jnp.concatenate([field[at], field[at + 1]], axis=1)
            f_hi, f_mid, f_lo = split3(values)
            right = jnp.concatenate([f_hi, f_mid, f_lo, f_hi, f_mid, f_hi], axis=0)
            result = dot(left, right)
            made[at] = result[:, :SZ]
            made[at + 1] = result[:, SZ:]
            for q in range(2):
                pltpu.make_async_copy(made.at[at + q], out.at[:, at + q, :], out_sem.at[at + q]).start()

    for r in range(ROWS):
        pltpu.make_async_copy(made.at[r], out.at[:, r, :], out_sem.at[r]).wait()


def finish(scale, field, grams):
    return pl.pallas_call(
        functools.partial(finish_kernel, scale),
        out_shape=jax.ShapeDtypeStruct((NB, ROWS, SZ), F32),
        in_specs=vmem_specs(2),
        out_specs=pl.BlockSpec(memory_space=pl.ANY),
        scratch_shapes=[
            pltpu.VMEM((ROWS, NB, SZ), F32),
            pltpu.VMEM((NB, NB), F32),
            pltpu.SemaphoreType.DMA((ROWS,)),
        ],
        compiler_params=PARAMS,
        name="finish",
    )(field, grams)


def shift(value, axis, by):
    count = lax.axis_size(axis)
    return lax.ppermute(value, axis, [(i, (i + by) % count) for i in range(count)])


def local(orbitals, potential, projector, point_cell, target, point_count, coupling):
    bands, size_x, size_y, size_z = orbitals.shape
    field, key, own, *weights = prepare(
        point_count.reshape(1), coupling, orbitals.reshape(NB, ROWS, SZ), point_cell, target, projector
    )
    pot = potential.reshape(ROWS, SZ)
    key = key.reshape(SLOTS)
    starts = jnp.sum(
        (key[None, :] < (lax.iota(jnp.int32, ROWS + 1) * (SZ * 64))[:, None]).astype(jnp.int32), axis=1
    )
    ordered = lax.sort((key, *[w.reshape(SLOTS) for w in weights]), num_keys=1, is_stable=False)
    points = jnp.stack([ordered[0].astype(F32), *ordered[1:]])
    mat = build(starts, points)

    other = ()
    for k in range(DEGREE):
        start, last = k == 0, k == DEGREE - 1
        if start:
            message, x_low, x_high, y_low, y_high = first(field, mat, own)
        faces = shift(message, "gz", 1)
        y_left = shift(y_high, "gy", 1)
        y_right = shift(y_low, "gy", -1)
        faces, x_low, x_high = lax.optimization_barrier((faces, x_low, x_high))
        x_left = shift(x_high, "gx", 1)
        x_right = shift(x_low, "gx", -1)
        rows = message.shape[0] - ZROWS
        sends, kept = spread_call(spread_zy_kernel, rows, message, faces)
        came = lax.all_to_all(sends, "gy", 0, 0)
        sends, kept = spread_call(spread_x_kernel, rows, kept, came)
        came = lax.all_to_all(sends, "gx", 0, 0)
        outs = step(start, last, field, faces, x_left, x_right, y_left, y_right, pot, kept, came, mat, *other)
        previous = field
        if last:
            field, gram = outs
        else:
            field, x_low, x_high, y_low, y_high, message = outs[:6]
            if start:
                scales = outs[6]
            other = (previous, scales)
    axes = ("gx", "gy", "gz")
    devices = 1
    for axis in axes:
        devices *= lax.axis_size(axis)
    grams = lax.all_to_all(jnp.broadcast_to(gram[None], (devices,) + gram.shape), axes, 0, 0)
    result = finish(1.0 / float(devices * ROWS * SZ), field, grams)
    return result.reshape(bands, size_x, size_y, size_z)


def solution(mesh):
    in_specs = (
        P(None, "gx", "gy", "gz"),
        P("gx", "gy", "gz"),
        P(None, ("gx", "gy", "gz")),
        P(("gx", "gy", "gz")),
        P(("gx", "gy", "gz")),
        P("gx", "gy", "gz"),
        P(("gx", "gy", "gz"), None),
    )
    out_specs = P(None, "gx", "gy", "gz")
    return jax.shard_map(local, mesh=mesh, in_specs=in_specs, out_specs=out_specs, check_vma=False)
```

```python
import functools

import jax
import jax.numpy as jnp
from jax import lax
from jax.experimental import pallas as pl
from jax.experimental.pallas import tpu as pltpu
from jax.sharding import PartitionSpec as P

DEGREE = 4
STENCIL = (
    -5369.0 / 1800.0,
    12.0 / 7.0,
    -15.0 / 56.0,
    10.0 / 189.0,
    -1.0 / 112.0,
    2.0 / 1925.0,
    -1.0 / 16632.0,
)
FILTER_CENTRE = 9.5
FILTER_HALF = 5.5
REACH = 6

NB = 32
SX = 8
SY = 8
SZ = 128
ROWS = SX * SY
PAIRS = ROWS // 2
FACE = REACH * SY
NPJ = 4
SLOTS = 8192
TGT = 40
CH = NPJ * TGT
GROUPS = ROWS // 4
TOTAL = (NB, CH)
BATCH = 16
EDGE = 2 * REACH
ZROWS = GROUPS * EDGE
PACK = 24
LANES = 128
STRIP = 8
LOWER = [(i, j) for i in range(4) for j in range(i + 1)]
F32 = jnp.float32
BF16 = jnp.bfloat16
NN = (((1,), (0,)), ((), ()))
NT = (((1,), (1,)), ((), ()))
VMEM_LIMIT = 16 * 1024 * 1024
PREPARE_LIMIT = 64256 * 1024


def dot(a, b, dims=NN):
    return lax.dot_general(a, b, dims, preferred_element_type=F32)


def split2(v):
    hi = v.astype(BF16)
    return hi, (v - hi.astype(F32)).astype(BF16)


def split3(v):
    hi = v.astype(BF16)
    rest = v - hi.astype(F32)
    mid = rest.astype(BF16)
    return hi, mid, (rest - mid.astype(F32)).astype(BF16)


def band(distance):
    found = jnp.zeros(distance.shape, F32)
    for m in range(1, REACH + 1):
        found = jnp.where(jnp.abs(distance) == m, -0.5 * STENCIL[m], found)
    return found


def write_z_matrices(first, second):
    source = lax.broadcasted_iota(jnp.int32, (SZ, SZ), 0)
    z = lax.broadcasted_iota(jnp.int32, (SZ, SZ), 1)
    inner_hi, inner_lo = split2(band(source - z))
    e = lax.broadcasted_iota(jnp.int32, (EDGE, SZ), 0)
    z = lax.broadcasted_iota(jnp.int32, (EDGE, SZ), 1)
    face = band(jnp.where(e < REACH, SZ + e - z, z + EDGE - e))
    face_hi = face.astype(BF16).astype(F32)
    first[...] = jnp.concatenate([inner_hi, inner_hi], axis=0)
    unused = jnp.zeros((SZ - 3 * EDGE, SZ), F32)
    sides = jnp.concatenate([face_hi, face_hi, face - face_hi, unused], axis=0).astype(BF16)
    second[...] = jnp.concatenate([inner_lo, sides], axis=0)


def any_specs(count):
    return [pl.BlockSpec(memory_space=pl.ANY)] * count


def vmem_specs(count):
    return [pl.BlockSpec(memory_space=pltpu.VMEM)] * count


PARAMS = pltpu.CompilerParams(vmem_limit_bytes=VMEM_LIMIT)


def z_faces(rows):
    turned = jnp.concatenate(rows, axis=0).T
    return jnp.concatenate([turned[:REACH], turned[SZ - REACH :]], axis=0)


BLOCK = jax.ShapeDtypeStruct((ROWS, NB, SZ), F32)
X_FACE = jax.ShapeDtypeStruct((FACE, NB, SZ), F32)
Y_FACE = jax.ShapeDtypeStruct((SX, REACH, NB, SZ), F32)
MESSAGE = jax.ShapeDtypeStruct((ZROWS + TGT, LANES), F32)
FRAME = jax.ShapeDtypeStruct((TGT, LANES), F32)
MATRIX = jax.ShapeDtypeStruct((PAIRS, 2 * CH, 2 * SZ), BF16)


def write_x_faces(x, rows, x_low, x_high):
    if x < REACH:
        for i in range(SY):
            x_low[x * SY + i] = rows[i]
    if x >= SX - REACH:
        for i in range(SY):
            x_high[(x - (SX - REACH)) * SY + i] = rows[i]


def write_y_faces(x, rows, y_low, y_high):
    for i in range(REACH):
        y_low[x, i] = rows[i]
        y_high[x, i] = rows[SY - REACH + i]


def prepare_kernel(count, coupling, src, cells, targets, projector, *refs):
    field, key, own = refs[:3]
    weights = refs[3 : 3 + NPJ]
    coupling_v, cells_v, targets_v, projector_v, in_sem, row_sem = refs[3 + NPJ :]
    pairs = ((cells, cells_v), (targets, targets_v), (projector, projector_v), (coupling, coupling_v))
    loads = [pltpu.make_async_copy(a, b, in_sem.at[i]) for i, (a, b) in enumerate(pairs)]
    rows = [pltpu.make_async_copy(src.at[:, row, :], field.at[row], row_sem.at[row]) for row in range(ROWS)]
    for load in loads + rows:
        load.start()
    for load in loads:
        load.wait()
    slot = lax.broadcasted_iota(jnp.int32, (SLOTS // LANES, LANES), 0) * LANES
    slot = slot + lax.broadcasted_iota(jnp.int32, (SLOTS // LANES, LANES), 1)
    target = targets_v[...]
    code = target // 2
    z_other = jnp.where(code % 3 != 1, 1, 0)
    wanted = ((code // 3) * 2 + z_other) * 2 + target % 2
    key[...] = jnp.where(slot < count[0], cells_v[...] * 64 + wanted, ROWS * SZ * 64)
    for j in range(NPJ):
        for i in range(SLOTS // LANES):
            weights[j][pl.ds(i, 1), :] = projector_v[pl.ds(j, 1), pl.ds(i * LANES, LANES)]
    channel = lax.broadcasted_iota(jnp.int32, (8, LANES), 0)
    at = lax.broadcasted_iota(jnp.int32, (8, LANES), 1)
    placed = jnp.zeros((8, LANES), F32)
    for a in range(2):
        for j in range(NPJ):
            value = jnp.broadcast_to(coupling_v[a : a + 1, j : j + 1], (8, LANES))
            placed = jnp.where((channel == j) & (at == 16 + a), value, placed)
    own[...] = placed
    for row in rows:
        row.wait()


def prepare(count, coupling, orbitals, cells, targets, projector):
    lines = (SLOTS // LANES, LANES)
    return pl.pallas_call(
        prepare_kernel,
        out_shape=[BLOCK, jax.ShapeDtypeStruct(lines, jnp.int32), jax.ShapeDtypeStruct((8, LANES), F32)]
        + [jax.ShapeDtypeStruct(lines, F32)] * NPJ,
        in_specs=[pl.BlockSpec(memory_space=pltpu.SMEM)] + any_specs(5),
        out_specs=vmem_specs(3 + NPJ),
        scratch_shapes=[
            pltpu.VMEM(coupling.shape, F32),
            pltpu.VMEM(lines, jnp.int32),
            pltpu.VMEM(lines, jnp.int32),
            pltpu.VMEM(projector.shape, F32),
            pltpu.SemaphoreType.DMA((4,)),
            pltpu.SemaphoreType.DMA((ROWS,)),
        ],
        compiler_params=pltpu.CompilerParams(vmem_limit_bytes=PREPARE_LIMIT),
        name="prepare",
    )(count, coupling, orbitals, cells.reshape(lines), targets.reshape(lines), projector)


def build_kernel(starts, points, out, held, sem):
    load = pltpu.make_async_copy(points, held.at[:, pl.ds(0, SLOTS)], sem)
    load.start()
    row = lax.broadcasted_iota(jnp.int32, (1 + NPJ, 2 * LANES), 0)
    load.wait()
    held[:, pl.ds(SLOTS, 2 * LANES)] = jnp.where(row == 0, float(ROWS * SZ * 64), 0.0)
    target_at = lax.broadcasted_iota(jnp.int32, (TGT, 2 * LANES), 0)
    z_at = lax.broadcasted_iota(jnp.int32, (SZ, 2 * LANES), 0)

    def window(row, block):
        seen = held[:, pl.ds(pl.multiple_of(block * LANES, LANES), 2 * LANES)]
        key = seen[:1].astype(jnp.int32)
        target = jnp.where((key >> 13) == row, key & 63, 63)
        chosen = target_at == target
        parts = []
        for j in range(NPJ):
            parts.append(jnp.where(chosen, seen[1 + j : 2 + j], 0.0))
        hi, lo = split2(jnp.concatenate(parts, axis=0))
        place = jnp.where(z_at == ((key >> 6) & 127), 1.0, 0.0).astype(BF16)
        both = dot(jnp.concatenate([hi, lo], axis=0), place, NT)
        return both[:CH] + both[CH:]

    @pl.loop(0, ROWS // BATCH)
    def _(step):
        first_row = step * BATCH
        bases = [starts[first_row + i] // LANES for i in range(BATCH)]
        for i in range(BATCH):
            hi, lo = split2(window(first_row + i, bases[i]))
            at = (step * (BATCH // 2) + i // 2, slice(None), pl.ds((i % 2) * SZ, SZ))
            out[at] = jnp.concatenate([hi, lo], axis=0)

        for i in range(BATCH):
            row = first_row + i
            windows = (starts[row + 1] - bases[i] * LANES + 2 * LANES - 1) // (2 * LANES)

            @pl.when(windows > 1)
            def _():
                at = (step * (BATCH // 2) + i // 2, slice(None), pl.ds((i % 2) * SZ, SZ))
                both = out[at].astype(F32)
                total = lax.fori_loop(
                    1,
                    windows,
                    lambda k, acc: acc + window(row, bases[i] + 2 * k),
                    both[:CH] + both[CH:],
                )
                hi, lo = split2(total)
                out[at] = jnp.concatenate([hi, lo], axis=0)


def build(starts, points):
    return pl.pallas_call(
        build_kernel,
        out_shape=MATRIX,
        in_specs=[pl.BlockSpec(memory_space=pltpu.SMEM)] + any_specs(1),
        out_specs=pl.BlockSpec(memory_space=pltpu.VMEM),
        scratch_shapes=[
            pltpu.VMEM((1 + NPJ, SLOTS + 2 * LANES), F32),
            pltpu.SemaphoreType.DMA(()),
        ],
        compiler_params=PARAMS,
        name="build",
    )(starts, points)


def partial_of(mat, values):
    hi, lo = split2(values)
    both = dot(jnp.concatenate([hi, lo], axis=0), mat[:CH], NT)
    return both[:NB] + both[NB:] + dot(hi, mat[CH:], NT)


def packed_partial(total):
    joined = total.T
    return jnp.concatenate([joined[j * TGT : (j + 1) * TGT] for j in range(NPJ)], axis=1)


def first_kernel(field, mat, own, out, x_low, x_high, y_low, y_high, total):
    for g in range(GROUPS):
        out[pl.ds(EDGE * g, EDGE), :] = z_faces([field[4 * g + i] for i in range(4)])
    for x in range(SX):
        rows = [field[x * SY + y] for y in range(SY)]
        write_x_faces(x, rows, x_low, x_high)
        write_y_faces(x, rows, y_low, y_high)
    total[...] = jnp.zeros_like(total)
    for pair in range(PAIRS):
        values = jnp.concatenate([field[2 * pair], field[2 * pair + 1]], axis=1)
        total[...] = total[...] + partial_of(mat[pair], values)
    out[pl.ds(ZROWS, TGT), :] = packed_partial(total[...])
    out[pl.ds(ZROWS + TGT, 8), :] = own[...]


def first(field, mat, own):
    return pl.pallas_call(
        first_kernel,
        out_shape=[jax.ShapeDtypeStruct((ZROWS + TGT + 8, LANES), F32), X_FACE, X_FACE, Y_FACE, Y_FACE],
        in_specs=vmem_specs(3),
        out_specs=vmem_specs(5),
        scratch_shapes=[pltpu.VMEM(TOTAL, F32)],
        compiler_params=PARAMS,
        name="first",
    )(field, mat, own)


def neighbours(axis):
    me = lax.axis_index(axis)
    return [(d, (me + d + 8) % 8, (me - d + 8) % 8) for d in (-2, -1, 1, 2)]


def packed(frame, stride, d):
    found = []
    for start in range(0, 36, 3 * stride):
        rows = frame[start : start + 3 * stride]
        gap = jnp.zeros((stride, LANES), F32)
        if d == 1:
            found.append(rows[stride:])
        elif d == -1:
            found.append(rows[: 2 * stride])
        elif d == 2:
            found += [rows[2 * stride :], gap]
        else:
            found += [gap, rows[:stride]]
    return jnp.concatenate(found, axis=0)


def shifted(frame, stride, d):
    target = lax.broadcasted_iota(jnp.int32, frame.shape, 1)
    digit = (target // stride) % 3
    valid = (digit + d >= 0) & (digit + d <= 2) & (target < 36)
    return jnp.where(valid, pltpu.roll(frame, (-stride * d) % LANES, 1), 0.0)


def send(axis, stride, frame, out):
    me = lax.axis_index(axis)
    for d in (-3, 0, 3, 4):
        out[(me + d + 8) % 8] = jnp.zeros(out.shape[1:], F32)
    for d, to, _ in neighbours(axis):
        out[to, pl.ds(0, PACK), :] = packed(frame[:TGT], stride, d)
        if frame.shape[0] > TGT:
            out[to, pl.ds(PACK, 8), :] = shifted(frame[TGT:], stride, d)


def received(axis, stride, frame, came):
    below = above = couplings = 0.0
    for d, _, source in neighbours(axis):
        block = came[source]
        if d > 0:
            below = below + block[:PACK]
        else:
            above = above + block[:PACK]
        if frame.shape[0] > TGT:
            couplings = couplings + block[PACK:]
    gap = jnp.zeros((stride, LANES), F32)
    first, last = [], []
    for start in range(0, PACK, 2 * stride):
        first += [below[start : start + 2 * stride], gap]
        last += [gap, above[start : start + 2 * stride]]
    rest = [jnp.zeros((TGT - 36, LANES), F32)]
    added = jnp.concatenate(first + rest, axis=0) + jnp.concatenate(last + rest, axis=0)
    if frame.shape[0] == TGT:
        return frame + added
    return frame + jnp.concatenate([added, couplings], axis=0)


def swap_z(theirs, along):
    target = lax.broadcasted_iota(jnp.int32, theirs.shape, along)
    up = pltpu.roll(theirs, theirs.shape[along] - 2, along)
    return jnp.where(target & 2 == 0, up, pltpu.roll(theirs, 2, along))


def spread_zy_kernel(mine, other, out, kept):
    frame = mine[pl.ds(ZROWS, TGT), :] + swap_z(other[pl.ds(ZROWS, TGT), :], 0)
    if kept.shape[0] > TGT:
        at = pl.ds(ZROWS + TGT, 8)
        frame = jnp.concatenate([frame, mine[at, :] + swap_z(other[at, :], 1)], axis=0)
    kept[...] = frame
    send("gy", 4, frame, out)


def spread_x_kernel(held, came, out, kept):
    frame = received("gy", 4, held[...], came)
    kept[...] = frame
    send("gx", 12, frame, out)


def spread_call(kernel, rows, *arrays):
    return pl.pallas_call(
        kernel,
        out_shape=[
            jax.ShapeDtypeStruct((8, rows - TGT + PACK, LANES), F32),
            jax.ShapeDtypeStruct((rows, LANES), F32),
        ],
        in_specs=vmem_specs(len(arrays)),
        out_specs=vmem_specs(2),
        compiler_params=PARAMS,
        name="spread",
    )(*arrays)


def step_kernel(first_step, last_step, *refs):
    count = 10 if first_step else 12
    field, faces, x_left, x_right, y_left, y_right, potential, kept, came, mat = refs[:10]
    if not first_step:
        previous, coupling = refs[10:12]
    refs = refs[count:]
    if last_step:
        (new, gram), refs = refs[:2], refs[2:]
    else:
        (new, x_low, x_high, y_low, y_high, message), refs = refs[:6], refs[6:]
        if first_step:
            coupling, refs = refs[0], refs[1:]
    total, coef, first_z, second_z = refs
    alpha = (1.0 if first_step else 2.0) / FILTER_HALF
    half = [0.0] + [-0.5 * c for c in STENCIL[1:]]
    diagonal = -1.5 * STENCIL[0] - FILTER_CENTRE
    write_z_matrices(first_z, second_z)

    def at(x, y, b):
        some = pl.ds(b, 8)
        if x < 0:
            return x_left[(x + REACH) * SY + y, some, :]
        if x >= SX:
            return x_right[(x - SX) * SY + y, some, :]
        if y < 0:
            return y_left[x, y + REACH, some, :]
        if y >= SY:
            return y_right[x, y - SY, some, :]
        return field[x * SY + y, some, :]

    for x in range(SX):
        along_z = []
        for g in (2 * x, 2 * x + 1):
            block = jnp.concatenate([field[4 * g + i] for i in range(4)], axis=0)
            hi, lo = split2(block)
            face = faces[pl.ds(g * EDGE, EDGE), :]
            face_hi = face.astype(BF16).astype(F32)
            side = jnp.concatenate(
                [face_hi, face - face_hi, face_hi, jnp.zeros((LANES - 3 * EDGE, LANES), F32)], axis=0
            ).T.astype(BF16)
            along_z.append(
                dot(jnp.concatenate([hi, lo], axis=1), first_z[...])
                + dot(jnp.concatenate([hi, side], axis=1), second_z[...])
            )
        for b in range(0, NB, 8):
            line = [at(x, y, b) for y in range(-REACH, SY + REACH)]
            for y in range(SY):
                part, i = divmod(y, 4)
                summed = along_z[part][i * NB + b : i * NB + b + 8]
                for m in range(1, REACH + 1):
                    around = (at(x + m, y, b) + at(x - m, y, b)) + (line[y + REACH + m] + line[y + REACH - m])
                    summed = summed + half[m] * around
                summed = summed + (potential[pl.ds(x * SY + y, 1), :] + diagonal) * line[y + REACH]
                result = alpha * summed
                if not first_step:
                    result = result - previous[x * SY + y, pl.ds(b, 8), :]
                new[x * SY + y, pl.ds(b, 8), :] = result

    total[...] = jnp.zeros_like(total)
    frame = received("gx", 12, kept[...], came)
    if first_step:
        by_channel = jnp.concatenate([frame[TGT:], jnp.zeros((LANES - 8, LANES), F32)], axis=0).T
        columns = [jnp.broadcast_to(by_channel[:TGT, j : j + 1], (TGT, NB)) for j in range(NPJ)]
        coupling[...] = jnp.concatenate(columns, axis=1)
        frame = frame[:TGT]
    frame = frame * (alpha * coupling[...])
    stacked = jnp.concatenate([frame[:, j * NB : (j + 1) * NB] for j in range(NPJ)], axis=0)
    turned = stacked.T
    coef[...] = jnp.concatenate(split2(turned), axis=0)

    c_both = coef[...]
    for x in range(SX):
        acc = total[...]
        rows = []
        for p in range(4):
            pair_mat = mat[x * 4 + p]
            both = dot(c_both, pair_mat[:CH])
            added = both[:NB] + both[NB:] + dot(c_both[:NB], pair_mat[CH:])
            for q in range(2):
                here = x * SY + 2 * p + q
                rows.append(new[here] + added[:, q * SZ : (q + 1) * SZ])
                new[here] = rows[-1]
        if not last_step:
            write_x_faces(x, rows, x_low, x_high)
            write_y_faces(x, rows, y_low, y_high)
        for p in range(4):
            values = jnp.concatenate(rows[2 * p : 2 * p + 2], axis=1)
            if last_step:
                joined = jnp.concatenate(split3(values), axis=0)
                acc = acc + dot(joined, joined, NT)
            else:
                acc = acc + partial_of(mat[x * 4 + p], values)
        total[...] = acc
        if not last_step:
            for part in range(2):
                message[pl.ds((2 * x + part) * EDGE, EDGE), :] = z_faces(rows[4 * part : 4 * part + 4])

    if last_step:
        t = total[...]
        summed = t[2 * NB :, :NB] + t[:NB, 2 * NB :] + t[NB : 2 * NB, NB : 2 * NB]
        summed = summed + (t[NB : 2 * NB, :NB] + t[:NB, NB : 2 * NB]) + t[:NB, :NB]
        blocks = [summed[8 * i : 8 * i + 8, 8 * j : 8 * j + 8] for i, j in LOWER]
        blocks = jnp.concatenate(blocks, axis=1)
        for r in range(8):
            gram[:, pl.ds(r * 8 * len(LOWER), 8 * len(LOWER))] = blocks[r : r + 1]
    else:
        message[pl.ds(ZROWS, TGT), :] = packed_partial(total[...])


def step(first_step, last_step, *arrays):
    total = (3 * NB, 3 * NB) if last_step else TOTAL
    if last_step:
        outs = [BLOCK, jax.ShapeDtypeStruct((1, 64 * len(LOWER)), F32)]
    else:
        outs = [BLOCK, X_FACE, X_FACE, Y_FACE, Y_FACE, MESSAGE] + ([FRAME] if first_step else [])
    return pl.pallas_call(
        functools.partial(step_kernel, first_step, last_step),
        out_shape=outs,
        in_specs=vmem_specs(len(arrays)),
        out_specs=vmem_specs(len(outs)),
        scratch_shapes=[
            pltpu.VMEM(total, F32),
            pltpu.VMEM((2 * NB, CH), BF16),
            pltpu.VMEM((2 * SZ, SZ), BF16),
            pltpu.VMEM((2 * SZ, SZ), BF16),
        ],
        compiler_params=PARAMS,
        name="step",
    )(*arrays)


def finish_kernel(scale, field, grams, out, made, inverse, out_sem):
    packed = grams[0]
    for slot in range(1, grams.shape[0]):
        packed = packed + grams[slot]
    packed = packed * scale
    width = 8 * len(LOWER)
    blocks = jnp.concatenate([packed[:, r * width : (r + 1) * width] for r in range(8)], axis=0)
    lower = []
    for i in range(4):
        found = [blocks[:, 8 * b : 8 * b + 8] for b, (k, _) in enumerate(LOWER) if k == i]
        lower.append(jnp.concatenate(found + [jnp.zeros((8, NB - 8 * i - 8), F32)] * (i < 3), axis=1))
    lower = jnp.concatenate(lower, axis=0)
    row = lax.broadcasted_iota(jnp.int32, (NB, NB), 0)
    column = lax.broadcasted_iota(jnp.int32, (NB, NB), 1)
    gram = jnp.where(row // 8 >= column // 8, lower, lower.T)
    eye = jnp.where(row == column, 1.0, 0.0)
    work = jnp.concatenate([gram, eye], axis=1)
    below = lax.broadcasted_iota(jnp.int32, (NB, 2 * NB), 0)
    for k in range(0, NB, STRIP):
        columns = [jnp.broadcast_to(work[:, k + i : k + i + 1], work.shape) for i in range(STRIP)]
        lines = [work[k + i : k + i + 1] for i in range(STRIP)]
        for i in range(STRIP):
            root = lax.rsqrt(columns[i][k + i : k + i + 1])
            columns[i] = columns[i] * root
            lines[i] = lines[i] * root
            inverse[pl.ds(k + i, 1), :] = lines[i][:, NB:]
            for j in range(i + 1, STRIP):
                beside = columns[i][k + j : k + j + 1]
                columns[j] = columns[j] - columns[i] * beside
                lines[j] = lines[j] - lines[i] * beside
        if k < NB - STRIP:
            removed = columns[0] * lines[0]
            for i in range(1, STRIP):
                removed = removed + columns[i] * lines[i]
            work = work - jnp.where(below >= k + STRIP, removed, 0.0)
    hi, mid, lo = split3(inverse[...])
    left = jnp.concatenate([lo, mid, hi, mid, hi, hi], axis=1)

    for x in range(SX):
        for p in range(SY // 2):
            at = x * SY + 2 * p
            values = jnp.concatenate([field[at], field[at + 1]], axis=1)
            f_hi, f_mid, f_lo = split3(values)
            right = jnp.concatenate([f_hi, f_mid, f_lo, f_hi, f_mid, f_hi], axis=0)
            result = dot(left, right)
            made[at] = result[:, :SZ]
            made[at + 1] = result[:, SZ:]
            for q in range(2):
                pltpu.make_async_copy(made.at[at + q], out.at[:, at + q, :], out_sem.at[at + q]).start()

    for r in range(ROWS):
        pltpu.make_async_copy(made.at[r], out.at[:, r, :], out_sem.at[r]).wait()


def finish(scale, field, grams):
    return pl.pallas_call(
        functools.partial(finish_kernel, scale),
        out_shape=jax.ShapeDtypeStruct((NB, ROWS, SZ), F32),
        in_specs=vmem_specs(2),
        out_specs=pl.BlockSpec(memory_space=pl.ANY),
        scratch_shapes=[
            pltpu.VMEM((ROWS, NB, SZ), F32),
            pltpu.VMEM((NB, NB), F32),
            pltpu.SemaphoreType.DMA((ROWS,)),
        ],
        compiler_params=PARAMS,
        name="finish",
    )(field, grams)


def shift(value, axis, by):
    count = lax.axis_size(axis)
    return lax.ppermute(value, axis, [(i, (i + by) % count) for i in range(count)])


def local(orbitals, potential, projector, point_cell, target, point_count, coupling):
    bands, size_x, size_y, size_z = orbitals.shape
    field, key, own, *weights = prepare(
        point_count.reshape(1), coupling, orbitals.reshape(NB, ROWS, SZ), point_cell, target, projector
    )
    pot = potential.reshape(ROWS, SZ)
    key = key.reshape(SLOTS)
    ordered = lax.sort((key, *[w.reshape(SLOTS) for w in weights]), num_keys=1, is_stable=False)
    starts = jnp.sum(
        (ordered[0][None, :] < (lax.iota(jnp.int32, ROWS + 1) * (SZ * 64))[:, None]).astype(jnp.int32), axis=1
    )
    points = jnp.stack([ordered[0].astype(F32), *ordered[1:]])
    mat = build(starts, points)

    other = ()
    for k in range(DEGREE):
        start, last = k == 0, k == DEGREE - 1
        if start:
            message, x_low, x_high, y_low, y_high = first(field, mat, own)
        faces = shift(message, "gz", 1)
        y_left = shift(y_high, "gy", 1)
        y_right = shift(y_low, "gy", -1)
        faces, x_low, x_high = lax.optimization_barrier((faces, x_low, x_high))
        x_left = shift(x_high, "gx", 1)
        x_right = shift(x_low, "gx", -1)
        rows = message.shape[0] - ZROWS
        sends, kept = spread_call(spread_zy_kernel, rows, message, faces)
        came = lax.all_to_all(sends, "gy", 0, 0)
        sends, kept = spread_call(spread_x_kernel, rows, kept, came)
        came = lax.all_to_all(sends, "gx", 0, 0)
        outs = step(start, last, field, faces, x_left, x_right, y_left, y_right, pot, kept, came, mat, *other)
        previous = field
        if last:
            field, gram = outs
        else:
            field, x_low, x_high, y_low, y_high, message = outs[:6]
            if start:
                scales = outs[6]
            other = (previous, scales)
    axes = ("gx", "gy", "gz")
    devices = 1
    for axis in axes:
        devices *= lax.axis_size(axis)
    grams = lax.all_to_all(jnp.broadcast_to(gram[None], (devices,) + gram.shape), axes, 0, 0)
    result = finish(1.0 / float(devices * ROWS * SZ), field, grams)
    return result.reshape(bands, size_x, size_y, size_z)


def solution(mesh):
    in_specs = (
        P(None, "gx", "gy", "gz"),
        P("gx", "gy", "gz"),
        P(None, ("gx", "gy", "gz")),
        P(("gx", "gy", "gz")),
        P(("gx", "gy", "gz")),
        P("gx", "gy", "gz"),
        P(("gx", "gy", "gz"), None),
    )
    out_specs = P(None, "gx", "gy", "gz")
    return jax.shard_map(local, mesh=mesh, in_specs=in_specs, out_specs=out_specs, check_vma=False)
```
